32 devices in a mesh: dp: 4 (over z), fsdp: 8 (over y, x, core).
Axes of the slice: x: 2, y: 2, z: 4, core: 2. Of those that a mesh axis runs over, the one named last changes fastest.
Arguments:
- clip_count: int32 [32], P(('dp', 'fsdp')), may hold values from 2 to 4, as said below
- frame_count: int32 [128], P(('dp', 'fsdp')), may hold values from 4 to 8, as said below
- frame_mask: int32 [128, 8], P(('dp', 'fsdp')), may hold values from 0 to 1, as said below
- features: bfloat16 [128, 8, 14, 14, 1024], P(('dp', 'fsdp')), may hold values from -6 to 6
- w_reduce1: bfloat16 [1024, 512], P(('dp', 'fsdp')), may hold values from -0.1875 to 0.1875
- w_spatial1: bfloat16 [9, 262144], P(None, ('dp', 'fsdp')), may hold values from -0.09375 to 0.09375
- w_expand1: bfloat16 [512, 2048], P(('dp', 'fsdp')), may hold values from -0.25 to 0.25
- w_project1: bfloat16 [1024, 2048], P(('dp', 'fsdp')), may hold values from -0.1875 to 0.1875
- w_reduce2: bfloat16 [2048, 512], P(('dp', 'fsdp')), may hold values from -0.125 to 0.125
- w_motion_in: bfloat16 [512, 32], P(('dp', 'fsdp')), may hold values from -0.25 to 0.25
- w_motion_out: bfloat16 [512, 32], P(('dp', 'fsdp')), may hold values from -1 to 1
- w_spatial2: bfloat16 [27, 16384], P(None, ('dp', 'fsdp')), may hold values from -0.1875 to 0.1875
- w_expand2: bfloat16 [512, 2048], P(('dp', 'fsdp')), may hold values from -0.25 to 0.25
- gains: float32 [8608], replicated, may hold values from 0.5 to 1.5
- biases: float32 [8608], replicated, may hold values from -2.5 to 2.5
- motion_taps: float32 [9, 32], replicated, may hold values from -2 to 2
- temporal_taps: float32 [3, 3, 128], replicated, may hold values from -3.5 to 3.5
- cotangent: bfloat16 [128, 8, 7, 7, 2048], P(('dp', 'fsdp')), may hold values from -6 to 6
Outputs:
- output: bfloat16 [128, 8, 7, 7, 2048], P(('dp', 'fsdp'))
- grad_features: bfloat16 [128, 8, 14, 14, 1024], P(('dp', 'fsdp'))
- grad_reduce1: float32 [1024, 512], P(('dp', 'fsdp'))
- grad_spatial1: float32 [9, 262144], P(None, ('dp', 'fsdp'))
- grad_expand1: float32 [512, 2048], P(('dp', 'fsdp'))
- grad_project1: float32 [1024, 2048], P(('dp', 'fsdp'))
- grad_reduce2: float32 [2048, 512], P(('dp', 'fsdp'))
- grad_motion_in: float32 [512, 32], P(('dp', 'fsdp'))
- grad_motion_out: float32 [512, 32], P(('dp', 'fsdp'))
- grad_spatial2: float32 [27, 16384], P(None, ('dp', 'fsdp'))
- grad_expand2: float32 [512, 2048], P(('dp', 'fsdp'))
- grad_gains: float32 [8608], replicated
- grad_biases: float32 [8608], replicated
- grad_motion_taps: float32 [9, 32], replicated
- grad_temporal_taps: float32 [3, 3, 128], replicated
The draws below stay inside these ranges and needn't reach their ends.
Inputs may be any that keep to these rules, and one draw needn't show every extreme that they name: Each device's live clips are its first clip_count slots; some device has all 4 live and some has the fewest. A clip's frames are its first frame_count slots; some clip has all 8 and some has the fewest. `frame_mask`: the first frame of every clip slot is usable.
All inputs are finite; a program needn't handle non-finite values.
Results may differ from the reference program's by a relative error of at most 0.024.
Values may be sent and summed in bfloat16 or wider, within the bound.
No kernel may reach another device: no remote copies, remote signals or barrier semaphores. Data moves between devices by JAX's collectives and lax.ppermute only.
A program may use at most 384 MiB of HBM per device.

```python
import jax
import jax.numpy as jnp
from jax import lax

C_IN = 1024
MID = 512
C_OUT = 2048
RED = 32
GROUP = 128
H_IN = 14
HW = 7
FRAMES = 8
CLIP_DEV = 4
CLIPS = 128
NORM_ALL = 8608
DEVICES = 32


def pinned_counts(key, length, lowest, highest):
    first_key, second_key = jax.random.split(key)
    counts = jax.random.randint(first_key, (length,), lowest, highest + 1)
    spot = jax.random.randint(second_key, (), 0, length)
    positions = jnp.arange(length)
    counts = jnp.where(positions == spot, highest, counts)
    counts = jnp.where(positions == (spot + 1) % length, lowest, counts)
    return counts.astype(jnp.int32)


def draw_clip_count(key, part):
    key = jax.random.fold_in(key, 11)
    return pinned_counts(key, DEVICES, (CLIP_DEV + 1) // 2, CLIP_DEV)


def draw_frame_count(key, part):
    key = jax.random.fold_in(key, 23)
    return pinned_counts(key, CLIPS, FRAMES // 2, FRAMES)


def draw_frame_mask(key, part):
    key = jax.random.fold_in(key, 37)
    levels = jax.random.randint(key, (CLIPS, FRAMES), 0, 8)
    usable = (levels < 7).astype(jnp.int32)
    first = (jnp.arange(FRAMES) == 0)[None, :]
    return jnp.where(first, 1, usable).astype(jnp.int32)


def block_levels(own_key, shape, cuts, least, largest):
    def one(position, parts):
        steps = jax.random.uniform(jax.random.fold_in(jax.random.fold_in(own_key, 6), position), (parts,), jnp.float32, least / len(cuts), largest / len(cuts))
        return jnp.repeat(jnp.exp(steps), shape[position] // parts).reshape((-1,) + (1,) * (len(shape) - position - 1))

    factor_of = one(*cuts[0])
    for cut in cuts[1:]:
        factor_of = factor_of * one(*cut)
    return factor_of


def noise(own_key, shape, width, most, cuts=(), kind=jnp.bfloat16):
    values = width * jax.random.normal(own_key, shape, jnp.float32)
    if cuts:
        values = values * block_levels(own_key, shape, cuts, -0.22, 0.18)
    return jnp.clip(values, -most, most).astype(kind)


def setup_inputs(seed: int = 0) -> dict:
    keys = jax.random.split(jax.random.key(seed), 19)
    clip_count = draw_clip_count(jax.random.fold_in(keys[18], 71), 0)
    frame_count = draw_frame_count(jax.random.fold_in(keys[18], 71), 0)
    frame_mask = draw_frame_mask(jax.random.fold_in(keys[18], 71), 0)
    features = noise(keys[3], (CLIPS, FRAMES, H_IN, H_IN, C_IN), 1.0, 6.0, ((0, 32),))
    w_reduce1 = noise(keys[4], (C_IN, MID), C_IN ** -0.5, 0.1875, ((0, 32),))
    w_spatial1 = noise(keys[5], (9, MID * MID), (9 * MID) ** -0.5, 0.09375, ((1, 32),))
    w_expand1 = noise(keys[6], (MID, C_OUT), MID ** -0.5, 0.25, ((0, 32),))
    w_project1 = noise(keys[7], (C_IN, C_OUT), C_IN ** -0.5, 0.1875, ((0, 32),))
    w_reduce2 = noise(keys[8], (C_OUT, MID), C_OUT ** -0.5, 0.125, ((0, 32),))
    w_motion_in = noise(keys[9], (MID, RED), MID ** -0.5, 0.25, ((0, 32),))
    w_motion_out = noise(keys[10], (MID, RED), RED ** -0.5, 1.0, ((0, 32),))
    w_spatial2 = noise(keys[11], (27, GROUP * GROUP), (9 * GROUP) ** -0.5, 0.1875, ((1, 32),))
    w_expand2 = noise(keys[12], (MID, C_OUT), MID ** -0.5, 0.25, ((0, 32),))
    gains = jnp.clip(1.0 + 0.1 * jax.random.normal(keys[13], (NORM_ALL,), jnp.float32), 0.5, 1.5)
    biases = noise(keys[14], (NORM_ALL,), 0.4, 2.5, (), jnp.float32)
    motion_taps = noise(keys[15], (9, RED), 9 ** -0.5, 2.0, (), jnp.float32)
    temporal_taps = noise(keys[16], (3, 3, GROUP), 3 ** -0.5, 3.5, (), jnp.float32)
    cotangent = noise(keys[17], (CLIPS, FRAMES, HW, HW, C_OUT), 1.0, 6.0, ((0, 32),))
    return {"clip_count": clip_count, "frame_count": frame_count, "frame_mask": frame_mask, "features": features, "w_reduce1": w_reduce1, "w_spatial1": w_spatial1, "w_expand1": w_expand1, "w_project1": w_project1, "w_reduce2": w_reduce2, "w_motion_in": w_motion_in, "w_motion_out": w_motion_out, "w_spatial2": w_spatial2, "w_expand2": w_expand2, "gains": gains, "biases": biases, "motion_taps": motion_taps, "temporal_taps": temporal_taps, "cotangent": cotangent}


@jax.custom_vjp
def low(v):
    return lax.optimization_barrier(v.astype(jnp.bfloat16)).astype(jnp.float32)

@jax.custom_vjp
def low_back(v):
    return v

def low_keep(v):
    return (low(v), None)

def low_pass(kept, grad):
    return (grad,)

def back_keep(v):
    return (v, None)

def back_low(kept, grad):
    return (low(grad),)
low.defvjp(low_keep, low_pass)
low_back.defvjp(back_keep, back_low)
EPSILON = 1e-05
HIGHEST = lax.Precision.HIGHEST

def product(left, weight):
    return jnp.einsum('...i,io->...o', left, weight, precision=HIGHEST)

def earlier(values):
    return jnp.concatenate([jnp.zeros_like(values[:, :1]), values[:, :-1]], axis=1)

def later(values):
    return jnp.concatenate([values[:, 1:], jnp.zeros_like(values[:, :1])], axis=1)

def spatial_cols(values, stride):
    padded = jnp.pad(values, ((0, 0), (0, 0), (1, 1), (1, 1), (0, 0)))
    size = values.shape[2] // stride
    reach = stride * (size - 1) + 1
    pieces = [padded[:, :, row:row + reach:stride, col:col + reach:stride, :] for row in range(3) for col in range(3)]
    return jnp.concatenate(pieces, axis=-1)

def motion_conv(values, taps):
    size = values.shape[2]
    padded = jnp.pad(values, ((0, 0), (0, 0), (1, 1), (1, 1), (0, 0)))
    result = jnp.zeros_like(values)
    for row in range(3):
        for col in range(3):
            result = result + taps[row * 3 + col] * padded[:, :, row:row + size, col:col + size, :]
    return result

def temporal(values, taps):
    return taps[0] * earlier(values) + taps[1] * values + taps[2] * later(values)

def normalize(values, gain, bias, weight, count):
    axes = tuple(range(values.ndim - 1))
    mean = lax.optimization_barrier(jnp.sum(values * weight, axis=axes)) / count
    square = lax.optimization_barrier(jnp.sum(values * values * weight, axis=axes)) / count
    scale = lax.rsqrt(square - mean * mean + EPSILON)
    return gain * (values - mean) * scale + bias

def forward(valid, features, w_reduce1, w_spatial1, w_expand1, w_project1, w_reduce2, w_motion_in, w_motion_out, w_spatial2, w_expand2, gains, biases, motion_taps, temporal_taps):
    widths = [MID, MID, C_OUT, C_OUT, MID, RED, MID, GROUP, GROUP, GROUP, C_OUT]
    starts = [sum(widths[:k]) for k in range(len(widths))]
    mask = valid[:, :, None, None, None]
    frames_total = jnp.sum(valid)
    big = H_IN * H_IN
    small = HW * HW

    def batch_norm(values, index, weight, pixels):
        begin = starts[index]
        finish = begin + widths[index]
        return normalize(values, gains[begin:finish], biases[begin:finish], weight, frames_total * pixels)
    first_raw = low_back(product(features, w_reduce1))
    act_a = low(jax.nn.silu(batch_norm(first_raw, 0, mask, big)) * mask)
    strided_raw = low_back(product(spatial_cols(act_a, 2), w_spatial1.reshape(9 * MID, MID)))
    act_b = low(jax.nn.silu(batch_norm(strided_raw, 1, mask, small)) * mask)
    widen_raw = low_back(product(act_b, w_expand1))
    shortcut_raw = low_back(product(features[:, :, ::2, ::2, :], w_project1))
    block_one = low(jax.nn.silu(batch_norm(widen_raw, 2, mask, small) + batch_norm(shortcut_raw, 3, mask, small)) * mask)
    narrow_raw = low_back(product(block_one, w_reduce2))
    act_d = low(jax.nn.silu(batch_norm(narrow_raw, 4, mask, small)) * mask)
    motion_raw = low_back(product(act_d, w_motion_in))
    reduced = batch_norm(motion_raw, 5, mask, small) * mask
    change = (motion_conv(later(reduced), motion_taps) - reduced) * later(mask)
    pooled = lax.optimization_barrier(jnp.mean(change, axis=(2, 3)))
    lifted = jnp.einsum('cfr,or->cfo', pooled, w_motion_out, precision=HIGHEST)
    attend = 2.0 * jax.nn.sigmoid(batch_norm(lifted, 6, valid[:, :, None], 1)) - 1.0
    excited = low(act_d * (1.0 + attend[:, :, None, None, :]))
    kernels = w_spatial2.reshape(3, 9 * GROUP, GROUP)
    outputs = [excited[..., :GROUP]]
    previous = None
    for group_index in range(1, 4):
        piece = excited[..., group_index * GROUP:(group_index + 1) * GROUP]
        if previous is not None:
            piece = piece + previous
        shifted = low(temporal(piece, temporal_taps[group_index - 1]))
        group_raw = low_back(product(spatial_cols(shifted, 1), kernels[group_index - 1]))
        previous = low(jax.nn.silu(batch_norm(group_raw, 6 + group_index, mask, small)) * mask)
        outputs.append(previous)
    joined = jnp.concatenate(outputs, axis=-1)
    final_raw = low_back(product(joined, w_expand2))
    return jax.nn.silu(batch_norm(final_raw, 10, mask, small) + block_one) * mask

def reference(clip_count, frame_count, frame_mask, features, w_reduce1, w_spatial1, w_expand1, w_project1, w_reduce2, w_motion_in, w_motion_out, w_spatial2, w_expand2, gains, biases, motion_taps, temporal_taps, cotangent):
    slots = jnp.arange(CLIPS, dtype=jnp.int32)
    owners = clip_count[(slots // CLIP_DEV).astype(jnp.int32)]
    live = slots % CLIP_DEV < owners
    frame_index = jnp.arange(FRAMES, dtype=jnp.int32)
    valid = (live[:, None] & (frame_index[None, :] < frame_count[:, None]) & (frame_mask == 1)).astype(jnp.float32)
    inputs = tuple((item.astype(jnp.float32) for item in (features, w_reduce1, w_spatial1, w_expand1, w_project1, w_reduce2, w_motion_in, w_motion_out, w_spatial2, w_expand2, gains, biases, motion_taps, temporal_taps)))

    def wrapped(*params):
        return forward(valid, *params)
    result, pullback = jax.vjp(wrapped, *inputs)
    grads = pullback(cotangent.astype(jnp.float32))
    return (result.astype(jnp.bfloat16), grads[0].astype(jnp.bfloat16), grads[1], grads[2], grads[3], grads[4], grads[5], grads[6], grads[7], grads[8], grads[9], grads[10], grads[11], grads[12], grads[13])
```

```python
import jax
import jax.numpy as jnp
from jax import lax
from jax.sharding import PartitionSpec as P

EPSILON = 1e-05
HIGHEST = lax.Precision.HIGHEST
AXES = ("dp", "fsdp")
BF = jnp.bfloat16
F32 = jnp.float32


def earlier(values):
    return jnp.concatenate([jnp.zeros_like(values[..., :1, :]), values[..., :-1, :]], axis=-2)


def later(values):
    return jnp.concatenate([values[..., 1:, :], jnp.zeros_like(values[..., :1, :])], axis=-2)


def taps_of(values, size):
    padded = jnp.pad(values, ((0, 0), (1, 1), (1, 1), (0, 0), (0, 0)))
    return [padded[:, r : r + size, c : c + size] for r in range(3) for c in range(3)]


def dot(left, weight):
    shape = left.shape
    flat = jnp.dot(left.reshape(-1, shape[-1]), weight, preferred_element_type=F32)
    return flat.reshape(shape[:-1] + (weight.shape[1],))


def dot_t(grad, weight):
    shape = grad.shape
    flat = lax.dot_general(
        grad.reshape(-1, shape[-1]), weight, (((1,), (1,)), ((), ())), preferred_element_type=F32
    )
    return flat.reshape(shape[:-1] + (weight.shape[0],))


def weight_grad(left, grad):
    return lax.dot_general(
        left.reshape(-1, left.shape[-1]),
        grad.reshape(-1, grad.shape[-1]),
        (((0,), (0,)), ((), ())),
        preferred_element_type=F32,
    )


def silu_slope(values):
    sig = jax.nn.sigmoid(values)
    return sig * (1.0 + values * (1.0 - sig))


def total_over(values):
    return jnp.sum(values, axis=tuple(range(values.ndim - 1)))


class Sums:
    def __init__(self, dp, fsdp):
        self.devices = dp * fsdp
        half = self.devices // 2
        self.groups = [[2 * i + c for i in range(half)] for c in range(2)]
        self.swap = [(i, i ^ 1) for i in range(self.devices)]

    def flat(self, values):
        size = values.shape[0]
        if size <= 2048:
            copies = jnp.broadcast_to(values[None], (self.devices, size))
            return jnp.sum(lax.all_to_all(copies, AXES, 0, 0), axis=0)
        core = lax.axis_index("fsdp") % 2
        halves = values.reshape(2, size // 2)
        mine = lax.dynamic_index_in_dim(halves, core, 0, False)
        other = lax.dynamic_index_in_dim(halves, 1 - core, 0, False)
        mine = mine + lax.ppermute(other, AXES, self.swap)
        copies = jnp.broadcast_to(mine[None], (self.devices // 2, size // 2))
        mine = jnp.sum(lax.all_to_all(copies, AXES, 0, 0, axis_index_groups=self.groups), axis=0)
        other = lax.ppermute(mine, AXES, self.swap)
        low = jnp.where(core == 0, mine, other)
        high = jnp.where(core == 0, other, mine)
        return jnp.concatenate([low, high])

    def __call__(self, *arrays):
        sizes = [a.size for a in arrays]
        extra = -sum(sizes) % 256
        parts = [a.reshape(-1) for a in arrays]
        if extra:
            parts.append(jnp.zeros((extra,), F32))
        merged = self.flat(jnp.concatenate(parts))
        out, begin = [], 0
        for a, size in zip(arrays, sizes):
            out.append(merged[begin : begin + size].reshape(a.shape))
            begin += size
        return out


def affine(total, square, count, gain, bias):
    mean = total / count
    inv = lax.rsqrt(square / count - mean * mean + EPSILON)
    alpha = gain * inv
    return mean, inv, alpha, bias - mean * alpha


def local(
    dp,
    fsdp,
    clip_count,
    frame_count,
    frame_mask,
    features,
    w_reduce1,
    w_spatial1,
    w_expand1,
    w_project1,
    w_reduce2,
    w_motion_in,
    w_motion_out,
    w_spatial2,
    w_expand2,
    gains,
    biases,
    motion_taps,
    temporal_taps,
    cotangent,
):
    devices = dp * fsdp
    sums = Sums(dp, fsdp)
    slots, frames, height = features.shape[:3]
    half = height // 2
    area = half * half
    c_in = features.shape[-1]
    middle = w_reduce1.shape[1]
    group = middle // 4
    wide = w_expand1.shape[1]
    narrow = w_motion_in.shape[1]
    valid = (
        (jnp.arange(slots)[:, None] < clip_count[0])
        & (jnp.arange(frames)[None, :] < frame_count[:, None])
        & (frame_mask == 1)
    ).astype(F32)
    mask = valid[:, None, None, :, None]
    fmask = valid[:, :, None]
    widths = [middle, middle, wide, wide, middle, narrow, middle, group, group, group, wide]
    starts = [sum(widths[:k]) for k in range(len(widths))]
    gain = [gains[s : s + w] for s, w in zip(starts, widths)]
    bias = [biases[s : s + w] for s, w in zip(starts, widths)]

    feats = features.transpose(0, 2, 3, 1, 4)
    cot = cotangent.transpose(0, 2, 3, 1, 4)

    def gather(value):
        return lax.all_gather(value, AXES, axis=0, tiled=False)

    own = middle // devices
    full_reduce1 = gather(w_reduce1).reshape(c_in, middle)
    full_spatial1 = (
        gather(w_spatial1.reshape(9, own, middle)).transpose(1, 0, 2, 3).reshape(9, middle, middle)
    )
    pack_wide = gather(jnp.concatenate([w_expand1, w_project1, w_expand2], axis=0))
    rows1, rowsp = w_expand1.shape[0], w_project1.shape[0]
    full_expand1 = pack_wide[:, :rows1].reshape(middle, wide)
    full_project1 = pack_wide[:, rows1 : rows1 + rowsp].reshape(c_in, wide)
    full_expand2 = pack_wide[:, rows1 + rowsp :].reshape(middle, wide)
    rows2 = w_reduce2.shape[0]
    def rows_of(value):
        return jnp.pad(value, ((0, 0), (0, -value.shape[1] % middle))).reshape(
            value.shape[0], -1, middle
        )

    smalls = jnp.concatenate(
        [w_spatial2.reshape(1, -1), w_motion_in.reshape(1, -1), w_motion_out.reshape(1, -1)], axis=1
    )
    pack_mid = gather(jnp.concatenate([w_reduce2, rows_of(smalls)[0]], axis=0))
    full_reduce2 = pack_mid[:, :rows2].reshape(wide, middle)
    flat_small = pack_mid[:, rows2:].reshape(devices, -1)
    size_s, size_m = w_spatial2.size, w_motion_in.size
    kernels = (
        flat_small[:, :size_s].reshape(devices, 27, -1).swapaxes(0, 1).reshape(3, 9, group, group)
    )
    small = flat_small[:, size_s : size_s + 2 * size_m].reshape(devices, 2, own, narrow)
    full_motion_in = small[:, 0].reshape(middle, narrow)
    full_motion_out = small[:, 1].reshape(middle, narrow).astype(F32)

    raw_a = dot(feats, full_reduce1)
    sum_a, square_a, frame_total, pairs = sums(
        total_over(raw_a * mask),
        total_over(raw_a * raw_a * mask),
        jnp.sum(valid),
        jnp.sum(valid[:, :-1] * valid[:, 1:]),
    )
    count_big = frame_total * (height * height)
    count = frame_total * area
    mean_a, inv_a, alpha_a, beta_a = affine(sum_a, square_a, count_big, gain[0], bias[0])
    act_a = (jax.nn.silu(raw_a * alpha_a + beta_a) * mask).astype(BF)
    padded_a = jnp.pad(act_a, ((0, 0), (1, 1), (1, 1), (0, 0), (0, 0)))
    split_a = padded_a.reshape(slots, half + 1, 2, half + 1, 2, frames, middle)
    cols_b = jnp.concatenate(
        [
            split_a[:, r // 2 : r // 2 + half, r % 2, c // 2 : c // 2 + half, c % 2]
            for r in range(3)
            for c in range(3)
        ],
        axis=-1,
    )
    raw_b = dot(cols_b, full_spatial1.reshape(9 * middle, middle))
    sampled = feats.reshape(slots, half, 2, half, 2, frames, c_in)[:, :, 0, :, 0]
    raw_p = dot(sampled, full_project1)

    def moments(raw):
        return total_over(raw * mask), total_over(raw * raw * mask)

    sum_b, square_b = sums(*moments(raw_b))
    mean_b, inv_b, alpha_b, beta_b = affine(sum_b, square_b, count, gain[1], bias[1])
    act_b = (jax.nn.silu(raw_b * alpha_b + beta_b) * mask).astype(BF)
    raw_c = dot(act_b, full_expand1)
    sum_c, square_c, sum_p, square_p = sums(*moments(raw_c), *moments(raw_p))
    mean_c, inv_c, alpha_c, beta_c = affine(sum_c, square_c, count, gain[2], bias[2])
    mean_p, inv_p, alpha_p, beta_p = affine(sum_p, square_p, count, gain[3], bias[3])
    sum_one = raw_c * alpha_c + beta_c + (raw_p * alpha_p + beta_p)
    block_one = (jax.nn.silu(sum_one) * mask).astype(BF)

    raw_d = dot(block_one, full_reduce2)
    sum_d, square_d = sums(*moments(raw_d))
    mean_d, inv_d, alpha_d, beta_d = affine(sum_d, square_d, count, gain[4], bias[4])
    norm_d = raw_d * alpha_d + beta_d
    act_d = (jax.nn.silu(norm_d) * mask).astype(BF)
    raw_m = dot(act_d, full_motion_in)

    spot = jnp.arange(half)
    reach = [(spot - k + 1 >= 0) & (spot - k + 1 < half) for k in range(3)]
    windows = jnp.stack(
        [(reach[r][:, None] & reach[c][None, :]) for r in range(3) for c in range(3)], axis=-1
    ).astype(F32)
    kmap = jnp.sum(windows[..., None] * motion_taps, axis=2)
    ksum = jnp.sum(kmap, axis=(0, 1))
    in_window = jnp.stack(
        [jnp.sum(raw_m * windows[None, :, :, k, None, None], axis=(1, 2)) for k in range(9)]
    )
    mapped = jnp.sum(in_window * motion_taps[:, None, None, :], axis=0)
    plain = jnp.sum(raw_m, axis=(1, 2))
    vnext = later(fmask)
    pool_raw = (vnext / area) * (later(mapped * fmask) - fmask * plain)
    pool_one = (vnext / area) * (later(fmask) * ksum - fmask * area)
    flat_raw = pool_raw.reshape(-1, narrow)
    flat_valid = valid.reshape(-1, 1)
    gram = lax.dot_general(
        flat_raw * flat_valid, flat_raw, (((0,), (0,)), ((), ())), precision=HIGHEST
    )
    sum_m, square_m, pool_a, gram_aa = sums(
        *moments(raw_m), jnp.sum(flat_raw * flat_valid, axis=0), gram
    )
    mean_m, inv_m, alpha_m, beta_m = affine(sum_m, square_m, count, gain[5], bias[5])
    step = ksum / area - 1.0
    pool_b = pairs * step
    gram_ab = pool_a[:, None] * step[None, :]
    gram_bb = pairs * step[:, None] * step[None, :]
    pooled = alpha_m * pool_raw + beta_m * pool_one
    lifted = jnp.einsum("cfr,or->cfo", pooled, full_motion_out, precision=HIGHEST)
    gram_p = (
        alpha_m[:, None] * alpha_m * gram_aa
        + alpha_m[:, None] * beta_m * gram_ab
        + beta_m[:, None] * alpha_m * gram_ab.T
        + beta_m[:, None] * beta_m * gram_bb
    )
    sum_x = jnp.dot(full_motion_out, alpha_m * pool_a + beta_m * pool_b, precision=HIGHEST)
    square_x = jnp.sum(jnp.dot(full_motion_out, gram_p, precision=HIGHEST) * full_motion_out, axis=1)
    mean_x, inv_x, alpha_x, beta_x = affine(sum_x, square_x, frame_total, gain[6], bias[6])
    sigma = jax.nn.sigmoid(lifted * alpha_x + beta_x)
    attend1 = 2.0 * sigma
    attend_px = attend1[:, None, None, :, :]
    excited = (act_d.astype(F32) * attend_px).astype(BF)

    pieces, cols_g, raws, stats = [], [], [], []
    outputs = [excited[..., :group]]
    previous = None
    for k in range(3):
        piece = excited[..., (k + 1) * group : (k + 2) * group].astype(F32)
        if previous is not None:
            piece = piece + previous.astype(F32)
        taps = temporal_taps[k]
        shifted = (taps[0] * earlier(piece) + taps[1] * piece + taps[2] * later(piece)).astype(BF)
        cols = jnp.concatenate(taps_of(shifted, half), axis=-1)
        raw = dot(cols, kernels[k].reshape(9 * group, group))
        stat = affine(*sums(*moments(raw)), count, gain[7 + k], bias[7 + k])
        previous = (jax.nn.silu(raw * stat[2] + stat[3]) * mask).astype(BF)
        pieces.append(piece)
        cols_g.append(cols)
        raws.append(raw)
        stats.append(stat)
        outputs.append(previous)
    joined = jnp.concatenate(outputs, axis=-1)
    raw_e = dot(joined, full_expand2)
    mean_e, inv_e, alpha_e, beta_e = affine(*sums(*moments(raw_e)), count, gain[10], bias[10])
    total_two = raw_e * alpha_e + beta_e + block_one.astype(F32)
    result = (jax.nn.silu(total_two) * mask).astype(BF)

    shifts = [None] * 11
    spreads = [None] * 11

    def grad_raw(index, grad, raw, mean, inv, weight, number):
        unit = (raw - mean) * inv
        return gain[index] * inv * (grad - weight * (shifts[index] + unit * spreads[index]) / number)

    grad_total = cot.astype(F32) * mask * silu_slope(total_two)
    shifts[10], spreads[10] = sums(
        total_over(grad_total), total_over(grad_total * ((raw_e - mean_e) * inv_e))
    )
    final_grad = grad_raw(10, grad_total, raw_e, mean_e, inv_e, mask, count).astype(BF)
    grad_expand2 = weight_grad(joined, final_grad)
    grad_joined = dot_t(final_grad, full_expand2)
    grad_groups = [grad_joined[..., :group], None, None, None]
    kernel_grads = [None] * 3
    temporal_grads = [None] * 3
    incoming = None
    for k in (2, 1, 0):
        grad_out = grad_joined[..., (k + 1) * group : (k + 2) * group]
        if incoming is not None:
            grad_out = grad_out + incoming
        mean, inv, alpha, beta = stats[k]
        grad_pre = grad_out * mask * silu_slope(raws[k] * alpha + beta)
        shifts[7 + k], spreads[7 + k] = sums(
            total_over(grad_pre), total_over(grad_pre * ((raws[k] - mean) * inv))
        )
        group_grad = grad_raw(7 + k, grad_pre, raws[k], mean, inv, mask, count).astype(BF)
        kernel_grads[k] = weight_grad(cols_g[k], group_grad)
        back = jnp.concatenate(taps_of(group_grad, half), axis=-1)
        flipped = kernels[k][::-1].transpose(0, 2, 1).reshape(9 * group, group)
        grad_shifted = dot(back, flipped)
        taps = temporal_taps[k]
        piece = pieces[k]
        incoming = (
            taps[0] * later(grad_shifted) + taps[1] * grad_shifted + taps[2] * earlier(grad_shifted)
        )
        temporal_grads[k] = jnp.stack(
            [
                total_over(grad_shifted * earlier(piece)),
                total_over(grad_shifted * piece),
                total_over(grad_shifted * later(piece)),
            ]
        )
        grad_groups[k + 1] = incoming
    grad_excited = jnp.concatenate(grad_groups, axis=-1)
    grad_attend = jnp.sum(grad_excited * act_d.astype(F32), axis=(1, 2))
    grad_x = grad_attend * 2.0 * sigma * (1.0 - sigma)
    unit_x = (lifted - mean_x) * inv_x
    pool_unit = (pool_raw - mean_m * pool_one) * inv_m
    grad_e = jnp.einsum("cfo,or->cfr", grad_x, full_motion_out * alpha_x[:, None], precision=HIGHEST)
    shifts[6], spreads[6], first_t, second_t = sums(
        jnp.sum(grad_x, axis=(0, 1)),
        jnp.sum(grad_x * unit_x, axis=(0, 1)),
        jnp.sum(grad_e * pool_one, axis=(0, 1)),
        jnp.sum(grad_e * pool_unit, axis=(0, 1)),
    )
    lift_b = jnp.dot(
        full_motion_out, alpha_m[:, None] * gram_ab + beta_m[:, None] * gram_bb, precision=HIGHEST
    )
    lift_a = jnp.dot(
        full_motion_out, alpha_m[:, None] * gram_aa + beta_m[:, None] * gram_ab.T, precision=HIGHEST
    )
    unit_b = inv_x[:, None] * (lift_b - mean_x[:, None] * pool_b)
    unit_a = inv_x[:, None] * (lift_a - mean_x[:, None] * pool_a)
    unit_u = (unit_a - unit_b * mean_m) * inv_m
    pool_u = (pool_a - pool_b * mean_m) * inv_m
    back_x = full_motion_out * alpha_x[:, None]
    shifts[5] = first_t - jnp.sum(
        back_x * (shifts[6][:, None] * pool_b + spreads[6][:, None] * unit_b), axis=0
    ) / frame_total
    spreads[5] = second_t - jnp.sum(
        back_x * (shifts[6][:, None] * pool_u + spreads[6][:, None] * unit_u), axis=0
    ) / frame_total
    grad_lifted = alpha_x * (grad_x - fmask * (shifts[6] + unit_x * spreads[6]) / frame_total)
    grad_motion_out = jnp.einsum("cfo,cfr->or", grad_lifted, pooled, precision=HIGHEST)
    grad_pooled = jnp.einsum("cfo,or->cfr", grad_lifted, full_motion_out, precision=HIGHEST)
    grad_change = grad_pooled * vnext / area
    reduced_windows = later(
        fmask * (alpha_m * in_window + beta_m * jnp.sum(windows, axis=(0, 1))[:, None, None, None])
    )
    motion_tap_grad = jnp.sum(grad_change * reduced_windows, axis=(1, 2))
    grad_motion = (
        kmap[None, :, :, None, :] * earlier(grad_change)[:, None, None]
        - grad_change[:, None, None]
    ) * mask
    motion_grad = grad_raw(5, grad_motion, raw_m, mean_m, inv_m, mask, count).astype(BF)
    grad_motion_in = weight_grad(act_d, motion_grad)
    grad_act = grad_excited * attend_px + dot_t(motion_grad, full_motion_in)
    grad_narrow = grad_act * mask * silu_slope(norm_d)
    shifts[4], spreads[4] = sums(
        total_over(grad_narrow), total_over(grad_narrow * ((raw_d - mean_d) * inv_d))
    )
    narrow_grad = grad_raw(4, grad_narrow, raw_d, mean_d, inv_d, mask, count).astype(BF)
    grad_reduce2 = weight_grad(block_one, narrow_grad)
    grad_block = grad_total + dot_t(narrow_grad, full_reduce2)

    def by_owner(values):
        return values.astype(BF).reshape((dp, fsdp) + values.shape[1:]).swapaxes(0, 1)

    def scatter(*arrays):
        merged = jnp.concatenate([by_owner(a) for a in arrays], axis=2)
        merged = lax.psum_scatter(merged, "fsdp", scatter_dimension=0, tiled=False)
        merged = lax.psum_scatter(merged, "dp", scatter_dimension=0, tiled=False)
        out, begin = [], 0
        for a in arrays:
            out.append(merged[begin : begin + a.shape[1]].astype(F32))
            begin += a.shape[1]
        return out

    grad_kernels = jnp.stack(kernel_grads).reshape(27, devices, -1).swapaxes(0, 1)
    small_grads = jnp.concatenate(
        [
            grad_kernels.reshape(devices, -1),
            grad_motion_in.reshape(devices, -1),
            grad_motion_out.reshape(devices, -1),
        ],
        axis=1,
    )
    own_reduce2, own_expand2, own_small = scatter(
        grad_reduce2.reshape(devices, -1, middle),
        grad_expand2.reshape(devices, -1, middle),
        rows_of(small_grads),
    )
    own_small = own_small.reshape(-1)
    own_kernels = own_small[:size_s]
    own_motion = own_small[size_s : size_s + 2 * size_m].reshape(2, own, narrow)

    grad_one = grad_block * mask * silu_slope(sum_one)
    shifts[2], spreads[2], spreads[3] = sums(
        total_over(grad_one),
        total_over(grad_one * ((raw_c - mean_c) * inv_c)),
        total_over(grad_one * ((raw_p - mean_p) * inv_p)),
    )
    shifts[3] = shifts[2]
    widen_grad = grad_raw(2, grad_one, raw_c, mean_c, inv_c, mask, count).astype(BF)
    shortcut_grad = grad_raw(3, grad_one, raw_p, mean_p, inv_p, mask, count).astype(BF)
    grad_act_b = dot_t(widen_grad, full_expand1)
    grad_expand1 = weight_grad(act_b, widen_grad)
    grad_project1 = weight_grad(sampled, shortcut_grad)
    own_expand1, own_project1 = scatter(
        grad_expand1.reshape(devices, -1, wide), grad_project1.reshape(devices, -1, wide)
    )
    grad_sampled = dot_t(shortcut_grad, full_project1)
    grad_strided = grad_act_b * mask * silu_slope(raw_b * alpha_b + beta_b)
    shifts[1], spreads[1] = sums(
        total_over(grad_strided), total_over(grad_strided * ((raw_b - mean_b) * inv_b))
    )
    strided_grad = grad_raw(1, grad_strided, raw_b, mean_b, inv_b, mask, count).astype(BF)
    grad_spatial1 = weight_grad(cols_b, strided_grad)
    (own_spatial1,) = scatter(
        grad_spatial1.reshape(9, devices, own, middle)
        .swapaxes(0, 1)
        .reshape(devices, 9 * own, middle)
    )
    beyond = jnp.pad(strided_grad, ((0, 0), (0, 1), (0, 1), (0, 0), (0, 0)))
    here = beyond[:, :half, :half]
    right = beyond[:, :half, 1:]
    below = beyond[:, 1:, :half]
    both = beyond[:, 1:, 1:]

    def back_taps(*pairs_of):
        left = jnp.concatenate([p[0] for p in pairs_of], axis=-1)
        weight = jnp.concatenate([full_spatial1[p[1]] for p in pairs_of], axis=1)
        return dot_t(left, weight)

    even_even = back_taps((here, 4))
    even_odd = back_taps((here, 5), (right, 3))
    odd_even = back_taps((here, 7), (below, 1))
    odd_odd = back_taps((here, 8), (right, 6), (below, 2), (both, 0))
    grad_act_a = jnp.stack(
        [jnp.stack([even_even, even_odd], axis=3), jnp.stack([odd_even, odd_odd], axis=3)], axis=2
    ).reshape(slots, height, height, frames, middle)
    grad_first = grad_act_a * mask * silu_slope(raw_a * alpha_a + beta_a)
    shifts[0], spreads[0], motion_total, temporal_total = sums(
        total_over(grad_first),
        total_over(grad_first * ((raw_a - mean_a) * inv_a)),
        motion_tap_grad,
        jnp.stack(temporal_grads),
    )
    first_grad = grad_raw(0, grad_first, raw_a, mean_a, inv_a, mask, count_big).astype(BF)
    grad_reduce1 = weight_grad(feats, first_grad)
    (own_reduce1,) = scatter(grad_reduce1.reshape(devices, -1, middle))
    grad_inputs = dot_t(first_grad, full_reduce1)
    spread_sampled = jnp.pad(
        grad_sampled[:, :, None, :, None], ((0, 0), (0, 0), (0, 1), (0, 0), (0, 1), (0, 0), (0, 0))
    ).reshape(grad_inputs.shape)
    grad_features = (grad_inputs + spread_sampled).astype(BF)
    return (
        result.transpose(0, 3, 1, 2, 4),
        grad_features.transpose(0, 3, 1, 2, 4),
        own_reduce1,
        own_spatial1.reshape(9, own * middle),
        own_expand1,
        own_project1,
        own_reduce2,
        own_motion[0],
        own_motion[1],
        own_kernels.reshape(27, -1),
        own_expand2.reshape(-1, wide),
        jnp.concatenate(spreads),
        jnp.concatenate(shifts),
        motion_total,
        temporal_total,
    )


def solution(mesh):
    dp, fsdp = mesh.shape["dp"], mesh.shape["fsdp"]

    def run(*arrays):
        return local(dp, fsdp, *arrays)

    rows = P(AXES, None)
    columns = P(None, AXES)
    clips = P(AXES, None, None, None, None)
    return jax.shard_map(
        run,
        mesh=mesh,
        in_specs=(
            P(AXES),
            P(AXES),
            rows,
            clips,
            rows,
            columns,
            rows,
            rows,
            rows,
            rows,
            rows,
            columns,
            rows,
            P(),
            P(),
            P(),
            P(),
            clips,
        ),
        out_specs=(
            clips,
            clips,
            rows,
            columns,
            rows,
            rows,
            rows,
            rows,
            rows,
            columns,
            rows,
            P(),
            P(),
            P(),
            P(),
        ),
        check_vma=False,
    )
```

```python
import jax
import jax.numpy as jnp
from jax import lax
from jax.experimental import pallas as pl
from jax.experimental.pallas import tpu as pltpu
from jax.sharding import PartitionSpec as P

EPSILON = 1e-05
HIGHEST = lax.Precision.HIGHEST
AXES = ("dp", "fsdp")
BF = jnp.bfloat16
F32 = jnp.float32


def by_clip(values, frames):
    return values.reshape(values.shape[:-2] + (-1, frames, values.shape[-1]))


def earlier(values):
    return jnp.concatenate([jnp.zeros_like(values[..., :1, :]), values[..., :-1, :]], axis=-2)


def later(values):
    return jnp.concatenate([values[..., 1:, :], jnp.zeros_like(values[..., :1, :])], axis=-2)


def taps_of(values, size):
    padded = jnp.pad(values, ((1, 1), (1, 1), (0, 0), (0, 0), (0, 0)))
    return [padded[r : r + size, c : c + size] for r in range(3) for c in range(3)]


def dot(left, weight):
    shape = left.shape
    flat = jnp.dot(left.reshape(-1, shape[-1]), weight, preferred_element_type=F32)
    return flat.reshape(shape[:-1] + (weight.shape[1],))


def dot_t(grad, weight):
    shape = grad.shape
    flat = lax.dot_general(
        grad.reshape(-1, shape[-1]), weight, (((1,), (1,)), ((), ())), preferred_element_type=F32
    )
    return flat.reshape(shape[:-1] + (weight.shape[0],))


def weight_grad(left, grad):
    return lax.dot_general(
        left.reshape(-1, left.shape[-1]),
        grad.reshape(-1, grad.shape[-1]),
        (((0,), (0,)), ((), ())),
        preferred_element_type=F32,
    )


def silu_slope(values):
    sig = jax.nn.sigmoid(values)
    return sig * (1.0 + values * (1.0 - sig))


def total_over(values):
    return jnp.sum(values, axis=tuple(range(values.ndim - 1)))


def silu_parts(norm):
    sig = 1.0 / (1.0 + jnp.exp(-norm))
    return sig, norm * sig


def call(body, grid, ins, in_blocks, outs, out_blocks, scratch=(), limit=56, flops=0, moved=0):
    def spec(block):
        if block is None:
            return pl.BlockSpec(memory_space=pltpu.VMEM)
        return pl.BlockSpec(block[0], block[1])

    return pl.pallas_call(
        body,
        grid=grid,
        in_specs=[spec(b) for b in in_blocks],
        out_specs=[spec(b) for b in out_blocks],
        out_shape=[jax.ShapeDtypeStruct(s, d) for s, d in outs],
        scratch_shapes=list(scratch),
        compiler_params=pltpu.CompilerParams(
            vmem_limit_bytes=limit * 1024 * 1024,
            dimension_semantics=("arbitrary",) * len(grid),
        ),
        cost_estimate=pl.CostEstimate(flops=flops, bytes_accessed=moved, transcendentals=0),
    )(*ins)


def whole(shape):
    return shape, lambda *_: (0,) * len(shape)


def kernel_reduce1(feats, weight, mask, slots, height, frames):
    c_in, middle = weight.shape
    half = height // 2
    rows = half * height * frames

    def body(x_ref, w_ref, m_ref, raw_ref, sum_ref):
        first = (pl.program_id(0) == 0) & (pl.program_id(1) == 0)

        @pl.when(first)
        def _():
            sum_ref[...] = jnp.zeros_like(sum_ref)

        raw = jnp.dot(x_ref[...], w_ref[...], preferred_element_type=F32)
        raw = raw.reshape(half * height, frames, middle)
        raw_ref[...] = raw.reshape(half, height, frames, middle)
        weight8 = m_ref[:, :1]
        sum_ref[0] += jnp.sum(raw, axis=0) * weight8
        sum_ref[1] += jnp.sum(raw * raw, axis=0) * weight8

    return call(
        body,
        (slots, 2),
        (feats, weight, mask),
        (
            ((rows, c_in), lambda c, h: (c * 2 + h, 0)),
            whole(weight.shape),
            ((frames, mask.shape[1]), lambda c, h: (c, 0)),
        ),
        (
            ((height, height, slots * frames, middle), F32),
            ((2, frames, middle), F32),
        ),
        (
            ((half, height, frames, middle), lambda c, h: (h, 0, c, 0)),
            whole((2, frames, middle)),
        ),
        flops=2 * feats.shape[0] * c_in * middle,
        moved=feats.size * 2 + feats.shape[0] * middle * 4,
    )


def kernel_conv_down(raw_a, alpha, beta, mask, taps):
    height, _, batch, middle = raw_a.shape
    half = height // 2
    rows = half * batch

    def body(a_ref, al_ref, be_ref, m_ref, *refs):
        w_refs, (act_ref, raw_ref, sum_ref, cols, w_ref) = refs[:9], refs[9:]
        step = pl.program_id(0)
        wide = 3 * middle

        @pl.when(step == 0)
        def _():
            sum_ref[...] = jnp.zeros_like(sum_ref)
            cols[...] = jnp.zeros_like(cols)
            for t in range(9):
                w_ref[t * middle : (t + 1) * middle] = taps[t].of(w_refs[t], 0)

        @pl.when(step > 0)
        def _():
            cols[:, :wide] = cols[:, 2 * wide :]

        al, be, m = al_ref[...], be_ref[...], m_ref[:, :1]
        for p in range(2):
            base = (1 + p) * wide
            for j in range(half):
                for q in range(2):
                    norm = a_ref[p, 2 * j + q] * al + be
                    act = (silu_parts(norm)[1] * m).astype(BF)
                    act_ref[p, 2 * j + q] = act
                    lane = base + (1 + q) * middle
                    cols[j * batch : (j + 1) * batch, lane : lane + middle] = act
                    if q == 1 and j + 1 < half:
                        cols[(j + 1) * batch : (j + 2) * batch, base : base + middle] = act
        raw = jnp.dot(cols[...], w_ref[...], preferred_element_type=F32)
        raw = raw.reshape(half, batch, middle)
        raw_ref[0] = raw
        sum_ref[0] += jnp.sum(raw, axis=0) * m
        sum_ref[1] += jnp.sum(raw * raw, axis=0) * m

    return call(
        body,
        (half,),
        (raw_a, alpha, beta, mask) + tuple(t.array for t in taps),
        (
            ((2, height, batch, middle), lambda i: (i, 0, 0, 0)),
            whole(alpha.shape),
            whole(beta.shape),
            whole(mask.shape),
        )
        + tuple(t.block() for t in taps),
        (
            (raw_a.shape, BF),
            ((half, half, batch, middle), F32),
            ((2, batch, middle), F32),
        ),
        (
            ((2, height, batch, middle), lambda i: (i, 0, 0, 0)),
            ((1, half, batch, middle), lambda i: (i, 0, 0, 0)),
            whole((2, batch, middle)),
        ),
        scratch=[pltpu.VMEM((rows, 9 * middle), BF), pltpu.VMEM((9 * middle, middle), BF)],
        flops=2 * half * rows * 9 * middle * middle,
        moved=raw_a.size * 6 + 18 * middle * middle,
    )


def kernel_conv_down_weights(act_a, grad):
    height, _, batch, middle = act_a.shape
    half = height // 2
    split = act_a.reshape(half, 2, half, 2, batch, middle)

    def body(a_ref, g_ref, out_ref, cols):
        step = pl.program_id(0)
        for r in range(3):
            for c in range(3):
                top, left = int(r == 0), int(c == 0)

                @pl.when(step == r * 3 + c)
                def _(r=r, c=c, top=top, left=left):
                    if top:
                        cols[0] = jnp.zeros_like(cols[0])
                    if left:
                        cols[:, 0] = jnp.zeros_like(cols[:, 0])
                    cols[top:, left:] = a_ref[
                        : half - top, int(r != 1), : half - left, int(c != 1)
                    ]

        taps = cols[...].reshape(half * half * batch, middle)
        out_ref[0] = lax.dot_general(
            taps, g_ref[...], (((0,), (0,)), ((), ())), preferred_element_type=F32
        ).astype(BF)

    return call(
        body,
        (9,),
        (split, grad.reshape(-1, middle)),
        (whole(split.shape), whole((half * half * batch, middle))),
        (((9, middle, middle), BF),),
        (((1, middle, middle), lambda t: (t, 0, 0)),),
        scratch=[pltpu.VMEM((half, half, batch, middle), BF)],
        flops=2 * half * half * batch * 9 * middle * middle,
        moved=act_a.size * 2 + grad.size * 2 + 18 * middle * middle,
    )[0]


def kernel_conv_down_back(grad, taps, raw_a, stats, mask):
    height, _, batch, middle = raw_a.shape
    half = height // 2
    rows = half * batch

    def body(g_ref, n_ref, a_ref, s_ref, m_ref, *refs):
        w_refs, (out_ref, sum_ref, here, below) = refs[:9], refs[9:]
        step = pl.program_id(0)

        @pl.when(step == 0)
        def _():
            sum_ref[...] = jnp.zeros_like(sum_ref)
            here[half] = jnp.zeros_like(here[half])
            below[half] = jnp.zeros_like(below[half])

        here[:half] = g_ref[0]

        @pl.when(step < half - 1)
        def _():
            below[:half] = n_ref[0]

        @pl.when(step == half - 1)
        def _():
            below[:half] = jnp.zeros_like(n_ref[0])

        def tap(ref, right, t):
            return lax.dot_general(
                ref[right : right + half].reshape(rows, middle),
                taps[t].of(w_refs[t], 0),
                (((1,), (1,)), ((), ())),
                preferred_element_type=F32,
            )

        al, be = s_ref[0:1], s_ref[1:2]
        mean, inv = s_ref[2:3], s_ref[3:4]
        m = m_ref[:, :1]
        plans = (
            (0, 0, ((here, 0, 4),)),
            (0, 1, ((here, 0, 5), (here, 1, 3))),
            (1, 0, ((here, 0, 7), (below, 0, 1))),
            (1, 1, ((here, 0, 8), (here, 1, 6), (below, 0, 2), (below, 1, 0))),
        )
        for p, q, parts in plans:
            back = tap(*parts[0])
            for part in parts[1:]:
                back = back + tap(*part)
            raw = a_ref[0, p, :, q]
            norm = raw * al + be
            sig, act = silu_parts(norm)
            slope = sig + act * (1.0 - sig)
            out = back.reshape(half, batch, middle) * slope * m
            out_ref[0, p, :, q] = out
            sum_ref[0] += jnp.sum(out, axis=0)
            sum_ref[1] += jnp.sum(out * ((raw - mean) * inv), axis=0)

    return call(
        body,
        (half,),
        (grad, grad, raw_a.reshape(half, 2, half, 2, batch, middle), stats, mask)
        + tuple(t.array for t in taps),
        (
            ((1, half, batch, middle), lambda i: (i, 0, 0, 0)),
            ((1, half, batch, middle), lambda i: (jnp.minimum(i + 1, half - 1), 0, 0, 0)),
            ((1, 2, half, 2, batch, middle), lambda i: (i, 0, 0, 0, 0, 0)),
            whole(stats.shape),
            whole(mask.shape),
        )
        + tuple(t.block() for t in taps),
        (
            ((half, 2, half, 2, batch, middle), F32),
            ((2, batch, middle), F32),
        ),
        (
            ((1, 2, half, 2, batch, middle), lambda i: (i, 0, 0, 0, 0, 0)),
            whole((2, batch, middle)),
        ),
        scratch=[pltpu.VMEM((half + 1, batch, middle), BF), pltpu.VMEM((half + 1, batch, middle), BF)],
        flops=2 * half * rows * 9 * middle * middle,
        moved=raw_a.size * 8 + 18 * middle * middle,
    )


def kernel_first_grad(grad, raw_a, feats, stats, mask, slots, frames):
    height, _, batch, middle = raw_a.shape
    half = height // 2
    rows = half * height * frames
    c_in = feats.shape[1]

    def body(g_ref, a_ref, x_ref, s_ref, m_ref, out_ref, w_ref, acc):
        first = (pl.program_id(0) == 0) & (pl.program_id(1) == 0)
        last = (pl.program_id(0) == slots - 1) & (pl.program_id(1) == 1)

        @pl.when(first)
        def _():
            acc[...] = jnp.zeros_like(acc)

        scale, mean, inv = s_ref[0:1], s_ref[1:2], s_ref[2:3]
        shift, spread = s_ref[3:4], s_ref[4:5]
        m = m_ref[:, :1]
        unit = (a_ref[...] - mean) * inv
        value = scale * (g_ref[...] - m * (shift + unit * spread))
        value = value.reshape(rows, middle).astype(BF)
        out_ref[...] = value
        acc[...] += lax.dot_general(
            x_ref[...], value, (((0,), (0,)), ((), ())), preferred_element_type=F32
        )

        @pl.when(last)
        def _():
            w_ref[...] = acc[...].astype(BF)

    block = (half, height, frames, middle)
    return call(
        body,
        (slots, 2),
        (grad.reshape(raw_a.shape), raw_a, feats, stats, mask),
        (
            (block, lambda c, h: (h, 0, c, 0)),
            (block, lambda c, h: (h, 0, c, 0)),
            ((rows, c_in), lambda c, h: (c * 2 + h, 0)),
            whole(stats.shape),
            ((frames, mask.shape[1]), lambda c, h: (c, 0)),
        ),
        (
            ((slots * 2 * rows, middle), BF),
            ((c_in, middle), BF),
        ),
        (
            ((rows, middle), lambda c, h: (c * 2 + h, 0)),
            whole((c_in, middle)),
        ),
        scratch=[pltpu.VMEM((c_in, middle), F32)],
        flops=2 * raw_a.size * c_in,
        moved=raw_a.size * 10 + feats.size * 2,
    )


def kernel_grad_features(grad, weight, sampled, height, slots, frames):
    c_in, middle = weight.shape
    half = height // 2
    rows = height * height * frames

    def body(g_ref, w_ref, s_ref, out_ref):
        value = lax.dot_general(
            g_ref[...], w_ref[...], (((1,), (1,)), ((), ())), preferred_element_type=F32
        )
        value = value.reshape(half, 2, half, 2, frames, c_in)
        even = value[:, 0, :, 0] + s_ref[...]
        line = jnp.stack([even, value[:, 0, :, 1]], axis=2)
        both = jnp.stack([line, value[:, 1]], axis=1)
        out_ref[...] = both.reshape(rows, c_in).astype(BF)

    return call(
        body,
        (slots,),
        (grad, weight, sampled),
        (
            ((rows, middle), lambda c: (c, 0)),
            whole(weight.shape),
            ((half, half, frames, c_in), lambda c: (0, 0, c, 0)),
        ),
        (((slots * rows, c_in), BF),),
        (((rows, c_in), lambda c: (c, 0)),),
        flops=2 * grad.size * c_in,
        moved=grad.size * 2 + slots * rows * c_in * 2 + sampled.size * 4,
    )[0]


CHUNK = 256


def fold(value):
    return jnp.sum(value.reshape(-1, 8, value.shape[-1]), axis=0)


def chunks(width):
    return [slice(b, min(b + CHUNK, width)) for b in range(0, width, CHUNK)]


def zero_first(*refs):
    @pl.when(pl.program_id(0) == 0)
    def _():
        for ref in refs:
            ref[...] = jnp.zeros_like(ref)


def row_block(half, batch, width):
    return (half, batch, width), lambda i: (i, 0, 0)


class Packed:
    def __init__(self, array, rows, first, count):
        self.array, self.rows, self.first, self.count = array, rows, first, count

    def block(self):
        size, index = self.rows * self.count, self.first // self.count
        return (self.array.shape[0], size, self.array.shape[2]), lambda *_: (0, index, 0)

    def of(self, ref, k):
        part = ref[:, k * self.rows : (k + 1) * self.rows, :]
        return part.reshape(-1, part.shape[-1])


def nt(left, right):
    return lax.dot_general(left, right, (((1,), (1,)), ((), ())), preferred_element_type=F32)


def tn(left, right):
    return lax.dot_general(left, right, (((0,), (0,)), ((), ())), preferred_element_type=F32)


def nn(left, right):
    return jnp.dot(left, right, preferred_element_type=F32)


def kernel_expand(raw_b, stats, mask, weight, half):
    _, batch, middle = raw_b.shape
    wide = weight.count * middle
    rows = half * batch

    def body(b_ref, s_ref, m_ref, w_ref, act_ref, raw_ref, sum_ref):
        zero_first(sum_ref)
        m = m_ref[...]

        @pl.loop(0, half)
        def _(j):
            for c in chunks(middle):
                norm = b_ref[j, :, c] * s_ref[0:1, c] + s_ref[1:2, c]
                act_ref[j, :, c] = (silu_parts(norm)[1] * m).astype(BF)

        m = m_ref[:, :1]
        act = act_ref[...].reshape(rows, middle)
        for k in range(weight.count):
            raw = nn(act, weight.of(w_ref, k)).reshape(half, batch, middle)
            span = slice(k * middle, (k + 1) * middle)
            raw_ref[:, :, span] = raw
            sum_ref[0, :, span] += fold(jnp.sum(raw, axis=0) * m)
            sum_ref[1, :, span] += fold(jnp.sum(raw * raw, axis=0) * m)

    pixels = half * half
    return call(
        body,
        (half,),
        (raw_b, stats, mask, weight.array),
        (row_block(half, batch, middle), whole(stats.shape), whole(mask.shape), weight.block()),
        (
            ((pixels, batch, middle), BF),
            ((pixels, batch, wide), F32),
            ((2, 8, wide), F32),
        ),
        (row_block(half, batch, middle), row_block(half, batch, wide), whole((2, 8, wide))),
        flops=2 * raw_b.size * wide,
        moved=raw_b.size * 6 + pixels * batch * wide * 4,
    )


def kernel_project(sampled, mask, weight, half):
    pixels, batch, c_in = sampled.shape
    middle = weight.array.shape[2]
    wide = weight.count * middle

    def body(x_ref, m_ref, w_ref, raw_ref, sum_ref):
        zero_first(sum_ref)
        m = m_ref[:, :1]
        left = x_ref[...].reshape(half * batch, c_in)
        for k in range(weight.count):
            raw = nn(left, weight.of(w_ref, k)).reshape(half, batch, middle)
            span = slice(k * middle, (k + 1) * middle)
            raw_ref[:, :, span] = raw
            sum_ref[0, :, span] += fold(jnp.sum(raw, axis=0) * m)
            sum_ref[1, :, span] += fold(jnp.sum(raw * raw, axis=0) * m)

    return call(
        body,
        (half,),
        (sampled, mask, weight.array),
        (row_block(half, batch, c_in), whole(mask.shape), weight.block()),
        (((pixels, batch, wide), F32), ((2, 8, wide), F32)),
        (row_block(half, batch, wide), whole((2, 8, wide))),
        flops=2 * sampled.size * wide,
        moved=sampled.size * 2 + pixels * batch * wide * 4,
    )


def kernel_block_one(raw_c, raw_p, stats, mask, weight, half):
    pixels, batch, wide = raw_c.shape
    middle = weight.array.shape[2]

    def body(c_ref, p_ref, s_ref, m_ref, w_ref, one_ref, raw_ref, sum_ref):
        zero_first(sum_ref)
        m = m_ref[...]

        @pl.loop(0, half)
        def _(j):
            for c in chunks(wide):
                total = c_ref[j, :, c] * s_ref[0:1, c] + p_ref[j, :, c] * s_ref[1:2, c] + s_ref[2:3, c]
                one_ref[j, :, c] = (silu_parts(total)[1] * m).astype(BF)

        m = m_ref[:, :1]
        raw = nn(one_ref[...].reshape(half * batch, wide), weight.of(w_ref, 0))
        raw = raw.reshape(half, batch, middle)
        raw_ref[...] = raw
        sum_ref[0] += fold(jnp.sum(raw, axis=0) * m)
        sum_ref[1] += fold(jnp.sum(raw * raw, axis=0) * m)

    return call(
        body,
        (half,),
        (raw_c, raw_p, stats, mask, weight.array),
        (
            row_block(half, batch, wide),
            row_block(half, batch, wide),
            whole(stats.shape),
            whole(mask.shape),
            weight.block(),
        ),
        (
            ((pixels, batch, wide), BF),
            ((pixels, batch, middle), F32),
            ((2, 8, middle), F32),
        ),
        (row_block(half, batch, wide), row_block(half, batch, middle), whole((2, 8, middle))),
        flops=2 * raw_c.size * middle,
        moved=raw_c.size * 10,
    )


def kernel_result(raw_e, block_one, cot, stats, mask, half):
    pixels, batch, wide = raw_e.shape

    def body(e_ref, o_ref, g_ref, s_ref, m_ref, res_ref, grad_ref, sum_ref):
        zero_first(sum_ref)
        m = m_ref[...]

        @pl.loop(0, half)
        def _(j):
            for c in chunks(wide):
                raw = e_ref[j, :, c]
                total = raw * s_ref[0:1, c] + s_ref[1:2, c] + o_ref[j, :, c].astype(F32)
                sig, act = silu_parts(total)
                res_ref[j, :, c] = (act * m).astype(BF)
                grad = g_ref[j, :, c].astype(F32) * m * (sig + act * (1.0 - sig))
                grad_ref[j, :, c] = grad
                sum_ref[0, :, c] += fold(grad)
                sum_ref[1, :, c] += fold(grad * ((raw - s_ref[2:3, c]) * s_ref[3:4, c]))

    return call(
        body,
        (half,),
        (raw_e, block_one, cot, stats, mask),
        (
            row_block(half, batch, wide),
            row_block(half, batch, wide),
            row_block(half, batch, wide),
            whole(stats.shape),
            whole(mask.shape),
        ),
        (
            ((pixels, batch, wide), BF),
            ((pixels, batch, wide), F32),
            ((2, 8, wide), F32),
        ),
        (row_block(half, batch, wide), row_block(half, batch, wide), whole((2, 8, wide))),
        flops=20 * raw_e.size,
        moved=raw_e.size * 14,
    )


def kernel_block_back(grad_narrow, raw_d, stats_d, weight, grad_total, raw_c, raw_p, stats, mask, half):
    pixels, batch, wide = raw_c.shape
    middle = raw_d.shape[2]

    def body(n_ref, d_ref, sd_ref, w_ref, t_ref, c_ref, p_ref, s_ref, m_ref, nar_ref, one_ref, sum_ref, back):
        zero_first(sum_ref)
        m = m_ref[...]

        @pl.loop(0, half)
        def _(j):
            for c in chunks(middle):
                unit = (d_ref[j, :, c] - sd_ref[1:2, c]) * sd_ref[2:3, c]
                value = sd_ref[0:1, c] * (
                    n_ref[j, :, c] - m * (sd_ref[3:4, c] + unit * sd_ref[4:5, c])
                )
                nar_ref[j, :, c] = value.astype(BF)

        left = nar_ref[...].reshape(half * batch, middle)
        back[...] = nt(left, weight.of(w_ref, 0)).reshape(half, batch, wide)

        @pl.loop(0, half)
        def _(j):
            for c in chunks(wide):
                raw_c, raw_p = c_ref[j, :, c], p_ref[j, :, c]
                total = raw_c * s_ref[0:1, c] + raw_p * s_ref[1:2, c] + s_ref[2:3, c]
                sig, act = silu_parts(total)
                grad = (t_ref[j, :, c] + back[j, :, c]) * m * (sig + act * (1.0 - sig))
                one_ref[j, :, c] = grad
                sum_ref[0, :, c] += fold(grad)
                sum_ref[1, :, c] += fold(grad * ((raw_c - s_ref[3:4, c]) * s_ref[4:5, c]))
                sum_ref[2, :, c] += fold(grad * ((raw_p - s_ref[5:6, c]) * s_ref[6:7, c]))

    return call(
        body,
        (half,),
        (grad_narrow, raw_d, stats_d, weight.array, grad_total, raw_c, raw_p, stats, mask),
        (
            row_block(half, batch, middle),
            row_block(half, batch, middle),
            whole(stats_d.shape),
            weight.block(),
            row_block(half, batch, wide),
            row_block(half, batch, wide),
            row_block(half, batch, wide),
            whole(stats.shape),
            whole(mask.shape),
        ),
        (
            ((pixels, batch, middle), BF),
            ((pixels, batch, wide), F32),
            ((3, 8, wide), F32),
        ),
        (row_block(half, batch, middle), row_block(half, batch, wide), whole((3, 8, wide))),
        scratch=[pltpu.VMEM((half, batch, wide), F32)],
        flops=2 * raw_c.size * middle,
        moved=raw_c.size * 16,
    )


def kernel_expand_back(grad_one, raw_c, raw_p, stats, weight, raw_b, stats_b, mask, half):
    pixels, batch, wide = raw_c.shape
    middle = raw_b.shape[2]

    def body(g_ref, c_ref, p_ref, s_ref, w_ref, b_ref, sb_ref, m_ref, wid_ref, sho_ref, out_ref, sum_ref):
        zero_first(sum_ref)
        m = m_ref[...]

        @pl.loop(0, half)
        def _(j):
            for c in chunks(wide):
                grad = g_ref[j, :, c]
                for raw_ref, to_ref, k in ((c_ref, wid_ref, 0), (p_ref, sho_ref, 5)):
                    unit = (raw_ref[j, :, c] - s_ref[k + 1 : k + 2, c]) * s_ref[k + 2 : k + 3, c]
                    value = s_ref[k : k + 1, c] * (
                        grad - m * (s_ref[k + 3 : k + 4, c] + unit * s_ref[k + 4 : k + 5, c])
                    )
                    to_ref[j, :, c] = value.astype(BF)

        m = m_ref[:, :1]
        back = None
        for k in range(weight.count):
            left = wid_ref[:, :, k * middle : (k + 1) * middle].reshape(half * batch, middle)
            part = nt(left, weight.of(w_ref, k))
            back = part if back is None else back + part
        raw = b_ref[...]
        sig, act = silu_parts(raw * sb_ref[0:1] + sb_ref[1:2])
        grad = back.reshape(half, batch, middle) * m * (sig + act * (1.0 - sig))
        out_ref[...] = grad
        sum_ref[0] += fold(jnp.sum(grad, axis=0))
        sum_ref[1] += fold(jnp.sum(grad * ((raw - sb_ref[2:3]) * sb_ref[3:4]), axis=0))

    return call(
        body,
        (half,),
        (grad_one, raw_c, raw_p, stats, weight.array, raw_b, stats_b, mask),
        (
            row_block(half, batch, wide),
            row_block(half, batch, wide),
            row_block(half, batch, wide),
            whole(stats.shape),
            weight.block(),
            row_block(half, batch, middle),
            whole(stats_b.shape),
            whole(mask.shape),
        ),
        (
            ((pixels, batch, wide), BF),
            ((pixels, batch, wide), BF),
            ((pixels, batch, middle), F32),
            ((2, 8, middle), F32),
        ),
        (
            row_block(half, batch, wide),
            row_block(half, batch, wide),
            row_block(half, batch, middle),
            whole((2, 8, middle)),
        ),
        flops=2 * raw_c.size * middle,
        moved=raw_c.size * 16,
    )


def kernel_sampled_back(grad, weight, half):
    pixels, batch, wide = grad.shape
    middle = weight.array.shape[2]
    c_in = weight.array.shape[0] * weight.rows

    def body(g_ref, w_ref, out_ref):
        back = None
        for k in range(weight.count):
            left = g_ref[:, :, k * middle : (k + 1) * middle].reshape(half * batch, middle)
            part = nt(left, weight.of(w_ref, k))
            back = part if back is None else back + part
        out_ref[...] = back.reshape(half, batch, c_in)

    return call(
        body,
        (half,),
        (grad, weight.array),
        (row_block(half, batch, wide), weight.block()),
        (((pixels, batch, c_in), F32),),
        (row_block(half, batch, c_in),),
        flops=2 * grad.size * c_in,
        moved=grad.size * 2 + pixels * batch * c_in * 4,
    )[0]


def kernel_join(excited, outputs, raw_g, stats_g, mask, weight, half):
    pixels, batch, middle = excited.shape
    group = middle // 4
    wide = weight.count * middle

    def body(x_ref, o1, o2, r_ref, sg_ref, m_ref, w_ref, join_ref, raw_ref, sum_ref):
        zero_first(sum_ref)
        m = m_ref[:, :group]
        join_ref[:, :, :group] = x_ref[...]
        join_ref[:, :, group : 2 * group] = o1[...]
        join_ref[:, :, 2 * group : 3 * group] = o2[...]
        act = silu_parts(r_ref[...] * sg_ref[0:1] + sg_ref[1:2])[1] * m
        join_ref[:, :, 3 * group :] = act.astype(BF)
        left = join_ref[...].reshape(half * batch, middle)
        m = m_ref[:, :1]
        for k in range(weight.count):
            raw = nn(left, weight.of(w_ref, k)).reshape(half, batch, middle)
            span = slice(k * middle, (k + 1) * middle)
            raw_ref[:, :, span] = raw
            sum_ref[0, :, span] += fold(jnp.sum(raw, axis=0) * m)
            sum_ref[1, :, span] += fold(jnp.sum(raw * raw, axis=0) * m)

    part = row_block(half, batch, group)
    return call(
        body,
        (half,),
        (excited, outputs[0], outputs[1], raw_g, stats_g, mask, weight.array),
        (part, part, part, part, whole(stats_g.shape), whole(mask.shape), weight.block()),
        (((pixels, batch, middle), BF), ((pixels, batch, wide), F32), ((2, 8, wide), F32)),
        (row_block(half, batch, middle), row_block(half, batch, wide), whole((2, 8, wide))),
        flops=2 * excited.size * wide,
        moved=excited.size * 4 + pixels * batch * wide * 4,
    )


def kernel_final_back(grad_total, raw_e, stats, mask, weight, raw_g, stats_g, half):
    pixels, batch, wide = raw_e.shape
    middle = weight.array.shape[2]
    group = middle // 4

    def body(g_ref, e_ref, s_ref, m_ref, w_ref, r_ref, sg_ref, fin_ref, out_ref, pre_ref, sum_ref):
        zero_first(sum_ref)
        m = m_ref[...]

        @pl.loop(0, half)
        def _(j):
            for c in chunks(wide):
                unit = (e_ref[j, :, c] - s_ref[1:2, c]) * s_ref[2:3, c]
                value = s_ref[0:1, c] * (
                    g_ref[j, :, c] - m * (s_ref[3:4, c] + unit * s_ref[4:5, c])
                )
                fin_ref[j, :, c] = value.astype(BF)

        back = None
        for k in range(weight.count):
            left = fin_ref[:, :, k * middle : (k + 1) * middle].reshape(half * batch, middle)
            part = nt(left, weight.of(w_ref, k))
            back = part if back is None else back + part
        back = back.reshape(half, batch, middle)
        out_ref[...] = back
        raw = r_ref[...]
        sig, act = silu_parts(raw * sg_ref[0:1] + sg_ref[1:2])
        pre = back[:, :, 3 * group :] * m_ref[:, :group] * (sig + act * (1.0 - sig))
        pre_ref[...] = pre
        sum_ref[0] += fold(jnp.sum(pre, axis=0))
        sum_ref[1] += fold(jnp.sum(pre * (raw - sg_ref[2:3]), axis=0))

    part = row_block(half, batch, group)
    return call(
        body,
        (half,),
        (grad_total, raw_e, stats, mask, weight.array, raw_g, stats_g),
        (
            row_block(half, batch, wide),
            row_block(half, batch, wide),
            whole(stats.shape),
            whole(mask.shape),
            weight.block(),
            part,
            whole(stats_g.shape),
        ),
        (
            ((pixels, batch, wide), BF),
            ((pixels, batch, middle), F32),
            ((pixels, batch, group), F32),
            ((2, 8, group), F32),
        ),
        (row_block(half, batch, wide), row_block(half, batch, middle), part, whole((2, 8, group))),
        flops=2 * raw_e.size * middle,
        moved=raw_e.size * 10,
    )


def kernel_weight_grad(left, right, dp, fsdp, rows, first, total, into=None):
    pixels, batch, depth = left.shape
    columns = right.shape[2]
    middle = min(columns, 512)
    owners = dp * fsdp

    def body(*refs):
        a_ref, b_ref, out_ref = refs[0], refs[1], refs[-1]
        value = tn(a_ref[...].reshape(-1, depth), b_ref[...].reshape(-1, middle)).astype(BF)
        value = value.reshape(dp, fsdp, rows, middle)
        for d in range(dp):
            out_ref[:, d] = value[d]

    ins = (left, right)
    in_specs = [
        pl.BlockSpec((pixels, batch, depth), lambda k: (0, 0, 0)),
        pl.BlockSpec((pixels, batch, middle), lambda k: (0, 0, k)),
    ]
    alias = {}
    if into is not None:
        ins += (into,)
        in_specs.append(pl.BlockSpec(memory_space=pl.ANY))
        alias = {2: 0}
    return pl.pallas_call(
        body,
        grid=(columns // middle,),
        in_specs=in_specs,
        out_specs=pl.BlockSpec((fsdp, dp, rows, middle), lambda k: (0, 0, first + k, 0)),
        out_shape=jax.ShapeDtypeStruct((fsdp, dp, total, middle), BF),
        input_output_aliases=alias,
        compiler_params=pltpu.CompilerParams(
            vmem_limit_bytes=56 * 1024 * 1024, dimension_semantics=("arbitrary",)
        ),
        cost_estimate=pl.CostEstimate(
            flops=2 * left.size * columns,
            bytes_accessed=left.size * 2 + right.size * 2 + owners * rows * columns * 2,
            transcendentals=0,
        ),
    )(*ins)


def frame_rows(rows):
    return lax.broadcasted_iota(jnp.int32, (1, rows, 128), 1)


def shift_frames(value, frames):
    shape = value.shape
    value = value.reshape(-1, frames, 128)
    spot = frame_rows(frames)
    before = jnp.where(spot == 0, 0.0, pltpu.roll(value, 1, 1))
    after_ = jnp.where(spot == frames - 1, 0.0, pltpu.roll(value, frames - 1, 1))
    return before.reshape(shape), after_.reshape(shape)


def nine_taps(pad, cols, half, batch):
    for r in range(3):
        for c in range(3):
            lane = (r * 3 + c) * 128
            part = pad[r : r + half, c : c + half]
            cols[:, lane : lane + 128] = part.reshape(half * half * batch, 128)


def clear_border(pad, half):
    pad[0] = jnp.zeros_like(pad[0])
    pad[half + 1] = jnp.zeros_like(pad[0])
    pad[:, 0] = jnp.zeros_like(pad[:, 0])
    pad[:, half + 1] = jnp.zeros_like(pad[:, 0])


def kernel_motion(rows_d, stats, mask, weight, windows, half):
    pixels, batch, middle = rows_d.shape
    narrow = weight.shape[1]

    def body(d_ref, s_ref, m_ref, w_ref, act_ref, raw_ref, win_ref, sq_ref):
        for c in chunks(middle):
            al, be, m = s_ref[0:1, c], s_ref[1:2, c], m_ref[...]

            @pl.loop(0, half)
            def _(i):
                for j in range(half):
                    act = silu_parts(d_ref[i * half + j, :, c] * al + be)[1] * m
                    act_ref[i * half + j, :, c] = act.astype(BF)

        raw = nn(act_ref[...].reshape(pixels * batch, middle), w_ref[...])
        raw_ref[...] = raw.reshape(pixels, batch, narrow)
        square = jnp.zeros((batch, narrow), F32)
        sums = [jnp.zeros((batch, narrow), F32) for _ in range(9)]
        for p in range(pixels):
            value = raw_ref[p]
            square = square + value * value
            for t in range(9):
                if windows[p // half][p % half][t]:
                    sums[t] = sums[t] + value
        for t in range(9):
            win_ref[t] = sums[t]
        sq_ref[...] = square

    return call(
        body,
        (1,),
        (rows_d, stats, mask, weight),
        (whole(rows_d.shape), whole(stats.shape), whole(mask.shape), whole(weight.shape)),
        (
            (rows_d.shape, BF),
            ((pixels, batch, narrow), F32),
            ((9, batch, narrow), F32),
            ((batch, narrow), F32),
        ),
        (
            whole(rows_d.shape),
            whole((pixels, batch, narrow)),
            whole((9, batch, narrow)),
            whole((batch, narrow)),
        ),
        flops=2 * rows_d.size * narrow,
        moved=rows_d.size * 6,
    )


def kernel_group(source, extra, taps, weight, mask, index, half, frames):
    pixels, batch, middle = source.shape
    group = 128

    def body(*refs):
        if index == 1:
            x_ref, e_ref, t_ref, w_ref, m_ref, first_ref, pad_ref, raw_ref, sum_ref, cols = refs
            excited = (x_ref[...].astype(F32) * e_ref[...]).astype(BF)
            first_ref[...] = excited
            piece = first_ref[:, :, group : 2 * group].astype(F32)
        else:
            x_ref, r_ref, s_ref, t_ref, w_ref, m_ref, first_ref, pad_ref, raw_ref, sum_ref, cols = refs
            act = silu_parts(r_ref[...] * s_ref[0:1] + s_ref[1:2])[1] * m_ref[:, :group]
            first_ref[...] = act.astype(BF)
            piece = x_ref[...].astype(F32) + first_ref[...].astype(F32)
        before, after_ = shift_frames(piece, frames)
        value = t_ref[0:1] * before + t_ref[1:2] * piece + t_ref[2:3] * after_
        clear_border(pad_ref, half)
        pad_ref[1 : half + 1, 1 : half + 1] = value.astype(BF).reshape(half, half, batch, group)
        nine_taps(pad_ref, cols, half, batch)
        raw = nn(cols[...], w_ref[...]).reshape(pixels, batch, group)
        raw_ref[...] = raw
        m = m_ref[:, :group]
        sum_ref[0] = fold(jnp.sum(raw, axis=0) * m)
        sum_ref[1] = fold(jnp.sum(raw * raw, axis=0) * m)

    block = (pixels, batch, group)
    if index == 1:
        ins = (source, extra, taps, weight, mask)
        first = (source.shape, BF)
        specs = tuple(whole(a.shape) for a in ins)
    else:
        ins = (source, extra[0], extra[1], taps, weight, mask)
        first = (block, BF)
        specs = ((block, lambda i: (0, 0, index)),) + tuple(whole(a.shape) for a in ins[1:])
    outs = (
        first,
        ((half + 2, half + 2, batch, group), BF),
        (block, F32),
        ((2, 8, group), F32),
    )
    return call(
        body,
        (1,),
        ins,
        specs,
        outs,
        tuple(whole(o[0]) for o in outs),
        scratch=[pltpu.VMEM((pixels * batch, 9 * group), BF)],
        flops=2 * pixels * batch * 9 * group * group,
        moved=pixels * batch * group * 12,
    )


def kernel_group_weights(pad, grad, half):
    pixels, batch, group = grad.shape

    def body(p_ref, g_ref, out_ref, cols):
        nine_taps(p_ref, cols, half, batch)
        out_ref[...] = tn(cols[...], g_ref[...].reshape(pixels * batch, group)).astype(BF)

    return call(
        body,
        (1,),
        (pad, grad),
        (whole(pad.shape), whole(grad.shape)),
        (((9 * group, group), BF),),
        (whole((9 * group, group)),),
        scratch=[pltpu.VMEM((pixels * batch, 9 * group), BF)],
        flops=2 * grad.size * 9 * group,
        moved=grad.size * 6,
    )[0]


def kernel_group_back(
    grad, raw, stats, weight, taps, excited, previous, joined, lower, mask, index, half, frames
):
    pixels, batch, group = grad.shape
    block = (pixels, batch, group)
    rows = pixels * batch

    def body(*refs):
        g_ref, r_ref, s_ref, w_ref, t_ref, x_ref, j_ref, m_ref = refs[:8]
        pad, cols = refs[-2:]
        m = m_ref[:, :group]
        raw = r_ref[...]
        value = s_ref[0:1] * g_ref[...] - m * (s_ref[2:3] + (raw - s_ref[1:2]) * s_ref[3:4])
        if index > 1:
            p_ref, l_ref, ls_ref, gg_ref, gp_ref, tg_ref, pre_ref, sum_ref = refs[8:16]
        else:
            g2_ref, g3_ref, d_ref, gg_ref, gp_ref, tg_ref, at_ref = refs[8:15]
        gg_ref[...] = value.astype(BF)
        clear_border(pad, half)
        pad[1 : half + 1, 1 : half + 1] = gg_ref[...].reshape(half, half, batch, group)
        nine_taps(pad, cols, half, batch)
        back = nn(cols[...], w_ref[...]).reshape(block)
        before, after_ = shift_frames(back, frames)
        below = t_ref[0:1] * after_ + t_ref[1:2] * back + t_ref[2:3] * before
        gp_ref[...] = below
        piece = x_ref[...].astype(F32)
        if index > 1:
            piece = piece + p_ref[...].astype(F32)
        tg_ref[0] = fold(jnp.sum(after_ * piece, axis=0))
        tg_ref[1] = fold(jnp.sum(back * piece, axis=0))
        tg_ref[2] = fold(jnp.sum(before * piece, axis=0))
        if index > 1:
            raw = l_ref[...]
            sig, act = silu_parts(raw * ls_ref[0:1] + ls_ref[1:2])
            pre = (j_ref[...] + below) * m * (sig + act * (1.0 - sig))
            pre_ref[...] = pre
            sum_ref[0] = fold(jnp.sum(pre, axis=0))
            sum_ref[1] = fold(jnp.sum(pre * (raw - ls_ref[2:3]), axis=0))
        else:
            for k, source in enumerate((j_ref, gp_ref, g2_ref, g3_ref)):
                span = slice(k * group, (k + 1) * group)
                at_ref[:, span] = jnp.sum(source[...] * d_ref[:, :, span].astype(F32), axis=0)

    column = lambda k: (block, lambda i: (0, 0, k))
    ins = [grad, raw, stats, weight, taps, excited, joined, mask]
    specs = [whole(a.shape) for a in ins]
    specs[5] = column(index)
    specs[6] = column(index - 1)
    outs = [(block, BF), (block, F32), ((3, 8, group), F32)]
    if index > 1:
        more = [previous, lower[0], lower[1]]
        outs += [(block, F32), ((2, 8, group), F32)]
    else:
        more = list(previous)
        outs += [((batch, 4 * group), F32)]
    return call(
        body,
        (1,),
        ins + more,
        specs + [whole(a.shape) for a in more],
        outs,
        [whole(o[0]) for o in outs],
        scratch=[
            pltpu.VMEM((half + 2, half + 2, batch, group), BF),
            pltpu.VMEM((rows, 9 * group), BF),
        ],
        flops=2 * rows * 9 * group * group,
        moved=rows * group * 24,
    )


def kernel_motion_back(
    joined, pieces, attend, rows_d, stats_d, raw_m, kmap, change, stats_m, weight, mask, half
):
    pixels, batch, middle = rows_d.shape
    narrow = raw_m.shape[2]
    group = middle // 4

    def body(j_ref, p1, p2, p3, e_ref, d_ref, sd_ref, r_ref, k_ref, c_ref, sm_ref, w_ref, m_ref, out_ref, mg_ref, sum_ref):
        zero_first(sum_ref)
        mn = m_ref[:, :narrow]
        grad = (k_ref[...] * c_ref[0] - c_ref[1]) * mn
        value = sm_ref[0:1] * grad - mn * (sm_ref[2:3] + (r_ref[...] - sm_ref[1:2]) * sm_ref[3:4])
        mg_ref[...] = value.astype(BF)
        back = nt(mg_ref[...].reshape(half * batch, narrow), w_ref[...])
        back = back.reshape(half, batch, middle)
        m = m_ref[:, :group]
        for k, ref in enumerate((j_ref, p1, p2, p3)):
            c = slice(k * group, (k + 1) * group)
            raw = d_ref[:, :, c]
            sig, act = silu_parts(raw * sd_ref[0:1, c] + sd_ref[1:2, c])
            out = (ref[...] * e_ref[:, c] + back[:, :, c]) * m * (sig + act * (1.0 - sig))
            out_ref[:, :, c] = out
            sum_ref[0, :, c] += fold(jnp.sum(out, axis=0))
            sum_ref[1, :, c] += fold(jnp.sum(out * (raw - sd_ref[2:3, c]), axis=0))

    part = row_block(half, batch, group)
    ins = (joined,) + tuple(pieces)
    ins += (attend, rows_d, stats_d, raw_m, kmap, change, stats_m, weight, mask)
    return call(
        body,
        (half,),
        ins,
        (
            part,
            part,
            part,
            part,
            whole(attend.shape),
            row_block(half, batch, middle),
            whole(stats_d.shape),
            row_block(half, batch, narrow),
            ((half, 1, narrow), lambda i: (i, 0, 0)),
            whole(change.shape),
            whole(stats_m.shape),
            whole(weight.shape),
            whole(mask.shape),
        ),
        (
            ((pixels, batch, middle), F32),
            ((pixels, batch, narrow), BF),
            ((2, 8, middle), F32),
        ),
        (row_block(half, batch, middle), row_block(half, batch, narrow), whole((2, 8, middle))),
        flops=2 * rows_d.size * narrow,
        moved=rows_d.size * 12,
    )


class Sums:
    def __init__(self, dp, fsdp):
        self.devices = dp * fsdp
        half = self.devices // 2
        self.groups = [[2 * i + c for i in range(half)] for c in range(2)]
        self.swap = [(i, i ^ 1) for i in range(self.devices)]

    def flat(self, values):
        size = values.shape[0]
        if size <= 2048:
            copies = jnp.broadcast_to(values[None], (self.devices, size))
            return jnp.sum(lax.all_to_all(copies, AXES, 0, 0), axis=0)
        core = lax.axis_index("fsdp") % 2
        halves = values.reshape(2, size // 2)
        mine = lax.dynamic_index_in_dim(halves, core, 0, False)
        other = lax.dynamic_index_in_dim(halves, 1 - core, 0, False)
        mine = mine + lax.ppermute(other, AXES, self.swap)
        copies = jnp.broadcast_to(mine[None], (self.devices // 2, size // 2))
        mine = jnp.sum(lax.all_to_all(copies, AXES, 0, 0, axis_index_groups=self.groups), axis=0)
        other = lax.ppermute(mine, AXES, self.swap)
        low = jnp.where(core == 0, mine, other)
        high = jnp.where(core == 0, other, mine)
        return jnp.concatenate([low, high])

    def __call__(self, *arrays):
        sizes = [a.size for a in arrays]
        extra = -sum(sizes) % 256
        parts = [a.reshape(-1) for a in arrays]
        if extra:
            parts.append(jnp.zeros((extra,), F32))
        merged = self.flat(jnp.concatenate(parts))
        out, begin = [], 0
        for a, size in zip(arrays, sizes):
            out.append(merged[begin : begin + size].reshape(a.shape))
            begin += size
        return out


def pairs_of(dp, fsdp):
    return [(i, i ^ 1) for i in range(dp * fsdp)]


def same_core(fsdp):
    return [[2 * i + c for i in range(fsdp // 2)] for c in range(2)]


def quick_gather(dp, fsdp, value):
    value = lax.all_to_all(jnp.broadcast_to(value[None], (dp,) + value.shape), "dp", 0, 0)
    value = lax.all_to_all(
        jnp.broadcast_to(value[None], (fsdp // 2,) + value.shape),
        "fsdp",
        0,
        0,
        axis_index_groups=same_core(fsdp),
    )
    other = lax.ppermute(value, AXES, pairs_of(dp, fsdp))
    core = lax.axis_index("fsdp") % 2
    low = jnp.where(core == 0, value, other)
    high = jnp.where(core == 0, other, value)
    both = jnp.stack([low, high], axis=2).swapaxes(0, 1)
    return both.reshape((dp * fsdp,) + both.shape[3:])


def quick_scatter(dp, fsdp, value):
    shape = value.shape[1:]
    value = value.astype(BF).reshape((dp, fsdp // 2, 2) + shape).transpose(2, 1, 0, 3, 4)
    core = lax.axis_index("fsdp") % 2
    mine = lax.dynamic_index_in_dim(value, core, 0, False)
    other = lax.dynamic_index_in_dim(value, 1 - core, 0, False)
    other = lax.ppermute(other, AXES, pairs_of(dp, fsdp))
    value = (mine.astype(F32) + other.astype(F32)).astype(BF)
    value = lax.all_to_all(value, "fsdp", 0, 0, axis_index_groups=same_core(fsdp))
    value = jnp.sum(value.astype(F32), axis=0).astype(BF)
    return jnp.sum(lax.all_to_all(value, "dp", 0, 0).astype(F32), axis=0)


def after(value, *others):
    return lax.optimization_barrier((value, others))[0]


def affine(total, square, count, gain, bias):
    mean = total / count
    inv = lax.rsqrt(square / count - mean * mean + EPSILON)
    alpha = gain * inv
    return mean, inv, alpha, bias - mean * alpha


def local(
    dp,
    fsdp,
    clip_count,
    frame_count,
    frame_mask,
    features,
    w_reduce1,
    w_spatial1,
    w_expand1,
    w_project1,
    w_reduce2,
    w_motion_in,
    w_motion_out,
    w_spatial2,
    w_expand2,
    gains,
    biases,
    motion_taps,
    temporal_taps,
    cotangent,
):
    devices = dp * fsdp
    sums = Sums(dp, fsdp)
    slots, frames, height = features.shape[:3]
    half = height // 2
    area = half * half
    c_in = features.shape[-1]
    middle = w_reduce1.shape[1]
    group = middle // 4
    wide = w_expand1.shape[1]
    narrow = w_motion_in.shape[1]
    valid = (
        (jnp.arange(slots)[:, None] < clip_count[0])
        & (jnp.arange(frames)[None, :] < frame_count[:, None])
        & (frame_mask == 1)
    ).astype(F32)
    mask = valid[None, None, :, :, None]
    mask_rows = jnp.broadcast_to(valid.reshape(-1, 1), (slots * frames, 256))
    fmask = valid[:, :, None]
    widths = [middle, middle, wide, wide, middle, narrow, middle, group, group, group, wide]
    starts = [sum(widths[:k]) for k in range(len(widths))]
    gain = [gains[s : s + w] for s, w in zip(starts, widths)]
    bias = [biases[s : s + w] for s, w in zip(starts, widths)]

    feats = features.transpose(0, 2, 3, 1, 4).reshape(-1, c_in)
    cot = cotangent.transpose(2, 3, 0, 1, 4)

    def gather(value):
        return lax.all_gather(value, AXES, axis=0, tiled=False)

    def rows_of(value):
        return jnp.pad(value, ((0, 0), (0, -value.shape[1] % middle))).reshape(
            value.shape[0], -1, middle
        )

    def columns_of(value):
        rows = value.shape[0]
        return value.reshape(rows, -1, middle).swapaxes(0, 1).reshape(-1, middle)

    own = middle // devices
    full_reduce1 = quick_gather(dp, fsdp, w_reduce1).reshape(c_in, middle)
    rows1, rowsp, rows2 = w_expand1.shape[0], w_project1.shape[0], w_reduce2.shape[0]
    blocks = wide // middle
    aligned = own % 16 == 0

    def gather_packed(*parts):
        value = gather(jnp.concatenate([part[0] for part in parts]))
        begin, flat, places = 0, [], []
        for part, rows, count in parts:
            places.append((rows * (1 if aligned else devices), begin // rows, count))
            mine = value[:, begin : begin + part.shape[0]]
            flat.append(mine.reshape(devices, -1, rows, middle).swapaxes(0, 1).reshape(-1, middle))
            begin += part.shape[0]
        array = value if aligned else jnp.concatenate(flat)[None]
        return [Packed(array, *place) for place in places]

    project1, expand1, reduce2, spatial1 = gather_packed(
        (columns_of(w_project1), rowsp, blocks),
        (columns_of(w_expand1), rows1, blocks),
        (w_reduce2, rows2, 1),
        (w_spatial1.reshape(-1, middle), own, 1),
    )
    taps1 = [Packed(spatial1.array, spatial1.rows, spatial1.first + t, 1) for t in range(9)]
    smalls = jnp.concatenate(
        [w_spatial2.reshape(1, -1), w_motion_in.reshape(1, -1), w_motion_out.reshape(1, -1)], axis=1
    )
    rowse = w_expand2.shape[0]
    late_rows = columns_of(w_expand2).shape[0]
    smalls = rows_of(smalls)[0]
    expand2, tail = gather_packed(
        (columns_of(w_expand2), rowse, blocks), (smalls, 1, smalls.shape[0])
    )
    if aligned:
        flat_small = tail.array[:, late_rows:].reshape(devices, -1)
    else:
        flat_small = (
            tail.array[0, late_rows * devices :]
            .reshape(-1, devices, middle)
            .swapaxes(0, 1)
            .reshape(devices, -1)
        )
    batch = slots * frames
    pixel_rows = (area, batch)
    size_s, size_m = w_spatial2.size, w_motion_in.size
    kernels = (
        flat_small[:, :size_s].reshape(devices, 27, -1).swapaxes(0, 1).reshape(3, 9, group, group)
    )
    small = flat_small[:, size_s : size_s + 2 * size_m].reshape(devices, 2, own, narrow)
    full_motion_in = small[:, 0].reshape(middle, narrow)
    full_motion_out = small[:, 1].reshape(middle, narrow).astype(F32)

    raw_a, sums_a = kernel_reduce1(feats, full_reduce1, mask_rows, slots, height, frames)
    sum_a, square_a, frame_total, pairs = sums(
        jnp.sum(sums_a[0], axis=0),
        jnp.sum(sums_a[1], axis=0),
        jnp.sum(valid),
        jnp.sum(valid[:, :-1] * valid[:, 1:]),
    )
    count_big = frame_total * (height * height)
    count = frame_total * area
    mean_a, inv_a, alpha_a, beta_a = affine(sum_a, square_a, count_big, gain[0], bias[0])
    act_a, raw_b, sums_b = kernel_conv_down(raw_a, alpha_a[None], beta_a[None], mask_rows, taps1)
    raw_b = raw_b.reshape(area, batch, middle)
    sampled = (
        features.reshape(slots, frames, half, 2, half, 2, c_in)[:, :, :, 0, :, 0]
        .transpose(2, 3, 0, 1, 4)
        .reshape(area, batch, c_in)
    )
    raw_p, sums_p = kernel_project(sampled, mask_rows, project1, half)

    def moments(raw):
        return total_over(raw * mask), total_over(raw * raw * mask)

    sum_b, square_b = sums(jnp.sum(sums_b[0], axis=0), jnp.sum(sums_b[1], axis=0))
    mean_b, inv_b, alpha_b, beta_b = affine(sum_b, square_b, count, gain[1], bias[1])
    act_b, raw_c, sums_c = kernel_expand(
        raw_b, jnp.stack([alpha_b, beta_b]), mask_rows, expand1, half
    )
    sums_c, sums_p = jnp.sum(sums_c, axis=1), jnp.sum(sums_p, axis=1)
    sum_c, square_c, sum_p, square_p = sums(sums_c[0], sums_c[1], sums_p[0], sums_p[1])
    mean_c, inv_c, alpha_c, beta_c = affine(sum_c, square_c, count, gain[2], bias[2])
    mean_p, inv_p, alpha_p, beta_p = affine(sum_p, square_p, count, gain[3], bias[3])
    stats_one = jnp.stack(
        [alpha_c, alpha_p, beta_c + beta_p, mean_c, inv_c, mean_p, inv_p, jnp.zeros_like(mean_p)]
    )
    block_one, rows_d, sums_d = kernel_block_one(
        raw_c, raw_p, stats_one, mask_rows, reduce2, half
    )

    sum_d, square_d = sums(jnp.sum(sums_d[0], axis=0), jnp.sum(sums_d[1], axis=0))
    mean_d, inv_d, alpha_d, beta_d = affine(sum_d, square_d, count, gain[4], bias[4])
    inside = [
        [
            [int(0 <= y - r + 1 < half and 0 <= x - c + 1 < half) for r in range(3) for c in range(3)]
            for x in range(half)
        ]
        for y in range(half)
    ]
    windows = jnp.array(inside, F32)
    act_d, raw_m, in_window, square_rows = kernel_motion(
        rows_d, jnp.stack([alpha_d, beta_d]), mask_rows, full_motion_in, inside, half
    )
    in_window = in_window.reshape(9, slots, frames, narrow)
    kmap = jnp.sum(windows[..., None] * motion_taps, axis=2)
    ksum = jnp.sum(kmap, axis=(0, 1))
    mapped = jnp.sum(in_window * motion_taps[:, None, None, :], axis=0)
    plain = in_window[4]
    vnext = later(fmask)
    pool_raw = (vnext / area) * (later(mapped * fmask) - fmask * plain)
    pool_one = (vnext / area) * (later(fmask) * ksum - fmask * area)
    flat_raw = pool_raw.reshape(-1, narrow)
    flat_valid = valid.reshape(-1, 1)
    gram = lax.dot_general(
        flat_raw * flat_valid, flat_raw, (((0,), (0,)), ((), ())), precision=HIGHEST
    )
    sum_m, square_m, pool_a, gram_aa = sums(
        total_over(plain * fmask),
        total_over(square_rows.reshape(plain.shape) * fmask),
        jnp.sum(flat_raw * flat_valid, axis=0), gram
    )
    mean_m, inv_m, alpha_m, beta_m = affine(sum_m, square_m, count, gain[5], bias[5])
    step = ksum / area - 1.0
    pool_b = pairs * step
    gram_ab = pool_a[:, None] * step[None, :]
    gram_bb = pairs * step[:, None] * step[None, :]
    pooled = alpha_m * pool_raw + beta_m * pool_one
    lifted = jnp.einsum("cfr,or->cfo", pooled, full_motion_out, precision=HIGHEST)
    gram_p = (
        alpha_m[:, None] * alpha_m * gram_aa
        + alpha_m[:, None] * beta_m * gram_ab
        + beta_m[:, None] * alpha_m * gram_ab.T
        + beta_m[:, None] * beta_m * gram_bb
    )
    sum_x = jnp.dot(full_motion_out, alpha_m * pool_a + beta_m * pool_b, precision=HIGHEST)
    square_x = jnp.sum(jnp.dot(full_motion_out, gram_p, precision=HIGHEST) * full_motion_out, axis=1)
    mean_x, inv_x, alpha_x, beta_x = affine(sum_x, square_x, frame_total, gain[6], bias[6])
    sigma = jax.nn.sigmoid(lifted * alpha_x + beta_x)
    attend1 = 2.0 * sigma
    attend_rows = attend1.reshape(batch, middle)
    tap_rows = [temporal_taps[k] for k in range(3)]
    excited, pad, raw, partial = kernel_group(
        act_d, attend_rows, tap_rows[0], kernels[0].reshape(-1, group), mask_rows, 1, half, frames
    )
    pads, raws, stats, outputs = [pad], [raw], [], []
    for k in range(3):
        total = jnp.sum(partial, axis=1)
        stats.append(affine(*sums(total[0], total[1]), count, gain[7 + k], bias[7 + k]))
        if k < 2:
            out, pad, raw, partial = kernel_group(
                excited,
                (raws[k], jnp.stack(stats[k][2:])),
                tap_rows[k + 1],
                kernels[k + 1].reshape(-1, group),
                mask_rows,
                k + 2,
                half,
                frames,
            )
            pads.append(pad)
            raws.append(raw)
            outputs.append(out)
    joined, raw_e, sums_e = kernel_join(
        excited, outputs, raws[2], jnp.stack(stats[2][2:]), mask_rows, expand2, half
    )
    sums_e = jnp.sum(sums_e, axis=1)
    mean_e, inv_e, alpha_e, beta_e = affine(
        *sums(sums_e[0], sums_e[1]), count, gain[10], bias[10]
    )
    def by_owner(values, number):
        return (
            values.astype(BF)
            .reshape(dp, fsdp, -1, number, middle)
            .transpose(1, 0, 3, 2, 4)
            .reshape(fsdp, dp, -1, middle)
        )

    shifts = [None] * 11
    spreads = [None] * 11

    def grad_raw(index, grad, raw, mean, inv, weight, number):
        unit = (raw - mean) * inv
        return gain[index] * inv * (grad - weight * (shifts[index] + unit * spreads[index]) / number)

    result, grad_total, sums_e = kernel_result(
        raw_e,
        block_one,
        cot.reshape(area, batch, wide),
        jnp.stack([alpha_e, beta_e, mean_e, inv_e]),
        mask_rows,
        half,
    )
    result = result.reshape(half, half, slots, frames, wide)
    shifts[10], spreads[10] = sums(jnp.sum(sums_e[0], axis=0), jnp.sum(sums_e[1], axis=0))

    def back_stats(index, mean, inv):
        scale = gain[index] * inv
        return [scale, mean, inv, shifts[index] / count, spreads[index] / count]

    def lower(k):
        return raws[k], jnp.stack([stats[k][2], stats[k][3], stats[k][0]])

    flipped = [kernels[k][::-1].transpose(0, 2, 1).reshape(9 * group, group) for k in range(3)]
    final_grad, grad_joined, grad_pre, partial = kernel_final_back(
        grad_total,
        raw_e,
        jnp.stack(back_stats(10, mean_e, inv_e)),
        mask_rows,
        expand2,
        *lower(2),
        half,
    )
    kernel_grads = [None] * 3
    temporal_grads = [None] * 3
    grad_pieces = [None] * 3
    for k in (2, 1, 0):
        mean, inv, alpha, _ = stats[k]
        partial = jnp.sum(partial, axis=1)
        shifts[7 + k], spreads[7 + k] = sums(partial[0], partial[1] * inv)
        got = kernel_group_back(
            grad_pre,
            raws[k],
            jnp.stack(
                [alpha, mean, alpha * shifts[7 + k] / count, alpha * inv * spreads[7 + k] / count]
            ),
            flipped[k],
            tap_rows[k],
            excited,
            outputs[k - 1] if k else (grad_pieces[1], grad_pieces[2], act_d),
            grad_joined,
            lower(k - 1) if k else None,
            mask_rows,
            k + 1,
            half,
            frames,
        )
        group_grad, grad_pieces[k], sums_t = got[:3]
        if k:
            grad_pre, partial = got[3:]
        else:
            grad_attend = got[3].reshape(slots, frames, middle)
        temporal_grads[k] = jnp.sum(sums_t, axis=1)
        kernel_grads[k] = kernel_group_weights(pads[k], group_grad, half)
    grad_kernels = rows_of(
        jnp.stack(kernel_grads).reshape(27, devices, -1).swapaxes(0, 1).astype(BF).reshape(devices, -1)
    )
    total_a = blocks * rowse + grad_kernels.shape[1]
    total_a += -total_a % 16
    if aligned:
        packed_a = kernel_weight_grad(joined, final_grad, dp, fsdp, rowse, 0, total_a)
        packed_a = lax.dynamic_update_slice(
            packed_a,
            grad_kernels.reshape(dp, fsdp, -1, middle).swapaxes(0, 1),
            (0, 0, blocks * rowse, 0),
        )
    else:
        packed_a = jnp.concatenate(
            [
                by_owner(weight_grad(joined, final_grad), blocks),
                grad_kernels.reshape(dp, fsdp, -1, middle).swapaxes(0, 1),
            ],
            axis=2,
        )
        packed_a = jnp.pad(
            packed_a, ((0, 0), (0, 0), (0, total_a - packed_a.shape[2]), (0, 0))
        )
    grad_attend, packed_a = lax.optimization_barrier((grad_attend, packed_a))
    mine_a = lax.psum_scatter(
        packed_a.reshape(-1, middle), "fsdp", scatter_dimension=0, tiled=True
    )
    grad_x = grad_attend * 2.0 * sigma * (1.0 - sigma)
    unit_x = (lifted - mean_x) * inv_x
    pool_unit = (pool_raw - mean_m * pool_one) * inv_m
    grad_e = jnp.einsum("cfo,or->cfr", grad_x, full_motion_out * alpha_x[:, None], precision=HIGHEST)
    shifts[6], spreads[6], first_t, second_t = sums(
        jnp.sum(grad_x, axis=(0, 1)),
        jnp.sum(grad_x * unit_x, axis=(0, 1)),
        jnp.sum(grad_e * pool_one, axis=(0, 1)),
        jnp.sum(grad_e * pool_unit, axis=(0, 1)),
    )
    lift_b = jnp.dot(
        full_motion_out, alpha_m[:, None] * gram_ab + beta_m[:, None] * gram_bb, precision=HIGHEST
    )
    lift_a = jnp.dot(
        full_motion_out, alpha_m[:, None] * gram_aa + beta_m[:, None] * gram_ab.T, precision=HIGHEST
    )
    unit_b = inv_x[:, None] * (lift_b - mean_x[:, None] * pool_b)
    unit_a = inv_x[:, None] * (lift_a - mean_x[:, None] * pool_a)
    unit_u = (unit_a - unit_b * mean_m) * inv_m
    pool_u = (pool_a - pool_b * mean_m) * inv_m
    back_x = full_motion_out * alpha_x[:, None]
    shifts[5] = first_t - jnp.sum(
        back_x * (shifts[6][:, None] * pool_b + spreads[6][:, None] * unit_b), axis=0
    ) / frame_total
    spreads[5] = second_t - jnp.sum(
        back_x * (shifts[6][:, None] * pool_u + spreads[6][:, None] * unit_u), axis=0
    ) / frame_total
    grad_lifted = alpha_x * (grad_x - fmask * (shifts[6] + unit_x * spreads[6]) / frame_total)
    grad_motion_out = jnp.einsum("cfo,cfr->or", grad_lifted, pooled, precision=HIGHEST)
    grad_pooled = jnp.einsum("cfo,or->cfr", grad_lifted, full_motion_out, precision=HIGHEST)
    grad_change = grad_pooled * vnext / area
    reduced_windows = later(
        fmask * (alpha_m * in_window + beta_m * jnp.sum(windows, axis=(0, 1))[:, None, None, None])
    )
    motion_tap_grad = jnp.sum(grad_change * reduced_windows, axis=(1, 2))
    grad_narrow, motion_grad, sums_narrow = kernel_motion_back(
        grad_joined,
        grad_pieces,
        attend_rows,
        rows_d,
        jnp.stack([alpha_d, beta_d, mean_d]),
        raw_m,
        kmap.reshape(area, 1, narrow),
        jnp.stack([earlier(grad_change), grad_change]).reshape(2, batch, narrow),
        jnp.stack(
            [alpha_m, mean_m, alpha_m * shifts[5] / count, alpha_m * inv_m * spreads[5] / count]
        ),
        full_motion_in,
        mask_rows,
        half,
    )
    grad_motion_in = weight_grad(act_d, motion_grad)
    sums_narrow = jnp.sum(sums_narrow, axis=1)
    shifts[4], spreads[4] = sums(sums_narrow[0], sums_narrow[1] * inv_d)
    small_grads = jnp.concatenate(
        [grad_motion_in.reshape(devices, -1), grad_motion_out.reshape(devices, -1)], axis=1
    )
    narrow_grad, grad_one, sums_one = kernel_block_back(
        grad_narrow,
        rows_d,
        jnp.stack(back_stats(4, mean_d, inv_d)),
        reduce2,
        grad_total,
        raw_c,
        raw_p,
        stats_one,
        mask_rows,
        half,
    )
    sums_one, mine_a = lax.optimization_barrier((sums_one, mine_a))
    mine_a = lax.psum_scatter(mine_a, "dp", scatter_dimension=0, tiled=True)
    sums_one = jnp.sum(sums_one, axis=1)
    shifts[2], spreads[2], spreads[3] = sums(sums_one[0], sums_one[1], sums_one[2])
    shifts[3] = shifts[2]
    widen_grad, shortcut_grad, grad_strided, sums_strided = kernel_expand_back(
        grad_one,
        raw_c,
        raw_p,
        jnp.stack(back_stats(2, mean_c, inv_c) + back_stats(3, mean_p, inv_p)),
        expand1,
        raw_b,
        jnp.stack([alpha_b, beta_b, mean_b, inv_b]),
        mask_rows,
        half,
    )
    if aligned:
        total = blocks * (rowsp + rows1) + rows2
        packed_b = kernel_weight_grad(
            block_one, narrow_grad, dp, fsdp, rows2, total // rows2 - 1, total
        )
        packed_b = kernel_weight_grad(
            act_b, widen_grad, dp, fsdp, rows1, blocks * rowsp // rows1, total, packed_b
        )
        packed_b = kernel_weight_grad(
            sampled, shortcut_grad, dp, fsdp, rowsp, 0, total, packed_b
        )
    else:
        packed_b = jnp.concatenate(
            [
                by_owner(weight_grad(sampled, shortcut_grad), blocks),
                by_owner(weight_grad(act_b, widen_grad), blocks),
                by_owner(weight_grad(block_one, narrow_grad), 1),
            ],
            axis=2,
        )
    sums_strided, packed_b, mine_a = lax.optimization_barrier((sums_strided, packed_b, mine_a))

    def columns_back(value, rows):
        return value.reshape(blocks, rows, middle).swapaxes(0, 1).reshape(rows, wide)

    mine_a = mine_a.astype(F32)
    own_expand2 = columns_back(mine_a[: blocks * rowse], rowse)
    own_kernels = mine_a[blocks * rowse :].reshape(-1)[:size_s]
    mine_b = packed_b.reshape(-1, middle)
    mine_b = lax.psum_scatter(mine_b, "fsdp", scatter_dimension=0, tiled=True)
    mine_b = lax.psum_scatter(mine_b, "dp", scatter_dimension=0, tiled=True).astype(F32)
    cut1 = blocks * rowsp
    cut2 = cut1 + blocks * rows1
    own_project1 = columns_back(mine_b[:cut1], rowsp)
    own_expand1 = columns_back(mine_b[cut1:cut2], rows1)
    own_reduce2 = mine_b[cut2:]
    grad_sampled = kernel_sampled_back(shortcut_grad, project1, half)
    shifts[1], spreads[1] = sums(jnp.sum(sums_strided[0], axis=0), jnp.sum(sums_strided[1], axis=0))
    strided_grad = grad_raw(
        1, grad_strided, raw_b, mean_b, inv_b, mask_rows[:, :1], count
    ).astype(BF)
    strided_grad = strided_grad.reshape(half, half, batch, middle)
    grad_spatial1 = kernel_conv_down_weights(act_a, strided_grad)
    strided_grad, grad_spatial1 = lax.optimization_barrier((strided_grad, grad_spatial1))
    own_spatial1 = quick_scatter(
        dp,
        fsdp,
        jnp.concatenate(
            [
                grad_spatial1.reshape(9, devices, own, middle)
                .swapaxes(0, 1)
                .reshape(devices, 9 * own, middle),
                rows_of(small_grads.astype(BF)),
            ],
            axis=1,
        ),
    )
    own_motion = own_spatial1[9 * own :].reshape(-1)[: 2 * size_m].reshape(2, own, narrow)
    own_spatial1 = own_spatial1[: 9 * own]
    grad_first, sums_first = kernel_conv_down_back(
        strided_grad,
        taps1,
        raw_a,
        jnp.stack([alpha_a, beta_a, mean_a, inv_a]),
        mask_rows,
    )
    shifts[0], spreads[0], motion_total, temporal_total = sums(
        jnp.sum(sums_first[0], axis=0),
        jnp.sum(sums_first[1], axis=0),
        motion_tap_grad,
        jnp.stack(temporal_grads),
    )
    first_grad, grad_reduce1 = kernel_first_grad(
        grad_first,
        raw_a,
        feats,
        jnp.stack([alpha_a, mean_a, inv_a, shifts[0] / count_big, spreads[0] / count_big]),
        mask_rows,
        slots,
        frames,
    )
    own_reduce1 = quick_scatter(dp, fsdp, grad_reduce1.reshape(devices, -1, middle))
    grad_features = kernel_grad_features(
        first_grad,
        full_reduce1,
        grad_sampled.reshape(half, half, slots * frames, c_in),
        height,
        slots,
        frames,
    )
    grad_features = grad_features.reshape(slots, height, height, frames, c_in)
    return (
        result.transpose(2, 3, 0, 1, 4),
        grad_features.transpose(0, 3, 1, 2, 4),
        own_reduce1,
        own_spatial1.reshape(9, own * middle),
        own_expand1,
        own_project1,
        own_reduce2,
        own_motion[0],
        own_motion[1],
        own_kernels.reshape(27, -1),
        own_expand2,
        jnp.concatenate(spreads),
        jnp.concatenate(shifts),
        motion_total,
        temporal_total,
    )


def solution(mesh):
    dp, fsdp = mesh.shape["dp"], mesh.shape["fsdp"]

    def run(*arrays):
        return local(dp, fsdp, *arrays)

    rows = P(AXES, None)
    columns = P(None, AXES)
    clips = P(AXES, None, None, None, None)
    return jax.shard_map(
        run,
        mesh=mesh,
        in_specs=(
            P(AXES),
            P(AXES),
            rows,
            clips,
            rows,
            columns,
            rows,
            rows,
            rows,
            rows,
            rows,
            columns,
            rows,
            P(),
            P(),
            P(),
            P(),
            clips,
        ),
        out_specs=(
            clips,
            clips,
            rows,
            columns,
            rows,
            rows,
            rows,
            rows,
            rows,
            columns,
            rows,
            P(),
            P(),
            P(),
            P(),
        ),
        check_vma=False,
    )
```

```python
import jax
import jax.numpy as jnp
from jax import lax
from jax.experimental import pallas as pl
from jax.experimental.pallas import tpu as pltpu
from jax.sharding import PartitionSpec as P

EPSILON = 1e-05
HIGHEST = lax.Precision.HIGHEST
AXES = ("dp", "fsdp")
BF = jnp.bfloat16
F32 = jnp.float32


def by_clip(values, frames):
    return values.reshape(values.shape[:-2] + (-1, frames, values.shape[-1]))


def earlier(values):
    return jnp.concatenate([jnp.zeros_like(values[..., :1, :]), values[..., :-1, :]], axis=-2)


def later(values):
    return jnp.concatenate([values[..., 1:, :], jnp.zeros_like(values[..., :1, :])], axis=-2)


def taps_of(values, size):
    padded = jnp.pad(values, ((1, 1), (1, 1), (0, 0), (0, 0), (0, 0)))
    return [padded[r : r + size, c : c + size] for r in range(3) for c in range(3)]


def dot(left, weight):
    shape = left.shape
    flat = jnp.dot(left.reshape(-1, shape[-1]), weight, preferred_element_type=F32)
    return flat.reshape(shape[:-1] + (weight.shape[1],))


def dot_t(grad, weight):
    shape = grad.shape
    flat = lax.dot_general(
        grad.reshape(-1, shape[-1]), weight, (((1,), (1,)), ((), ())), preferred_element_type=F32
    )
    return flat.reshape(shape[:-1] + (weight.shape[0],))


def weight_grad(left, grad):
    return lax.dot_general(
        left.reshape(-1, left.shape[-1]),
        grad.reshape(-1, grad.shape[-1]),
        (((0,), (0,)), ((), ())),
        preferred_element_type=F32,
    )


def silu_slope(values):
    sig = jax.nn.sigmoid(values)
    return sig * (1.0 + values * (1.0 - sig))


def total_over(values):
    return jnp.sum(values, axis=tuple(range(values.ndim - 1)))


def silu_parts(norm):
    sig = 0.5 * jnp.tanh(0.5 * norm) + 0.5
    return sig, norm * sig


def call(body, grid, ins, in_blocks, outs, out_blocks, scratch=(), limit=56, flops=0, moved=0):
    def spec(block):
        if block is None:
            return pl.BlockSpec(memory_space=pltpu.VMEM)
        return pl.BlockSpec(block[0], block[1])

    return pl.pallas_call(
        body,
        grid=grid,
        in_specs=[spec(b) for b in in_blocks],
        out_specs=[spec(b) for b in out_blocks],
        out_shape=[jax.ShapeDtypeStruct(s, d) for s, d in outs],
        scratch_shapes=list(scratch),
        compiler_params=pltpu.CompilerParams(
            vmem_limit_bytes=limit * 1024 * 1024,
            dimension_semantics=("arbitrary",) * len(grid),
        ),
        cost_estimate=pl.CostEstimate(flops=flops, bytes_accessed=moved, transcendentals=0),
    )(*ins)


def whole(shape):
    return shape, lambda *_: (0,) * len(shape)


def mean_of(raw, weight):
    return jnp.sum(raw * weight, axis=0, keepdims=True) / jnp.maximum(jnp.sum(weight), 1.0)


def kernel_reduce1(feats, weight, mask, height, frames):
    c_in, middle = weight.shape
    slots = feats.shape[0]
    half = height // 2
    rows = 2 * height * frames

    def body(x_ref, w_ref, m_ref, raw_ref, off_ref, sum_ref):
        first = (pl.program_id(0) == 0) & (pl.program_id(1) == 0)

        @pl.when(first)
        def _():
            sum_ref[...] = jnp.zeros_like(sum_ref)
            few = nn(x_ref[0, : height * frames], w_ref[...]).reshape(height, frames, middle)
            off_ref[0:1] = mean_of(jnp.sum(few, axis=0) * (1.0 / height), m_ref[:frames, :1])

        left = x_ref[...].reshape(2 * rows, c_in)
        m = m_ref[:, :1].reshape(2, 1, 1, frames, 1)
        for c in chunks(middle):
            raw = nn(left, w_ref[:, c]).reshape(2, 2, height, frames, -1)
            offset = off_ref[0:1, c]
            sum_ref[0, :, c] += jnp.sum(jnp.sum(raw, axis=(1, 2)) * m[:, 0, 0], axis=0)
            sum_ref[1, :, c] += jnp.sum(jnp.sum(raw * raw, axis=(1, 2)) * m[:, 0, 0], axis=0)
            low = raw - offset
            raw_ref[:, :, :, c] = jnp.concatenate([low[0], low[1]], axis=2).astype(BF)

    return call(
        body,
        (slots // 2, half),
        (feats, weight, mask),
        (
            ((2, rows, c_in), lambda c, h: (c, h, 0)),
            whole(weight.shape),
            ((2 * frames, mask.shape[1]), lambda c, h: (c, 0)),
        ),
        (
            ((height, height, slots * frames, middle), BF),
            ((8, middle), F32),
            ((2, frames, middle), F32),
        ),
        (
            ((2, height, 2 * frames, middle), lambda c, h: (h, 0, c, 0)),
            whole((8, middle)),
            whole((2, frames, middle)),
        ),
        flops=2 * feats.size * middle,
        moved=feats.size * 2 + feats.size // c_in * middle * 2,
    )


def exchange_shape(width):
    return (lax.psum(1, AXES), 1, width)


def send_sums(send_ref, sum_ref, last=True):
    def send():
        rows = [jnp.sum(sum_ref[n], axis=0, keepdims=True) for n in range(sum_ref.shape[0])]
        row = jnp.concatenate(rows, axis=1)
        send_ref[...] = jnp.broadcast_to(row[None], send_ref.shape)

    if last is True:
        send()
    else:
        pl.when(last)(send)


def kernel_act(raw_a, stats, mask):
    height, _, batch, middle = raw_a.shape
    block = (2, height, batch, middle), lambda i: (i, 0, 0, 0)

    def body(a_ref, s_ref, m_ref, act_ref):
        m = m_ref[...]
        for c in chunks(middle):
            al, be = s_ref[0:1, c], s_ref[1:2, c]
            for p in range(2):
                for j in range(height):
                    act_ref[p, j, :, c] = (silu_parts(a_ref[p, j, :, c].astype(F32) * al + be)[1] * m).astype(BF)

    return call(
        body,
        (height // 2,),
        (raw_a, stats, mask),
        (block, whole(stats.shape), whole(mask.shape)),
        ((raw_a.shape, BF),),
        (block,),
        flops=10 * raw_a.size,
        moved=raw_a.size * 6,
    )[0]


def kernel_conv_down(act_a, mask, taps):
    height, _, batch, middle = act_a.shape
    half = height // 2
    rows = half * batch

    def body(a_ref, m_ref, *refs):
        w_refs, (raw_ref, send_ref, cols, w_ref, sum_ref) = refs[:9], refs[9:]
        step = pl.program_id(0)
        wide = 3 * middle

        @pl.when(step == 0)
        def _():
            sum_ref[...] = jnp.zeros_like(sum_ref)
            cols[...] = jnp.zeros_like(cols)
            for t in range(9):
                w_ref[t * middle : (t + 1) * middle] = taps[t].of(w_refs[t], 0)

        @pl.when(step > 0)
        def _():
            cols[:, :wide] = cols[:, 2 * wide :]

        m = m_ref[:, :1]
        for p in range(2):
            base = (1 + p) * wide
            for j in range(half):
                for q in range(2):
                    act = a_ref[p, 2 * j + q]
                    lane = base + (1 + q) * middle
                    cols[j * batch : (j + 1) * batch, lane : lane + middle] = act
                    if q == 1 and j + 1 < half:
                        cols[(j + 1) * batch : (j + 2) * batch, base : base + middle] = act
        raw = jnp.dot(cols[...], w_ref[...], preferred_element_type=F32)
        raw = raw.reshape(half, batch, middle)
        raw_ref[0] = raw
        sum_ref[0] += jnp.sum(raw, axis=0) * m
        sum_ref[1] += jnp.sum(raw * raw, axis=0) * m
        send_sums(send_ref, sum_ref, step == half - 1)

    return call(
        body,
        (half,),
        (act_a, mask) + tuple(t.array for t in taps),
        (((2, height, batch, middle), lambda i: (i, 0, 0, 0)), whole(mask.shape))
        + tuple(t.block() for t in taps),
        (
            ((half, half, batch, middle), F32),
            (exchange_shape(2 * middle), F32),
        ),
        (
            ((1, half, batch, middle), lambda i: (i, 0, 0, 0)),
            whole(exchange_shape(2 * middle)),
        ),
        scratch=[pltpu.VMEM((rows, 9 * middle), BF), pltpu.VMEM((9 * middle, middle), BF), pltpu.VMEM((2, batch, middle), F32)],
        flops=2 * half * rows * 9 * middle * middle,
        moved=act_a.size * 2 + 18 * middle * middle,
    )


def kernel_conv_down_weights(act_a, grad, dp, fsdp):
    height, _, batch, middle = act_a.shape
    half = height // 2
    split = act_a.reshape(half, 2, half, 2, batch, middle)
    own = middle // (dp * fsdp)
    aligned = own % 16 == 0

    def body(a_ref, g_ref, out_ref, cols):
        step = pl.program_id(0)
        for r in range(3):
            for c in range(3):
                top, left = int(r == 0), int(c == 0)

                @pl.when(step == r * 3 + c)
                def _(r=r, c=c, top=top, left=left):
                    if top:
                        cols[0] = jnp.zeros_like(cols[0])
                    if left:
                        cols[:, 0] = jnp.zeros_like(cols[:, 0])
                    cols[top:, left:] = a_ref[
                        : half - top, int(r != 1), : half - left, int(c != 1)
                    ]

        value = tn(cols[...].reshape(half * half * batch, middle), g_ref[...]).astype(BF)
        if not aligned:
            out_ref[0] = value
            return
        value = value.reshape(dp, fsdp // 2, 2, own, middle)
        for place, d in enumerate(by_low_bit(dp)):
            for f in range(fsdp // 2):
                for core in range(2):
                    out_ref[core, place, f] = value[d, f, core]

    if aligned:
        out = ((2, dp, fsdp // 2, 9 * own, middle), BF)
        out_block = (2, dp, fsdp // 2, own, middle), lambda t: (0, 0, 0, t, 0)
    else:
        out = ((9, middle, middle), BF)
        out_block = (1, middle, middle), lambda t: (t, 0, 0)
    value = call(
        body,
        (9,),
        (split, grad.reshape(-1, middle)),
        (whole(split.shape), whole((half * half * batch, middle))),
        (out,),
        (out_block,),
        scratch=[pltpu.VMEM((half, half, batch, middle), BF)],
        flops=2 * half * half * batch * 9 * middle * middle,
        moved=act_a.size * 2 + grad.size * 2 + 18 * middle * middle,
    )[0]
    if not aligned:
        value = value.reshape(9, dp, fsdp // 2, 2, own, middle).transpose(3, 1, 2, 0, 4, 5)
        value = value.reshape(2, dp, fsdp // 2, 9 * own, middle)[:, jnp.array(by_low_bit(dp))]
    return value


def kernel_conv_down_back(grad, taps, raw_a, stats, mask):
    height, _, batch, middle = raw_a.shape
    half = height // 2
    rows = half * batch

    def body(g_ref, n_ref, a_ref, s_ref, m_ref, *refs):
        w_refs, (out_ref, send_ref, here, below, sum_ref) = refs[:9], refs[9:]
        step = pl.program_id(0)

        @pl.when(step == 0)
        def _():
            sum_ref[...] = jnp.zeros_like(sum_ref)
            here[half] = jnp.zeros_like(here[half])
            below[half] = jnp.zeros_like(below[half])

        here[:half] = g_ref[0]

        @pl.when(step < half - 1)
        def _():
            below[:half] = n_ref[0]

        @pl.when(step == half - 1)
        def _():
            below[:half] = jnp.zeros_like(n_ref[0])

        def tap(ref, right, t):
            return lax.dot_general(
                ref[right : right + half].reshape(rows, middle),
                taps[t].of(w_refs[t], 0),
                (((1,), (1,)), ((), ())),
                preferred_element_type=F32,
            )

        al, be = s_ref[0:1], s_ref[1:2]
        mean, inv = s_ref[2:3], s_ref[3:4]
        m = m_ref[:, :1]
        plans = (
            (0, 0, ((here, 0, 4),)),
            (0, 1, ((here, 0, 5), (here, 1, 3))),
            (1, 0, ((here, 0, 7), (below, 0, 1))),
            (1, 1, ((here, 0, 8), (here, 1, 6), (below, 0, 2), (below, 1, 0))),
        )
        for p, q, parts in plans:
            back = tap(*parts[0])
            for part in parts[1:]:
                back = back + tap(*part)
            raw = a_ref[0, p, :, q].astype(F32)
            norm = raw * al + be
            sig, act = silu_parts(norm)
            slope = sig + act * (1.0 - sig)
            out = back.reshape(half, batch, middle) * slope * m
            out_ref[0, p, :, q] = out.astype(BF)
            sum_ref[0] += jnp.sum(out, axis=0)
            sum_ref[1] += jnp.sum(out * ((raw - mean) * inv), axis=0)
        send_sums(send_ref, sum_ref, step == half - 1)

    return call(
        body,
        (half,),
        (grad, grad, raw_a.reshape(half, 2, half, 2, batch, middle), stats, mask)
        + tuple(t.array for t in taps),
        (
            ((1, half, batch, middle), lambda i: (i, 0, 0, 0)),
            ((1, half, batch, middle), lambda i: (jnp.minimum(i + 1, half - 1), 0, 0, 0)),
            ((1, 2, half, 2, batch, middle), lambda i: (i, 0, 0, 0, 0, 0)),
            whole(stats.shape),
            whole(mask.shape),
        )
        + tuple(t.block() for t in taps),
        (
            ((half, 2, half, 2, batch, middle), BF),
            (exchange_shape(2 * middle), F32),
        ),
        (
            ((1, 2, half, 2, batch, middle), lambda i: (i, 0, 0, 0, 0, 0)),
            whole(exchange_shape(2 * middle)),
        ),
        scratch=[
            pltpu.VMEM((half + 1, batch, middle), BF),
            pltpu.VMEM((half + 1, batch, middle), BF),
            pltpu.VMEM((2, batch, middle), F32),
        ],
        flops=2 * half * rows * 9 * middle * middle,
        moved=raw_a.size * 8 + 18 * middle * middle,
    )


def kernel_first_grad(grad, raw_a, feats, stats, mask, frames):
    height, _, batch, middle = raw_a.shape
    half = height // 2
    rows = half * height * frames
    line = height * frames
    slots, _, c_in = feats.shape

    def body(g_ref, a_ref, x_ref, s_ref, m_ref, out_ref, w_ref, acc):
        first = (pl.program_id(0) == 0) & (pl.program_id(1) == 0)
        last = (pl.program_id(0) == slots // 2 - 1) & (pl.program_id(1) == 1)

        @pl.when(first)
        def _():
            acc[...] = jnp.zeros_like(acc)

        m = m_ref[...]
        for c in chunks(middle):
            scale, mean, shift, spread = (s_ref[n : n + 1, c] for n in range(4))
            for r in range(half):
                raw = a_ref[r, :, :, c].astype(F32)
                value = scale * g_ref[r, :, :, c].astype(F32) - m * (shift + (raw - mean) * spread)
                for clip in range(2):
                    part = value[:, clip * frames : (clip + 1) * frames]
                    out_ref[clip, r * line : (r + 1) * line, c] = part.reshape(line, -1).astype(BF)
        for clip in range(2):
            acc[...] += tn(x_ref[clip], out_ref[clip])

        @pl.when(last)
        def _():
            w_ref[...] = acc[...].astype(BF)

    block = (half, height, 2 * frames, middle), lambda c, h: (h, 0, c, 0)
    return call(
        body,
        (slots // 2, 2),
        (grad.reshape(raw_a.shape), raw_a, feats, stats, mask),
        (
            block,
            block,
            ((2, rows, c_in), lambda c, h: (c, h, 0)),
            whole(stats.shape),
            ((2 * frames, mask.shape[1]), lambda c, h: (c, 0)),
        ),
        (
            ((slots, 2 * rows, middle), BF),
            ((c_in, middle), BF),
        ),
        (
            ((2, rows, middle), lambda c, h: (c, h, 0)),
            whole((c_in, middle)),
        ),
        scratch=[pltpu.VMEM((c_in, middle), F32)],
        flops=2 * raw_a.size * c_in,
        moved=raw_a.size * 6 + feats.size * 2,
    )


def kernel_grad_features(grad, weight, shortcut, project, height, frames, pair, into=None):
    c_in, middle = weight.shape
    slots, all_rows, _ = grad.shape
    half = height // 2
    pixels, batch, wide = shortcut.shape
    size = 256
    parts = c_in // size

    def body(g_ref, w_ref, s_ref, p_ref, *refs):
        out_ref = refs[-1]
        even = None
        for k in range(project.count):
            left = s_ref[:, :, k * middle : (k + 1) * middle].reshape(pixels * 2 * frames, middle)
            part = nt(left, project.of(p_ref, k))
            even = part if even is None else even + part
        even = even.reshape(half, half, 2, frames, size)
        for clip in range(2):
            value = nt(g_ref[clip], w_ref[...]).reshape(half, 2, half, 2, frames, size)
            both = jnp.stack([value[:, 0, :, 0] + even[:, :, clip], value[:, 0, :, 1]], axis=2)
            line = jnp.stack([both, value[:, 1]], axis=1)
            out_ref[clip] = line.reshape(all_rows, size).astype(BF)

    groups, _, _ = project.array.shape
    if groups == 1:
        size_rows = project.rows // parts
        project_block = pl.BlockSpec((1, project.count * project.rows, middle), lambda n: (0, 0, 0))
    else:
        project_block = pl.BlockSpec(
            (groups // parts, project.count * project.rows, middle), lambda n: (n, 0, 0)
        )
    if groups == 1:

        def of(ref, k):
            begin = k * project.rows + pl.program_id(0) * size_rows
            return ref[0, pl.ds(pl.multiple_of(begin, size_rows), size_rows), :]

        project.of = of
    ins = (grad, weight, shortcut, project.array)
    in_specs = [
        pl.BlockSpec((2, all_rows, middle), lambda n: (pair, 0, 0)),
        pl.BlockSpec((size, middle), lambda n: (n, 0)),
        pl.BlockSpec((pixels, 2 * frames, wide), lambda n: (0, pair, 0)),
        project_block,
    ]
    alias = {}
    if into is not None:
        ins += (into,)
        in_specs.append(pl.BlockSpec(memory_space=pl.ANY))
        alias = {4: 0}
    return pl.pallas_call(
        body,
        grid=(parts,),
        in_specs=in_specs,
        out_specs=pl.BlockSpec((2, all_rows, size), lambda n: (pair, 0, n)),
        out_shape=jax.ShapeDtypeStruct((slots, all_rows, c_in), BF),
        input_output_aliases=alias,
        compiler_params=pltpu.CompilerParams(
            vmem_limit_bytes=56 * 1024 * 1024, dimension_semantics=("arbitrary",)
        ),
        cost_estimate=pl.CostEstimate(
            flops=(grad.size + shortcut.size) * c_in,
            bytes_accessed=grad.size + shortcut.size + slots * all_rows * c_in,
            transcendentals=0,
        ),
    )(*ins)


CHUNK = 256


def fold(value):
    return jnp.sum(value.reshape(-1, 8, value.shape[-1]), axis=0)


def chunks(width):
    return [slice(b, min(b + CHUNK, width)) for b in range(0, width, CHUNK)]


def zero_first(*refs):
    @pl.when(pl.program_id(0) == 0)
    def _():
        for ref in refs:
            ref[...] = jnp.zeros_like(ref)


def row_block(half, batch, width):
    return (half, batch, width), lambda i: (i, 0, 0)


class Packed:
    def __init__(self, array, rows, first, count):
        self.array, self.rows, self.first, self.count = array, rows, first, count

    def block(self):
        size, index = self.rows * self.count, self.first // self.count
        return (self.array.shape[0], size, self.array.shape[2]), lambda *_: (0, index, 0)

    def part(self, ref, k, size):
        if self.array.shape[0] == 1:
            return ref[0, k * size : (k + 1) * size, :]
        parts = size // self.rows
        return ref[k * parts : (k + 1) * parts].reshape(size, -1)

    def of(self, ref, k):
        part = ref[:, k * self.rows : (k + 1) * self.rows, :]
        return part.reshape(-1, part.shape[-1])


def nt(left, right):
    return lax.dot_general(left, right, (((1,), (1,)), ((), ())), preferred_element_type=F32)


def tn(left, right):
    return lax.dot_general(left, right, (((0,), (0,)), ((), ())), preferred_element_type=F32)


def nn(left, right):
    return jnp.dot(left, right, preferred_element_type=F32)


def kernel_expand(raw_b, stats, mask, weight, half):
    _, batch, middle = raw_b.shape
    wide = weight.count * middle
    rows = half * batch

    def body(b_ref, s_ref, m_ref, w_ref, act_ref, raw_ref, off_ref, sum_ref):
        zero_first(sum_ref)
        m = m_ref[...]

        for c in chunks(middle):
            al, be = s_ref[0:1, c], s_ref[1:2, c]
            for j in range(half):
                act_ref[j, :, c] = (silu_parts(b_ref[j, :, c] * al + be)[1] * m).astype(BF)


        @pl.when(pl.program_id(0) == 0)
        def _():
            for k in range(weight.count):
                few = nn(act_ref[half // 2], weight.of(w_ref, k))
                off_ref[0:1, k * middle : (k + 1) * middle] = mean_of(few, m_ref[:, :1])

        m = m_ref[:, :1]
        act = act_ref[...].reshape(rows, middle)
        for k in range(weight.count):
            raw = nn(act, weight.of(w_ref, k)).reshape(half, batch, middle)
            span = slice(k * middle, (k + 1) * middle)
            offset = off_ref[0:1, span]
            raw_ref[:, :, span] = (raw - offset).astype(BF)
            sum_ref[0, :, span] += fold(jnp.sum(raw, axis=0) * m)
            sum_ref[1, :, span] += fold(jnp.sum(raw * raw, axis=0) * m)

    pixels = half * half
    return call(
        body,
        (half,),
        (raw_b, stats, mask, weight.array),
        (row_block(half, batch, middle), whole(stats.shape), whole(mask.shape), weight.block()),
        (
            ((pixels, batch, middle), BF),
            ((pixels, batch, wide), BF), ((8, wide), F32),
            ((2, 8, wide), F32),
        ),
        (row_block(half, batch, middle), row_block(half, batch, wide), whole((8, wide)), whole((2, 8, wide))),
        flops=2 * raw_b.size * wide,
        moved=raw_b.size * 6 + pixels * batch * wide * 4,
    )


def kernel_project(sampled, mask, weight, half):
    pixels, batch, c_in = sampled.shape
    middle = weight.array.shape[2]
    wide = weight.count * middle

    def body(x_ref, m_ref, w_ref, raw_ref, off_ref, sum_ref):
        zero_first(sum_ref)

        @pl.when(pl.program_id(0) == 0)
        def _():
            for k in range(weight.count):
                few = nn(x_ref[half // 2], weight.of(w_ref, k))
                off_ref[0:1, k * middle : (k + 1) * middle] = mean_of(few, m_ref[:, :1])

        m = m_ref[:, :1]
        left = x_ref[...].reshape(half * batch, c_in)
        for k in range(weight.count):
            raw = nn(left, weight.of(w_ref, k)).reshape(half, batch, middle)
            span = slice(k * middle, (k + 1) * middle)
            offset = off_ref[0:1, span]
            raw_ref[:, :, span] = (raw - offset).astype(BF)
            sum_ref[0, :, span] += fold(jnp.sum(raw, axis=0) * m)
            sum_ref[1, :, span] += fold(jnp.sum(raw * raw, axis=0) * m)

    return call(
        body,
        (half,),
        (sampled, mask, weight.array),
        (row_block(half, batch, c_in), whole(mask.shape), weight.block()),
        (((pixels, batch, wide), BF), ((8, wide), F32), ((2, 8, wide), F32)),
        (row_block(half, batch, wide), whole((8, wide)), whole((2, 8, wide))),
        flops=2 * sampled.size * wide,
        moved=sampled.size * 2 + pixels * batch * wide * 4,
    )


def kernel_block_one(raw_c, raw_p, stats, mask, weight, half):
    pixels, batch, wide = raw_c.shape
    middle = weight.array.shape[2]

    def body(c_ref, p_ref, s_ref, m_ref, w_ref, one_ref, raw_ref, send_ref, sum_ref):
        zero_first(sum_ref)
        m = m_ref[...]

        raw = None
        for k in range(wide // middle):
            for c in chunks(middle):
                c = slice(k * middle + c.start, k * middle + c.stop)
                al, ap, be = s_ref[0:1, c], s_ref[1:2, c], s_ref[2:3, c]
                for j in range(half):
                    total = c_ref[j, :, c].astype(F32) * al + p_ref[j, :, c].astype(F32) * ap + be
                    one_ref[j, :, c] = (silu_parts(total)[1] * m).astype(BF)
            left = one_ref[:, :, k * middle : (k + 1) * middle].reshape(half * batch, middle)
            part = nn(left, weight.part(w_ref, k, middle))
            raw = part if raw is None else raw + part
        raw = raw.reshape(half, batch, middle)
        m = m_ref[:, :1]
        raw_ref[...] = raw
        sum_ref[0] += fold(jnp.sum(raw, axis=0) * m)
        sum_ref[1] += fold(jnp.sum(raw * raw, axis=0) * m)
        send_sums(send_ref, sum_ref, pl.program_id(0) == half - 1)

    return call(
        body,
        (half,),
        (raw_c, raw_p, stats, mask, weight.array),
        (
            row_block(half, batch, wide),
            row_block(half, batch, wide),
            whole(stats.shape),
            whole(mask.shape),
            weight.block(),
        ),
        (
            ((pixels, batch, wide), BF),
            ((pixels, batch, middle), F32),
            (exchange_shape(2 * middle), F32),
        ),
        (row_block(half, batch, wide), row_block(half, batch, middle), whole(exchange_shape(2 * middle))),
        scratch=[pltpu.VMEM((2, 8, middle), F32)],
        flops=2 * raw_c.size * middle,
        moved=raw_c.size * 10,
    )


def kernel_result(raw_e, block_one, cot, stats, mask, half):
    pixels, batch, wide = raw_e.shape
    slots, _, _, frames, _ = cot.shape

    def body(e_ref, o_ref, g_ref, s_ref, m_ref, res_ref, grad_ref, sum_ref):
        zero_first(sum_ref)
        m = m_ref[...]
        for c in chunks(wide):
            al, be, mean = s_ref[0:1, c], s_ref[1:2, c], s_ref[2:3, c]
            first = second = None
            for j in range(half):
                raw = e_ref[j, :, c].astype(F32)
                sig, act = silu_parts(raw * al + be + o_ref[j, :, c].astype(F32))
                res = act * m
                for s in range(slots):
                    res_ref[s, 0, j, :, c] = res[s * frames : (s + 1) * frames].astype(BF)
                cot = jnp.concatenate([g_ref[s, 0, j, :, c].astype(F32) for s in range(slots)])
                grad = cot * m * (sig + act * (1.0 - sig))
                grad_ref[j, :, c] = grad.astype(BF)
                other = grad * (raw - mean)
                first = grad if first is None else first + grad
                second = other if second is None else second + other
            sum_ref[0, :, c] += fold(first)
            sum_ref[1, :, c] += fold(second)

    outside = (slots, 1, half, frames, wide), lambda i: (0, i, 0, 0, 0)
    return call(
        body,
        (half,),
        (raw_e, block_one, cot, stats, mask),
        (
            row_block(half, batch, wide),
            row_block(half, batch, wide),
            outside,
            whole(stats.shape),
            whole(mask.shape),
        ),
        (
            (cot.shape, BF),
            ((pixels, batch, wide), BF),
            ((2, 8, wide), F32),
        ),
        (outside, row_block(half, batch, wide), whole((2, 8, wide))),
        flops=20 * raw_e.size,
        moved=raw_e.size * 14,
    )


def kernel_block_back(grad_narrow, raw_d, stats_d, weight, grad_total, raw_c, raw_p, stats, mask, half):
    pixels, batch, wide = raw_c.shape
    middle = raw_d.shape[2]

    def body(n_ref, d_ref, sd_ref, w_ref, t_ref, c_ref, p_ref, s_ref, m_ref, nar_ref, one_ref, sum_ref, back):
        zero_first(sum_ref)
        m = m_ref[...]

        for c in chunks(middle):
            scale, mean, shift, spread = (sd_ref[n : n + 1, c] for n in range(4))
            for j in range(half):
                value = scale * n_ref[j, :, c] - m * (shift + (d_ref[j, :, c] - mean) * spread)
                nar_ref[j, :, c] = value.astype(BF)

        left = nar_ref[...].reshape(half * batch, middle)
        for k in range(wide // middle):
            back[k] = nt(left, weight.part(w_ref, k, middle)).reshape(half, batch, middle)
            for d in chunks(middle):
                c = slice(k * middle + d.start, k * middle + d.stop)
                al, ap, be, mean_c, _, mean_p = (s_ref[n : n + 1, c] for n in range(6))
                sums = [None] * 3
                for j in range(half):
                    raw_c, raw_p = c_ref[j, :, c].astype(F32), p_ref[j, :, c].astype(F32)
                    sig, act = silu_parts(raw_c * al + raw_p * ap + be)
                    grad = (t_ref[j, :, c].astype(F32) + back[k, j, :, d]) * m * (sig + act * (1.0 - sig))
                    one_ref[j, :, c] = grad.astype(BF)
                    parts = (grad, grad * (raw_c - mean_c), grad * (raw_p - mean_p))
                    sums = [p if t is None else t + p for t, p in zip(sums, parts)]
                for n in range(3):
                    sum_ref[n, :, c] += fold(sums[n])

    return call(
        body,
        (half,),
        (grad_narrow, raw_d, stats_d, weight.array, grad_total, raw_c, raw_p, stats, mask),
        (
            row_block(half, batch, middle),
            row_block(half, batch, middle),
            whole(stats_d.shape),
            weight.block(),
            row_block(half, batch, wide),
            row_block(half, batch, wide),
            row_block(half, batch, wide),
            whole(stats.shape),
            whole(mask.shape),
        ),
        (
            ((pixels, batch, middle), BF),
            ((pixels, batch, wide), BF),
            ((3, 8, wide), F32),
        ),
        (row_block(half, batch, middle), row_block(half, batch, wide), whole((3, 8, wide))),
        scratch=[pltpu.VMEM((wide // middle, half, batch, middle), F32)],
        flops=2 * raw_c.size * middle,
        moved=raw_c.size * 16,
    )


def kernel_expand_back(grad_one, raw_c, raw_p, stats, weight, raw_b, stats_b, mask, half):
    pixels, batch, wide = raw_c.shape
    middle = raw_b.shape[2]

    def body(g_ref, c_ref, p_ref, s_ref, w_ref, b_ref, sb_ref, m_ref, wid_ref, sho_ref, out_ref, send_ref, sum_ref):
        zero_first(sum_ref)
        m = m_ref[...]
        back = None
        for k in range(weight.count):
            for c in chunks(middle):
                c = slice(k * middle + c.start, k * middle + c.stop)
                rows_s = [s_ref[n : n + 1, c] for n in range(8)]
                for j in range(half):
                    grad = g_ref[j, :, c].astype(F32)
                    for raw_ref, to_ref, n in ((c_ref, wid_ref, 0), (p_ref, sho_ref, 4)):
                        scale, mean, shift, spread = rows_s[n : n + 4]
                        value = scale * grad - m * (shift + (raw_ref[j, :, c].astype(F32) - mean) * spread)
                        to_ref[j, :, c] = value.astype(BF)
            left = wid_ref[:, :, k * middle : (k + 1) * middle].reshape(half * batch, middle)
            part = nt(left, weight.of(w_ref, k))
            back = part if back is None else back + part
        m = m_ref[:, :1]
        raw = b_ref[...]
        sig, act = silu_parts(raw * sb_ref[0:1] + sb_ref[1:2])
        grad = back.reshape(half, batch, middle) * m * (sig + act * (1.0 - sig))
        out_ref[...] = grad
        sum_ref[0] += fold(jnp.sum(grad, axis=0))
        sum_ref[1] += fold(jnp.sum(grad * ((raw - sb_ref[2:3]) * sb_ref[3:4]), axis=0))
        send_sums(send_ref, sum_ref, pl.program_id(0) == half - 1)

    return call(
        body,
        (half,),
        (grad_one, raw_c, raw_p, stats, weight.array, raw_b, stats_b, mask),
        (
            row_block(half, batch, wide),
            row_block(half, batch, wide),
            row_block(half, batch, wide),
            whole(stats.shape),
            weight.block(),
            row_block(half, batch, middle),
            whole(stats_b.shape),
            whole(mask.shape),
        ),
        (
            ((pixels, batch, wide), BF),
            ((pixels, batch, wide), BF),
            ((pixels, batch, middle), F32),
            (exchange_shape(2 * middle), F32),
        ),
        (
            row_block(half, batch, wide),
            row_block(half, batch, wide),
            row_block(half, batch, middle),
            whole(exchange_shape(2 * middle)),
        ),
        scratch=[pltpu.VMEM((2, 8, middle), F32)],
        flops=2 * raw_c.size * middle,
        moved=raw_c.size * 16,
    )


def kernel_join(excited, outputs, raw_g, stats_g, mask, weight, half):
    pixels, batch, middle = excited.shape
    group = middle // 4
    wide = weight.count * middle

    def body(x_ref, o1, o2, r_ref, sg_ref, m_ref, w_ref, join_ref, raw_ref, off_ref, sum_ref):
        zero_first(sum_ref)
        m = m_ref[:, :group]
        join_ref[:, :, :group] = x_ref[...]
        join_ref[:, :, group : 2 * group] = o1[...]
        join_ref[:, :, 2 * group : 3 * group] = o2[...]
        act = silu_parts(r_ref[...] * sg_ref[0:1] + sg_ref[1:2])[1] * m
        join_ref[:, :, 3 * group :] = act.astype(BF)

        @pl.when(pl.program_id(0) == 0)
        def _():
            for k in range(weight.count):
                few = nn(join_ref[half // 2], weight.of(w_ref, k))
                off_ref[0:1, k * middle : (k + 1) * middle] = mean_of(few, m_ref[:, :1])

        left = join_ref[...].reshape(half * batch, middle)
        m = m_ref[:, :1]
        for k in range(weight.count):
            raw = nn(left, weight.of(w_ref, k)).reshape(half, batch, middle)
            span = slice(k * middle, (k + 1) * middle)
            offset = off_ref[0:1, span]
            raw_ref[:, :, span] = (raw - offset).astype(BF)
            sum_ref[0, :, span] += fold(jnp.sum(raw, axis=0) * m)
            sum_ref[1, :, span] += fold(jnp.sum(raw * raw, axis=0) * m)

    part = row_block(half, batch, group)
    return call(
        body,
        (half,),
        (excited, outputs[0], outputs[1], raw_g, stats_g, mask, weight.array),
        (part, part, part, part, whole(stats_g.shape), whole(mask.shape), weight.block()),
        (((pixels, batch, middle), BF), ((pixels, batch, wide), BF), ((8, wide), F32), ((2, 8, wide), F32)),
        (row_block(half, batch, middle), row_block(half, batch, wide), whole((8, wide)), whole((2, 8, wide))),
        flops=2 * excited.size * wide,
        moved=excited.size * 4 + pixels * batch * wide * 4,
    )


def kernel_final_back(grad_total, raw_e, stats, mask, weight, raw_g, stats_g, half):
    pixels, batch, wide = raw_e.shape
    middle = weight.array.shape[2]
    group = middle // 4

    def body(g_ref, e_ref, s_ref, m_ref, w_ref, r_ref, sg_ref, fin_ref, out_ref, pre_ref, send_ref, sum_ref):
        zero_first(sum_ref)
        m = m_ref[...]

        back = None
        for k in range(weight.count):
            for c in chunks(middle):
                c = slice(k * middle + c.start, k * middle + c.stop)
                scale, mean, shift, spread = (s_ref[n : n + 1, c] for n in range(4))
                for j in range(half):
                    value = scale * g_ref[j, :, c].astype(F32) - m * (
                        shift + (e_ref[j, :, c].astype(F32) - mean) * spread
                    )
                    fin_ref[j, :, c] = value.astype(BF)
            left = fin_ref[:, :, k * middle : (k + 1) * middle].reshape(half * batch, middle)
            part = nt(left, weight.of(w_ref, k))
            back = part if back is None else back + part
        back = back.reshape(half, batch, middle)
        out_ref[...] = back
        raw = r_ref[...]
        sig, act = silu_parts(raw * sg_ref[0:1] + sg_ref[1:2])
        pre = back[:, :, 3 * group :] * m_ref[:, :group] * (sig + act * (1.0 - sig))
        pre_ref[...] = pre
        sum_ref[0] += fold(jnp.sum(pre, axis=0))
        sum_ref[1] += fold(jnp.sum(pre * (raw - sg_ref[2:3]), axis=0))
        send_sums(send_ref, sum_ref, pl.program_id(0) == half - 1)

    part = row_block(half, batch, group)
    return call(
        body,
        (half,),
        (grad_total, raw_e, stats, mask, weight.array, raw_g, stats_g),
        (
            row_block(half, batch, wide),
            row_block(half, batch, wide),
            whole(stats.shape),
            whole(mask.shape),
            weight.block(),
            part,
            whole(stats_g.shape),
        ),
        (
            ((pixels, batch, wide), BF),
            ((pixels, batch, middle), F32),
            ((pixels, batch, group), F32),
            (exchange_shape(2 * group), F32),
        ),
        (row_block(half, batch, wide), row_block(half, batch, middle), part, whole(exchange_shape(2 * group))),
        scratch=[pltpu.VMEM((2, 8, group), F32)],
        flops=2 * raw_e.size * middle,
        moved=raw_e.size * 10,
    )


def kernel_weight_grad(left, right, dp, fsdp, rows, first, total, into=None):
    pixels, batch, depth = left.shape
    columns = right.shape[2]
    middle = min(columns, 512)
    owners = dp * fsdp

    def body(*refs):
        a_ref, b_ref, out_ref = refs[0], refs[1], refs[-1]
        value = tn(a_ref[...].reshape(-1, depth), b_ref[...].reshape(-1, middle)).astype(BF)
        value = value.reshape(dp, fsdp, rows, middle)
        for d in range(dp):
            out_ref[:, d] = value[d]

    ins = (left, right)
    in_specs = [
        pl.BlockSpec((pixels, batch, depth), lambda k: (0, 0, 0)),
        pl.BlockSpec((pixels, batch, middle), lambda k: (0, 0, k)),
    ]
    alias = {}
    if into is not None:
        ins += (into,)
        in_specs.append(pl.BlockSpec(memory_space=pl.ANY))
        alias = {2: 0}
    return pl.pallas_call(
        body,
        grid=(columns // middle,),
        in_specs=in_specs,
        out_specs=pl.BlockSpec((fsdp, dp, rows, middle), lambda k: (0, 0, first + k, 0)),
        out_shape=jax.ShapeDtypeStruct((fsdp, dp, total, middle), BF),
        input_output_aliases=alias,
        compiler_params=pltpu.CompilerParams(
            vmem_limit_bytes=56 * 1024 * 1024, dimension_semantics=("arbitrary",)
        ),
        cost_estimate=pl.CostEstimate(
            flops=2 * left.size * columns,
            bytes_accessed=left.size * 2 + right.size * 2 + owners * rows * columns * 2,
            transcendentals=0,
        ),
    )(*ins)


def frame_rows(rows):
    return lax.broadcasted_iota(jnp.int32, (1, rows, 128), 1)


def shift_frames(value, frames):
    shape = value.shape
    value = value.reshape(-1, frames, 128)
    spot = frame_rows(frames)
    before = jnp.where(spot == 0, 0.0, pltpu.roll(value, 1, 1))
    after_ = jnp.where(spot == frames - 1, 0.0, pltpu.roll(value, frames - 1, 1))
    return before.reshape(shape), after_.reshape(shape)


def nine_taps(pad, cols, half, batch):
    for r in range(3):
        for c in range(3):
            lane = (r * 3 + c) * 128
            part = pad[r : r + half, c : c + half]
            cols[:, lane : lane + 128] = part.reshape(half * half * batch, 128)


def clear_border(pad, half):
    pad[0] = jnp.zeros_like(pad[0])
    pad[half + 1] = jnp.zeros_like(pad[0])
    pad[:, 0] = jnp.zeros_like(pad[:, 0])
    pad[:, half + 1] = jnp.zeros_like(pad[:, 0])


def kernel_motion(rows_d, stats, mask, weight, windows, half):
    pixels, batch, middle = rows_d.shape
    narrow = weight.shape[1]

    def body(d_ref, s_ref, m_ref, w_ref, act_ref, raw_ref, win_ref, sq_ref):
        for c in chunks(middle):
            al, be, m = s_ref[0:1, c], s_ref[1:2, c], m_ref[...]

            @pl.loop(0, half)
            def _(i):
                for j in range(half):
                    act = silu_parts(d_ref[i * half + j, :, c] * al + be)[1] * m
                    act_ref[i * half + j, :, c] = act.astype(BF)

        raw = nn(act_ref[...].reshape(pixels * batch, middle), w_ref[...])
        raw_ref[...] = raw.reshape(pixels, batch, narrow)
        square = jnp.zeros((batch, narrow), F32)
        sums = [jnp.zeros((batch, narrow), F32) for _ in range(9)]
        for p in range(pixels):
            value = raw_ref[p]
            square = square + value * value
            for t in range(9):
                if windows[p // half][p % half][t]:
                    sums[t] = sums[t] + value
        for t in range(9):
            win_ref[t] = sums[t]
        sq_ref[...] = square

    return call(
        body,
        (1,),
        (rows_d, stats, mask, weight),
        (whole(rows_d.shape), whole(stats.shape), whole(mask.shape), whole(weight.shape)),
        (
            (rows_d.shape, BF),
            ((pixels, batch, narrow), F32),
            ((9, batch, narrow), F32),
            ((batch, narrow), F32),
        ),
        (
            whole(rows_d.shape),
            whole((pixels, batch, narrow)),
            whole((9, batch, narrow)),
            whole((batch, narrow)),
        ),
        flops=2 * rows_d.size * narrow,
        moved=rows_d.size * 6,
    )


def kernel_group(source, extra, taps, weight, mask, index, half, frames):
    pixels, batch, middle = source.shape
    group = 128

    def body(*refs):
        if index == 1:
            x_ref, e_ref, t_ref, w_ref, m_ref, first_ref, pad_ref, raw_ref, send_ref, cols, sum_ref = refs
            excited = (x_ref[...].astype(F32) * e_ref[...]).astype(BF)
            first_ref[...] = excited
            piece = first_ref[:, :, group : 2 * group].astype(F32)
        else:
            x_ref, r_ref, s_ref, t_ref, w_ref, m_ref, first_ref, pad_ref, raw_ref, send_ref, cols, sum_ref = refs
            act = silu_parts(r_ref[...] * s_ref[0:1] + s_ref[1:2])[1] * m_ref[:, :group]
            first_ref[...] = act.astype(BF)
            piece = x_ref[...].astype(F32) + first_ref[...].astype(F32)
        before, after_ = shift_frames(piece, frames)
        value = t_ref[0:1] * before + t_ref[1:2] * piece + t_ref[2:3] * after_
        clear_border(pad_ref, half)
        pad_ref[1 : half + 1, 1 : half + 1] = value.astype(BF).reshape(half, half, batch, group)
        nine_taps(pad_ref, cols, half, batch)
        raw = nn(cols[...], w_ref[...]).reshape(pixels, batch, group)
        raw_ref[...] = raw
        m = m_ref[:, :group]
        sum_ref[0] = fold(jnp.sum(raw, axis=0) * m)
        sum_ref[1] = fold(jnp.sum(raw * raw, axis=0) * m)
        send_sums(send_ref, sum_ref)

    block = (pixels, batch, group)
    if index == 1:
        ins = (source, extra, taps, weight, mask)
        first = (source.shape, BF)
        specs = tuple(whole(a.shape) for a in ins)
    else:
        ins = (source, extra[0], extra[1], taps, weight, mask)
        first = (block, BF)
        specs = ((block, lambda i: (0, 0, index)),) + tuple(whole(a.shape) for a in ins[1:])
    outs = (
        first,
        ((half + 2, half + 2, batch, group), BF),
        (block, F32),
        (exchange_shape(2 * group), F32),
    )
    return call(
        body,
        (1,),
        ins,
        specs,
        outs,
        tuple(whole(o[0]) for o in outs),
        scratch=[pltpu.VMEM((pixels * batch, 9 * group), BF), pltpu.VMEM((2, 8, group), F32)],
        flops=2 * pixels * batch * 9 * group * group,
        moved=pixels * batch * group * 12,
    )


def kernel_group_weights(pad, grad, half):
    pixels, batch, group = grad.shape

    def body(p_ref, g_ref, out_ref, cols):
        nine_taps(p_ref, cols, half, batch)
        out_ref[...] = tn(cols[...], g_ref[...].reshape(pixels * batch, group)).astype(BF)

    return call(
        body,
        (1,),
        (pad, grad),
        (whole(pad.shape), whole(grad.shape)),
        (((9 * group, group), BF),),
        (whole((9 * group, group)),),
        scratch=[pltpu.VMEM((pixels * batch, 9 * group), BF)],
        flops=2 * grad.size * 9 * group,
        moved=grad.size * 6,
    )[0]


def kernel_group_back(
    grad, raw, stats, weight, taps, excited, previous, joined, lower, mask, index, half, frames
):
    pixels, batch, group = grad.shape
    block = (pixels, batch, group)
    rows = pixels * batch

    def body(*refs):
        g_ref, r_ref, s_ref, w_ref, t_ref, x_ref, j_ref, m_ref = refs[:8]
        pad, cols, sum_ref = refs[-3:]
        m = m_ref[:, :group]
        raw = r_ref[...]
        value = s_ref[0:1] * g_ref[...] - m * (s_ref[2:3] + (raw - s_ref[1:2]) * s_ref[3:4])
        if index > 1:
            p_ref, l_ref, ls_ref, gg_ref, gp_ref, tg_ref, pre_ref, send_ref = refs[8:16]
        else:
            g2_ref, g3_ref, d_ref, gg_ref, gp_ref, tg_ref, at_ref = refs[8:15]
        gg_ref[...] = value.astype(BF)
        clear_border(pad, half)
        pad[1 : half + 1, 1 : half + 1] = gg_ref[...].reshape(half, half, batch, group)
        nine_taps(pad, cols, half, batch)
        back = nn(cols[...], w_ref[...]).reshape(block)
        before, after_ = shift_frames(back, frames)
        below = t_ref[0:1] * after_ + t_ref[1:2] * back + t_ref[2:3] * before
        gp_ref[...] = below
        piece = x_ref[...].astype(F32)
        if index > 1:
            piece = piece + p_ref[...].astype(F32)
        tg_ref[0] = fold(jnp.sum(after_ * piece, axis=0))
        tg_ref[1] = fold(jnp.sum(back * piece, axis=0))
        tg_ref[2] = fold(jnp.sum(before * piece, axis=0))
        if index > 1:
            raw = l_ref[...]
            sig, act = silu_parts(raw * ls_ref[0:1] + ls_ref[1:2])
            pre = (j_ref[...] + below) * m * (sig + act * (1.0 - sig))
            pre_ref[...] = pre
            sum_ref[0] = fold(jnp.sum(pre, axis=0))
            sum_ref[1] = fold(jnp.sum(pre * (raw - ls_ref[2:3]), axis=0))
            send_sums(send_ref, sum_ref)
        else:
            for k, source in enumerate((j_ref, gp_ref, g2_ref, g3_ref)):
                span = slice(k * group, (k + 1) * group)
                at_ref[:, span] = jnp.sum(source[...] * d_ref[:, :, span].astype(F32), axis=0)

    column = lambda k: (block, lambda i: (0, 0, k))
    ins = [grad, raw, stats, weight, taps, excited, joined, mask]
    specs = [whole(a.shape) for a in ins]
    specs[5] = column(index)
    specs[6] = column(index - 1)
    outs = [(block, BF), (block, F32), ((3, 8, group), F32)]
    if index > 1:
        more = [previous, lower[0], lower[1]]
        outs += [(block, F32), (exchange_shape(2 * group), F32)]
    else:
        more = list(previous)
        outs += [((batch, 4 * group), F32)]
    return call(
        body,
        (1,),
        ins + more,
        specs + [whole(a.shape) for a in more],
        outs,
        [whole(o[0]) for o in outs],
        scratch=[
            pltpu.VMEM((half + 2, half + 2, batch, group), BF),
            pltpu.VMEM((rows, 9 * group), BF),
            pltpu.VMEM((2, 8, group), F32),
        ],
        flops=2 * rows * 9 * group * group,
        moved=rows * group * 24,
    )


def kernel_motion_back(
    joined, pieces, attend, rows_d, stats_d, raw_m, kmap, change, stats_m, weight, mask, half
):
    pixels, batch, middle = rows_d.shape
    narrow = raw_m.shape[2]
    group = middle // 4

    def body(j_ref, p1, p2, p3, e_ref, d_ref, sd_ref, r_ref, k_ref, c_ref, sm_ref, w_ref, m_ref, out_ref, mg_ref, send_ref, sum_ref):
        zero_first(sum_ref)
        mn = m_ref[:, :narrow]
        grad = (k_ref[...] * c_ref[0] - c_ref[1]) * mn
        value = sm_ref[0:1] * grad - mn * (sm_ref[2:3] + (r_ref[...] - sm_ref[1:2]) * sm_ref[3:4])
        mg_ref[...] = value.astype(BF)
        back = nt(mg_ref[...].reshape(half * batch, narrow), w_ref[...])
        back = back.reshape(half, batch, middle)
        m = m_ref[:, :group]
        for k, ref in enumerate((j_ref, p1, p2, p3)):
            c = slice(k * group, (k + 1) * group)
            raw = d_ref[:, :, c]
            sig, act = silu_parts(raw * sd_ref[0:1, c] + sd_ref[1:2, c])
            out = (ref[...] * e_ref[:, c] + back[:, :, c]) * m * (sig + act * (1.0 - sig))
            out_ref[:, :, c] = out
            sum_ref[0, :, c] += fold(jnp.sum(out, axis=0))
            sum_ref[1, :, c] += fold(jnp.sum(out * (raw - sd_ref[2:3, c]), axis=0))
        send_sums(send_ref, sum_ref, pl.program_id(0) == half - 1)

    part = row_block(half, batch, group)
    ins = (joined,) + tuple(pieces)
    ins += (attend, rows_d, stats_d, raw_m, kmap, change, stats_m, weight, mask)
    return call(
        body,
        (half,),
        ins,
        (
            part,
            part,
            part,
            part,
            whole(attend.shape),
            row_block(half, batch, middle),
            whole(stats_d.shape),
            row_block(half, batch, narrow),
            ((half, 1, narrow), lambda i: (i, 0, 0)),
            whole(change.shape),
            whole(stats_m.shape),
            whole(weight.shape),
            whole(mask.shape),
        ),
        (
            ((pixels, batch, middle), F32),
            ((pixels, batch, narrow), BF),
            (exchange_shape(2 * middle), F32),
        ),
        (row_block(half, batch, middle), row_block(half, batch, narrow), whole(exchange_shape(2 * middle))),
        scratch=[pltpu.VMEM((2, 8, middle), F32)],
        flops=2 * rows_d.size * narrow,
        moved=rows_d.size * 12,
    )


class Sums:
    def __init__(self, dp, fsdp):
        self.devices = dp * fsdp
        half = self.devices // 2
        self.groups = [[2 * i + c for i in range(half)] for c in range(2)]
        self.swap = [(i, i ^ 1) for i in range(self.devices)]

    def flat(self, values):
        size = values.shape[0]
        if size <= 2048:
            copies = jnp.broadcast_to(values[None], (self.devices, size))
            return jnp.sum(lax.all_to_all(copies, AXES, 0, 0), axis=0)
        core = lax.axis_index("fsdp") % 2
        halves = values.reshape(2, size // 2)
        mine = lax.dynamic_index_in_dim(halves, core, 0, False)
        other = lax.dynamic_index_in_dim(halves, 1 - core, 0, False)
        mine = mine + lax.ppermute(other, AXES, self.swap)
        copies = jnp.broadcast_to(mine[None], (self.devices // 2, size // 2))
        mine = jnp.sum(lax.all_to_all(copies, AXES, 0, 0, axis_index_groups=self.groups), axis=0)
        other = lax.ppermute(mine, AXES, self.swap)
        low = jnp.where(core == 0, mine, other)
        high = jnp.where(core == 0, other, mine)
        return jnp.concatenate([low, high])

    def ready(self, copies, count):
        total = jnp.sum(lax.all_to_all(copies, AXES, 0, 0, tiled=True), axis=(0, 1))
        return list(total.reshape(count, -1))

    def __call__(self, *arrays):
        sizes = [a.size for a in arrays]
        extra = -sum(sizes) % 256
        parts = [a.reshape(-1) for a in arrays]
        if extra:
            parts.append(jnp.zeros((extra,), F32))
        merged = self.flat(jnp.concatenate(parts))
        out, begin = [], 0
        for a, size in zip(arrays, sizes):
            out.append(merged[begin : begin + size].reshape(a.shape))
            begin += size
        return out


def pairs_of(dp, fsdp):
    return [(i, i ^ 1) for i in range(dp * fsdp)]


def same_core(fsdp):
    return [[2 * i + c for i in range(fsdp // 2)] for c in range(2)]


def quick_gather(dp, fsdp, value):
    value = lax.all_to_all(jnp.broadcast_to(value[None], (dp,) + value.shape), "dp", 0, 0)
    value = lax.all_to_all(
        jnp.broadcast_to(value[None], (fsdp // 2,) + value.shape),
        "fsdp",
        0,
        0,
        axis_index_groups=same_core(fsdp),
    )
    other = lax.ppermute(value, AXES, pairs_of(dp, fsdp))
    core = lax.axis_index("fsdp") % 2
    low = jnp.where(core == 0, value, other)
    high = jnp.where(core == 0, other, value)
    both = jnp.stack([low, high], axis=2).swapaxes(0, 1)
    return both.reshape((dp * fsdp,) + both.shape[3:])


def scatter_cores(dp, fsdp, value):
    core = lax.axis_index("fsdp") % 2
    mine = lax.dynamic_index_in_dim(value, core, 0, False)
    other = lax.dynamic_index_in_dim(value, 1 - core, 0, False)
    other = lax.ppermute(other, AXES, pairs_of(dp, fsdp))
    return (mine.astype(F32) + other.astype(F32)).astype(BF)


def scatter_halves(dp, value, bit):
    mine = (lax.axis_index("dp") >> bit) & 1
    other = lax.dynamic_index_in_dim(value, 1 - mine, 0, False)
    other = lax.ppermute(other, "dp", [(i, i ^ (1 << bit)) for i in range(dp)])
    mine = lax.dynamic_index_in_dim(value, mine, 0, False)
    return (mine.astype(F32) + other.astype(F32)).astype(BF)


def scatter_fsdp(fsdp, value):
    value = lax.all_to_all(value, "fsdp", 0, 0, axis_index_groups=same_core(fsdp))
    return jnp.sum(value.astype(F32), axis=0)


def scatter_dp(value):
    return jnp.sum(lax.all_to_all(value, "dp", 0, 0).astype(F32), axis=0)


def by_low_bit(count):
    order = [0]
    while len(order) < count:
        order = [2 * i for i in order] + [2 * i + 1 for i in order]
    return order


def after(value, *others):
    return lax.optimization_barrier((value, others))[0]


def affine(total, square, count, gain, bias, offset=0.0):
    mean = total / count
    inv = lax.rsqrt(square / count - mean * mean + EPSILON)
    alpha = gain * inv
    mean = mean - offset
    return mean, inv, alpha, bias - mean * alpha


def local(
    dp,
    fsdp,
    clip_count,
    frame_count,
    frame_mask,
    features,
    w_reduce1,
    w_spatial1,
    w_expand1,
    w_project1,
    w_reduce2,
    w_motion_in,
    w_motion_out,
    w_spatial2,
    w_expand2,
    gains,
    biases,
    motion_taps,
    temporal_taps,
    cotangent,
):
    devices = dp * fsdp
    sums = Sums(dp, fsdp)
    slots, frames, height = features.shape[:3]
    half = height // 2
    area = half * half
    c_in = features.shape[-1]
    middle = w_reduce1.shape[1]
    group = middle // 4
    wide = w_expand1.shape[1]
    narrow = w_motion_in.shape[1]
    valid = (
        (jnp.arange(slots)[:, None] < clip_count[0])
        & (jnp.arange(frames)[None, :] < frame_count[:, None])
        & (frame_mask == 1)
    ).astype(F32)
    mask = valid[None, None, :, :, None]
    mask_rows = jnp.broadcast_to(valid.reshape(-1, 1), (slots * frames, 256))
    fmask = valid[:, :, None]
    widths = [middle, middle, wide, wide, middle, narrow, middle, group, group, group, wide]
    starts = [sum(widths[:k]) for k in range(len(widths))]
    gain = [gains[s : s + w] for s, w in zip(starts, widths)]
    bias = [biases[s : s + w] for s, w in zip(starts, widths)]

    feats = features.transpose(0, 2, 3, 1, 4).reshape(slots, -1, c_in)

    def gather(value):
        return lax.all_gather(value, AXES, axis=0, tiled=False)

    def rows_of(value):
        return jnp.pad(value, ((0, 0), (0, -value.shape[1] % middle))).reshape(
            value.shape[0], -1, middle
        )

    def columns_of(value):
        rows = value.shape[0]
        return value.reshape(rows, -1, middle).swapaxes(0, 1).reshape(-1, middle)

    own = middle // devices
    full_reduce1 = quick_gather(dp, fsdp, w_reduce1).reshape(c_in, middle)
    rows1, rowsp, rows2 = w_expand1.shape[0], w_project1.shape[0], w_reduce2.shape[0]
    blocks = wide // middle
    aligned = own % 16 == 0

    def gather_packed(*parts):
        value = gather(jnp.concatenate([part[0] for part in parts]))
        begin, flat, places = 0, [], []
        for part, rows, count in parts:
            places.append((rows * (1 if aligned else devices), begin // rows, count))
            mine = value[:, begin : begin + part.shape[0]]
            flat.append(mine.reshape(devices, -1, rows, middle).swapaxes(0, 1).reshape(-1, middle))
            begin += part.shape[0]
        array = value if aligned else jnp.concatenate(flat)[None]
        return [Packed(array, *place) for place in places]

    project1, expand1, reduce2, spatial1 = gather_packed(
        (columns_of(w_project1), rowsp, blocks),
        (columns_of(w_expand1), rows1, blocks),
        (w_reduce2, rows2, 1),
        (w_spatial1.reshape(-1, middle), own, 1),
    )
    taps1 = [Packed(spatial1.array, spatial1.rows, spatial1.first + t, 1) for t in range(9)]
    smalls = jnp.concatenate(
        [w_spatial2.reshape(1, -1), w_motion_in.reshape(1, -1), w_motion_out.reshape(1, -1)], axis=1
    )
    rowse = w_expand2.shape[0]
    late_rows = columns_of(w_expand2).shape[0]
    smalls = rows_of(smalls)[0]
    expand2, tail = gather_packed(
        (columns_of(w_expand2), rowse, blocks), (smalls, 1, smalls.shape[0])
    )
    if aligned:
        flat_small = tail.array[:, late_rows:].reshape(devices, -1)
    else:
        flat_small = (
            tail.array[0, late_rows * devices :]
            .reshape(-1, devices, middle)
            .swapaxes(0, 1)
            .reshape(devices, -1)
        )
    batch = slots * frames
    pixel_rows = (area, batch)
    size_s, size_m = w_spatial2.size, w_motion_in.size
    kernels = (
        flat_small[:, :size_s].reshape(devices, 27, -1).swapaxes(0, 1).reshape(3, 9, group, group)
    )
    small = flat_small[:, size_s : size_s + 2 * size_m].reshape(devices, 2, own, narrow)
    full_motion_in = small[:, 0].reshape(middle, narrow)
    full_motion_out = small[:, 1].reshape(middle, narrow).astype(F32)

    raw_a, off_a, sums_a = kernel_reduce1(feats, full_reduce1, mask_rows, height, frames)
    sum_a, square_a, frame_total, pairs = sums(
        jnp.sum(sums_a[0], axis=0),
        jnp.sum(sums_a[1], axis=0),
        jnp.sum(valid),
        jnp.sum(valid[:, :-1] * valid[:, 1:]),
    )
    count_big = frame_total * (height * height)
    count = frame_total * area
    mean_a, inv_a, alpha_a, beta_a = affine(
        sum_a, square_a, count_big, gain[0], bias[0], off_a[0]
    )
    act_a = kernel_act(raw_a, jnp.stack([alpha_a, beta_a]), mask_rows)
    raw_b, sums_b = kernel_conv_down(act_a, mask_rows, taps1)
    raw_b = raw_b.reshape(area, batch, middle)
    sampled = (
        features.reshape(slots, frames, half, 2, half, 2, c_in)[:, :, :, 0, :, 0]
        .transpose(2, 3, 0, 1, 4)
        .reshape(area, batch, c_in)
    )
    raw_p, off_p, sums_p = kernel_project(sampled, mask_rows, project1, half)

    def moments(raw):
        return total_over(raw * mask), total_over(raw * raw * mask)

    sum_b, square_b = sums.ready(sums_b, 2)
    mean_b, inv_b, alpha_b, beta_b = affine(sum_b, square_b, count, gain[1], bias[1])
    act_b, raw_c, off_c, sums_c = kernel_expand(
        raw_b, jnp.stack([alpha_b, beta_b]), mask_rows, expand1, half
    )
    sums_c, sums_p = jnp.sum(sums_c, axis=1), jnp.sum(sums_p, axis=1)
    sum_c, square_c, sum_p, square_p = sums(sums_c[0], sums_c[1], sums_p[0], sums_p[1])
    mean_c, inv_c, alpha_c, beta_c = affine(sum_c, square_c, count, gain[2], bias[2], off_c[0])
    mean_p, inv_p, alpha_p, beta_p = affine(sum_p, square_p, count, gain[3], bias[3], off_p[0])
    stats_one = jnp.stack(
        [alpha_c, alpha_p, beta_c + beta_p, mean_c, inv_c, mean_p, inv_p, jnp.zeros_like(mean_p)]
    )
    block_one, rows_d, sums_d = kernel_block_one(
        raw_c, raw_p, stats_one, mask_rows, reduce2, half
    )

    sum_d, square_d = sums.ready(sums_d, 2)
    mean_d, inv_d, alpha_d, beta_d = affine(sum_d, square_d, count, gain[4], bias[4])
    inside = [
        [
            [int(0 <= y - r + 1 < half and 0 <= x - c + 1 < half) for r in range(3) for c in range(3)]
            for x in range(half)
        ]
        for y in range(half)
    ]
    windows = jnp.array(inside, F32)
    act_d, raw_m, in_window, square_rows = kernel_motion(
        rows_d, jnp.stack([alpha_d, beta_d]), mask_rows, full_motion_in, inside, half
    )
    in_window = in_window.reshape(9, slots, frames, narrow)
    kmap = jnp.sum(windows[..., None] * motion_taps, axis=2)
    ksum = jnp.sum(kmap, axis=(0, 1))
    mapped = jnp.sum(in_window * motion_taps[:, None, None, :], axis=0)
    plain = in_window[4]
    vnext = later(fmask)
    pool_raw = (vnext / area) * (later(mapped * fmask) - fmask * plain)
    pool_one = (vnext / area) * (later(fmask) * ksum - fmask * area)
    flat_raw = pool_raw.reshape(-1, narrow)
    flat_valid = valid.reshape(-1, 1)
    gram = lax.dot_general(
        flat_raw * flat_valid, flat_raw, (((0,), (0,)), ((), ())), precision=HIGHEST
    )
    sum_m, square_m, pool_a, gram_aa = sums(
        total_over(plain * fmask),
        total_over(square_rows.reshape(plain.shape) * fmask),
        jnp.sum(flat_raw * flat_valid, axis=0), gram
    )
    mean_m, inv_m, alpha_m, beta_m = affine(sum_m, square_m, count, gain[5], bias[5])
    step = ksum / area - 1.0
    pool_b = pairs * step
    gram_ab = pool_a[:, None] * step[None, :]
    gram_bb = pairs * step[:, None] * step[None, :]
    pooled = alpha_m * pool_raw + beta_m * pool_one
    lifted = jnp.einsum("cfr,or->cfo", pooled, full_motion_out, precision=HIGHEST)
    gram_p = (
        alpha_m[:, None] * alpha_m * gram_aa
        + alpha_m[:, None] * beta_m * gram_ab
        + beta_m[:, None] * alpha_m * gram_ab.T
        + beta_m[:, None] * beta_m * gram_bb
    )
    sum_x = jnp.dot(full_motion_out, alpha_m * pool_a + beta_m * pool_b, precision=HIGHEST)
    square_x = jnp.sum(jnp.dot(full_motion_out, gram_p, precision=HIGHEST) * full_motion_out, axis=1)
    mean_x, inv_x, alpha_x, beta_x = affine(sum_x, square_x, frame_total, gain[6], bias[6])
    sigma = jax.nn.sigmoid(lifted * alpha_x + beta_x)
    attend1 = 2.0 * sigma
    attend_rows = attend1.reshape(batch, middle)
    tap_rows = [temporal_taps[k] for k in range(3)]
    excited, pad, raw, partial = kernel_group(
        act_d, attend_rows, tap_rows[0], kernels[0].reshape(-1, group), mask_rows, 1, half, frames
    )
    pads, raws, stats, outputs = [pad], [raw], [], []
    for k in range(3):
        stats.append(affine(*sums.ready(partial, 2), count, gain[7 + k], bias[7 + k]))
        if k < 2:
            out, pad, raw, partial = kernel_group(
                excited,
                (raws[k], jnp.stack(stats[k][2:])),
                tap_rows[k + 1],
                kernels[k + 1].reshape(-1, group),
                mask_rows,
                k + 2,
                half,
                frames,
            )
            pads.append(pad)
            raws.append(raw)
            outputs.append(out)
    joined, raw_e, off_e, sums_e = kernel_join(
        excited, outputs, raws[2], jnp.stack(stats[2][2:]), mask_rows, expand2, half
    )
    sums_e = jnp.sum(sums_e, axis=1)
    mean_e, inv_e, alpha_e, beta_e = affine(
        *sums(sums_e[0], sums_e[1]), count, gain[10], bias[10], off_e[0]
    )
    def by_owner(values, number):
        return (
            values.astype(BF)
            .reshape(dp, fsdp, -1, number, middle)
            .transpose(1, 0, 3, 2, 4)
            .reshape(fsdp, dp, -1, middle)
        )

    shifts = [None] * 11
    spreads = [None] * 11

    def grad_raw(index, grad, raw, mean, inv, weight, number):
        unit = (raw - mean) * inv
        return gain[index] * inv * (grad - weight * (shifts[index] + unit * spreads[index]) / number)

    result, grad_total, sums_e = kernel_result(
        raw_e,
        block_one,
        cotangent.transpose(0, 2, 3, 1, 4),
        jnp.stack([alpha_e, beta_e, mean_e]),
        mask_rows,
        half,
    )
    sums_e = jnp.sum(sums_e, axis=1)
    shifts[10], spreads[10] = sums(sums_e[0], sums_e[1] * inv_e)

    def back_stats(index, mean, inv):
        scale = gain[index] * inv
        return [scale, mean, scale * shifts[index] / count, scale * inv * spreads[index] / count]

    def lower(k):
        return raws[k], jnp.stack([stats[k][2], stats[k][3], stats[k][0]])

    flipped = [kernels[k][::-1].transpose(0, 2, 1).reshape(9 * group, group) for k in range(3)]
    final_grad, grad_joined, grad_pre, partial = kernel_final_back(
        grad_total,
        raw_e,
        jnp.stack(back_stats(10, mean_e, inv_e)),
        mask_rows,
        expand2,
        *lower(2),
        half,
    )
    kernel_grads = [None] * 3
    temporal_grads = [None] * 3
    grad_pieces = [None] * 3
    for k in (2, 1, 0):
        mean, inv, alpha, _ = stats[k]
        shifts[7 + k], spreads[7 + k] = sums.ready(partial, 2)
        spreads[7 + k] = spreads[7 + k] * inv
        got = kernel_group_back(
            grad_pre,
            raws[k],
            jnp.stack(
                [alpha, mean, alpha * shifts[7 + k] / count, alpha * inv * spreads[7 + k] / count]
            ),
            flipped[k],
            tap_rows[k],
            excited,
            outputs[k - 1] if k else (grad_pieces[1], grad_pieces[2], act_d),
            grad_joined,
            lower(k - 1) if k else None,
            mask_rows,
            k + 1,
            half,
            frames,
        )
        group_grad, grad_pieces[k], sums_t = got[:3]
        if k:
            grad_pre, partial = got[3:]
        else:
            grad_attend = got[3].reshape(slots, frames, middle)
        temporal_grads[k] = jnp.sum(sums_t, axis=1)
        kernel_grads[k] = kernel_group_weights(pads[k], group_grad, half)
    grad_kernels = rows_of(
        jnp.stack(kernel_grads).reshape(27, devices, -1).swapaxes(0, 1).astype(BF).reshape(devices, -1)
    )
    total_a = blocks * rowse + grad_kernels.shape[1]
    total_a += -total_a % 16
    if aligned:
        packed_a = kernel_weight_grad(joined, final_grad, dp, fsdp, rowse, 0, blocks * rowse)
        rest = grad_kernels.reshape(dp, fsdp, -1, middle).swapaxes(0, 1)
        rest = jnp.pad(rest, ((0, 0), (0, 0), (0, -rest.shape[2] % 16), (0, 0)))
        packed_a = jnp.concatenate([packed_a, rest], axis=2)
    else:
        packed_a = jnp.concatenate(
            [
                by_owner(weight_grad(joined, final_grad), blocks),
                grad_kernels.reshape(dp, fsdp, -1, middle).swapaxes(0, 1),
            ],
            axis=2,
        )
        packed_a = jnp.pad(
            packed_a, ((0, 0), (0, 0), (0, total_a - packed_a.shape[2]), (0, 0))
        )
    grad_x = grad_attend * 2.0 * sigma * (1.0 - sigma)
    unit_x = (lifted - mean_x) * inv_x
    pool_unit = (pool_raw - mean_m * pool_one) * inv_m
    grad_e = jnp.einsum("cfo,or->cfr", grad_x, full_motion_out * alpha_x[:, None], precision=HIGHEST)
    shifts[6], spreads[6], first_t, second_t = sums(
        jnp.sum(grad_x, axis=(0, 1)),
        jnp.sum(grad_x * unit_x, axis=(0, 1)),
        jnp.sum(grad_e * pool_one, axis=(0, 1)),
        jnp.sum(grad_e * pool_unit, axis=(0, 1)),
    )
    shifts[6], packed_a = lax.optimization_barrier((shifts[6], packed_a))
    mine_a = lax.psum_scatter(
        packed_a.reshape(-1, middle), "fsdp", scatter_dimension=0, tiled=True
    )
    lift_b = jnp.dot(
        full_motion_out, alpha_m[:, None] * gram_ab + beta_m[:, None] * gram_bb, precision=HIGHEST
    )
    lift_a = jnp.dot(
        full_motion_out, alpha_m[:, None] * gram_aa + beta_m[:, None] * gram_ab.T, precision=HIGHEST
    )
    unit_b = inv_x[:, None] * (lift_b - mean_x[:, None] * pool_b)
    unit_a = inv_x[:, None] * (lift_a - mean_x[:, None] * pool_a)
    unit_u = (unit_a - unit_b * mean_m) * inv_m
    pool_u = (pool_a - pool_b * mean_m) * inv_m
    back_x = full_motion_out * alpha_x[:, None]
    shifts[5] = first_t - jnp.sum(
        back_x * (shifts[6][:, None] * pool_b + spreads[6][:, None] * unit_b), axis=0
    ) / frame_total
    spreads[5] = second_t - jnp.sum(
        back_x * (shifts[6][:, None] * pool_u + spreads[6][:, None] * unit_u), axis=0
    ) / frame_total
    grad_lifted = alpha_x * (grad_x - fmask * (shifts[6] + unit_x * spreads[6]) / frame_total)
    grad_motion_out = jnp.einsum("cfo,cfr->or", grad_lifted, pooled, precision=HIGHEST)
    grad_pooled = jnp.einsum("cfo,or->cfr", grad_lifted, full_motion_out, precision=HIGHEST)
    grad_change = grad_pooled * vnext / area
    reduced_windows = later(
        fmask * (alpha_m * in_window + beta_m * jnp.sum(windows, axis=(0, 1))[:, None, None, None])
    )
    motion_tap_grad = jnp.sum(grad_change * reduced_windows, axis=(1, 2))
    grad_narrow, motion_grad, sums_narrow = kernel_motion_back(
        grad_joined,
        grad_pieces,
        attend_rows,
        rows_d,
        jnp.stack([alpha_d, beta_d, mean_d]),
        raw_m,
        kmap.reshape(area, 1, narrow),
        jnp.stack([earlier(grad_change), grad_change]).reshape(2, batch, narrow),
        jnp.stack(
            [alpha_m, mean_m, alpha_m * shifts[5] / count, alpha_m * inv_m * spreads[5] / count]
        ),
        full_motion_in,
        mask_rows,
        half,
    )
    grad_motion_in = weight_grad(act_d, motion_grad)
    shifts[4], spreads[4] = sums.ready(sums_narrow, 2)
    spreads[4] = spreads[4] * inv_d
    small_grads = jnp.concatenate(
        [grad_motion_in.reshape(devices, -1), grad_motion_out.reshape(devices, -1)], axis=1
    )
    narrow_grad, grad_one, sums_one = kernel_block_back(
        grad_narrow,
        rows_d,
        jnp.stack(back_stats(4, mean_d, inv_d)),
        reduce2,
        grad_total,
        raw_c,
        raw_p,
        stats_one,
        mask_rows,
        half,
    )
    sums_one, mine_a = lax.optimization_barrier((sums_one, mine_a))
    mine_a = lax.psum_scatter(mine_a, "dp", scatter_dimension=0, tiled=True)
    sums_one = jnp.sum(sums_one, axis=1)
    shifts[2], spreads[2], spreads[3], motion_total, temporal_total = sums(
        sums_one[0],
        sums_one[1] * inv_c,
        sums_one[2] * inv_p,
        motion_tap_grad,
        jnp.stack(temporal_grads),
    )
    shifts[3] = shifts[2]
    stats_two = jnp.stack(back_stats(2, mean_c, inv_c) + back_stats(3, mean_p, inv_p))
    total = blocks * (rowsp + rows1)
    if aligned:
        packed_r = kernel_weight_grad(block_one, narrow_grad, dp, fsdp, rows2, 0, rows2)
    else:
        packed_r = by_owner(weight_grad(block_one, narrow_grad), 1)
    stats_two, packed_r = lax.optimization_barrier((stats_two, packed_r))
    mine_r = lax.psum_scatter(
        packed_r.reshape(-1, middle), "fsdp", scatter_dimension=0, tiled=True
    )
    widen_grad, shortcut_grad, grad_strided, sums_strided = kernel_expand_back(
        grad_one,
        raw_c,
        raw_p,
        stats_two,
        expand1,
        raw_b,
        jnp.stack([alpha_b, beta_b, mean_b, inv_b]),
        mask_rows,
        half,
    )
    if aligned:
        packed_b = kernel_weight_grad(
            act_b, widen_grad, dp, fsdp, rows1, blocks * rowsp // rows1, total
        )
        packed_b = kernel_weight_grad(
            sampled, shortcut_grad, dp, fsdp, rowsp, 0, total, packed_b
        )
    else:
        packed_b = jnp.concatenate(
            [
                by_owner(weight_grad(sampled, shortcut_grad), blocks),
                by_owner(weight_grad(act_b, widen_grad), blocks),
            ],
            axis=2,
        )
    shifts[1], spreads[1] = sums.ready(sums_strided, 2)
    shifts[1], spreads[1], packed_b, mine_a, mine_r = lax.optimization_barrier(
        (shifts[1], spreads[1], packed_b, mine_a, mine_r)
    )

    def columns_back(value, rows):
        return value.reshape(blocks, rows, middle).swapaxes(0, 1).reshape(rows, wide)

    mine_a = mine_a.astype(F32)
    own_expand2 = columns_back(mine_a[: blocks * rowse], rowse)
    own_kernels = mine_a[blocks * rowse :].reshape(-1)[:size_s]
    mine_b = packed_b.reshape(-1, middle)
    mine_b = lax.psum_scatter(mine_b, "fsdp", scatter_dimension=0, tiled=True)
    strided_grad = grad_raw(
        1, grad_strided, raw_b, mean_b, inv_b, mask_rows[:, :1], count
    ).astype(BF)
    strided_grad = strided_grad.reshape(half, half, batch, middle)
    sum_c1 = scatter_cores(dp, fsdp, kernel_conv_down_weights(act_a, strided_grad, dp, fsdp))
    strided_grad, sum_c1 = lax.optimization_barrier((strided_grad, sum_c1))
    sum_c = scatter_halves(dp, sum_c1.reshape((2, -1) + sum_c1.shape[1:]), 0)
    grad_first, sums_first = kernel_conv_down_back(
        strided_grad,
        taps1,
        raw_a,
        jnp.stack([alpha_a, beta_a, mean_a, inv_a]),
        mask_rows,
    )
    shifts[0], spreads[0] = sums.ready(sums_first, 2)
    stats_first = jnp.stack(
        [
            alpha_a,
            mean_a,
            alpha_a * shifts[0] / count_big,
            alpha_a * inv_a * spreads[0] / count_big,
        ]
    )
    stats_first, sum_c, mine_b = lax.optimization_barrier((stats_first, sum_c, mine_b))
    mine_b = jnp.concatenate([mine_b.reshape(dp, -1, middle), mine_r.reshape(dp, -1, middle)], axis=1)
    mine_b = mine_b.reshape(-1, middle)
    mine_b = lax.psum_scatter(mine_b, "dp", scatter_dimension=0, tiled=True).astype(F32)
    cut1 = blocks * rowsp
    cut2 = cut1 + blocks * rows1
    own_project1 = columns_back(mine_b[:cut1], rowsp)
    own_expand1 = columns_back(mine_b[cut1:cut2], rows1)
    own_reduce2 = mine_b[cut2:]
    for bit in range(1, dp.bit_length() - 1):
        sum_c = scatter_halves(dp, sum_c.reshape((2, -1) + sum_c.shape[1:]), bit)
    sum_c = sum_c.reshape(fsdp // 2, -1, middle)
    first_grad, grad_reduce1 = kernel_first_grad(
        grad_first, raw_a, feats, stats_first, mask_rows, frames
    )
    grad_reduce1, sum_c = lax.optimization_barrier((grad_reduce1, sum_c))
    sum_d = jnp.concatenate(
        [grad_reduce1.reshape(devices, -1, middle), rows_of(small_grads.astype(BF))], axis=1
    )
    rows_d = sum_d.shape[1]
    sum_d = sum_d.reshape((dp, fsdp // 2, 2) + sum_d.shape[1:]).transpose(2, 1, 0, 3, 4)
    sum_d = scatter_cores(dp, fsdp, sum_d).reshape(fsdp // 2, -1, middle)
    both = scatter_fsdp(fsdp, jnp.concatenate([sum_d, sum_c], axis=1))
    own_spatial1 = both[dp * rows_d :]
    sum_d = scatter_dp(both[: dp * rows_d].astype(BF).reshape(dp, rows_d, middle))
    rows_first = c_in // devices
    own_reduce1 = sum_d[:rows_first]
    own_motion = sum_d[rows_first:].reshape(-1)[: 2 * size_m].reshape(2, own, narrow)
    grad_features = None
    for pair in range(slots // 2):
        grad_features = kernel_grad_features(
            first_grad, full_reduce1, shortcut_grad, project1, height, frames, pair, grad_features
        )
    grad_features = grad_features.reshape(slots, height, height, frames, c_in)
    return (
        result.transpose(0, 3, 1, 2, 4),
        grad_features.transpose(0, 3, 1, 2, 4),
        own_reduce1,
        own_spatial1.reshape(9, own * middle),
        own_expand1,
        own_project1,
        own_reduce2,
        own_motion[0],
        own_motion[1],
        own_kernels.reshape(27, -1),
        own_expand2,
        jnp.concatenate(spreads),
        jnp.concatenate(shifts),
        motion_total,
        temporal_total,
    )


def solution(mesh):
    dp, fsdp = mesh.shape["dp"], mesh.shape["fsdp"]

    def run(*arrays):
        return local(dp, fsdp, *arrays)

    rows = P(AXES, None)
    columns = P(None, AXES)
    clips = P(AXES, None, None, None, None)
    return jax.shard_map(
        run,
        mesh=mesh,
        in_specs=(
            P(AXES),
            P(AXES),
            rows,
            clips,
            rows,
            columns,
            rows,
            rows,
            rows,
            rows,
            rows,
            columns,
            rows,
            P(),
            P(),
            P(),
            P(),
            clips,
        ),
        out_specs=(
            clips,
            clips,
            rows,
            columns,
            rows,
            rows,
            rows,
            rows,
            rows,
            columns,
            rows,
            P(),
            P(),
            P(),
            P(),
        ),
        check_vma=False,
    )
```

```python
import jax
import jax.numpy as jnp
from jax import lax
from jax.experimental import pallas as pl
from jax.experimental.pallas import tpu as pltpu
from jax.sharding import PartitionSpec as P

EPSILON = 1e-05
HIGHEST = lax.Precision.HIGHEST
AXES = ("dp", "fsdp")
BF = jnp.bfloat16
F32 = jnp.float32


def by_clip(values, frames):
    return values.reshape(values.shape[:-2] + (-1, frames, values.shape[-1]))


def earlier(values):
    return jnp.concatenate([jnp.zeros_like(values[..., :1, :]), values[..., :-1, :]], axis=-2)


def later(values):
    return jnp.concatenate([values[..., 1:, :], jnp.zeros_like(values[..., :1, :])], axis=-2)


def taps_of(values, size):
    padded = jnp.pad(values, ((1, 1), (1, 1), (0, 0), (0, 0), (0, 0)))
    return [padded[r : r + size, c : c + size] for r in range(3) for c in range(3)]


def dot(left, weight):
    shape = left.shape
    flat = jnp.dot(left.reshape(-1, shape[-1]), weight, preferred_element_type=F32)
    return flat.reshape(shape[:-1] + (weight.shape[1],))


def dot_t(grad, weight):
    shape = grad.shape
    flat = lax.dot_general(
        grad.reshape(-1, shape[-1]), weight, (((1,), (1,)), ((), ())), preferred_element_type=F32
    )
    return flat.reshape(shape[:-1] + (weight.shape[0],))


def weight_grad(left, grad):
    return lax.dot_general(
        left.reshape(-1, left.shape[-1]),
        grad.reshape(-1, grad.shape[-1]),
        (((0,), (0,)), ((), ())),
        preferred_element_type=F32,
    )


def silu_slope(values):
    sig = jax.nn.sigmoid(values)
    return sig * (1.0 + values * (1.0 - sig))


def total_over(values):
    return jnp.sum(values, axis=tuple(range(values.ndim - 1)))


def silu_parts(norm):
    sig = 0.5 * jnp.tanh(0.5 * norm) + 0.5
    return sig, norm * sig


def call(body, grid, ins, in_blocks, outs, out_blocks, scratch=(), limit=56, flops=0, moved=0):
    def spec(block):
        if block is None:
            return pl.BlockSpec(memory_space=pltpu.VMEM)
        return pl.BlockSpec(block[0], block[1])

    return pl.pallas_call(
        body,
        grid=grid,
        in_specs=[spec(b) for b in in_blocks],
        out_specs=[spec(b) for b in out_blocks],
        out_shape=[jax.ShapeDtypeStruct(s, d) for s, d in outs],
        scratch_shapes=list(scratch),
        compiler_params=pltpu.CompilerParams(
            vmem_limit_bytes=limit * 1024 * 1024,
            dimension_semantics=("arbitrary",) * len(grid),
        ),
        cost_estimate=pl.CostEstimate(flops=flops, bytes_accessed=moved, transcendentals=0),
    )(*ins)


def whole(shape):
    return shape, lambda *_: (0,) * len(shape)


def mean_of(raw, weight):
    return jnp.sum(raw * weight, axis=0, keepdims=True) / jnp.maximum(jnp.sum(weight), 1.0)


def kernel_reduce1(feats, weight, mask, height, frames):
    c_in, middle = weight.shape
    slots = feats.shape[0]
    half = height // 2
    rows = 2 * height * frames

    def body(x_ref, w_ref, m_ref, raw_ref, off_ref, sum_ref):
        first = (pl.program_id(0) == 0) & (pl.program_id(1) == 0)

        @pl.when(first)
        def _():
            sum_ref[...] = jnp.zeros_like(sum_ref)
            few = nn(x_ref[0, : height * frames], w_ref[...]).reshape(height, frames, middle)
            off_ref[0:1] = mean_of(jnp.sum(few, axis=0) * (1.0 / height), m_ref[:frames, :1])

        left = x_ref[...].reshape(2 * rows, c_in)
        m = m_ref[:, :1].reshape(2, 1, 1, frames, 1)
        for c in chunks(middle):
            raw = nn(left, w_ref[:, c]).reshape(2, 2, height, frames, -1)
            offset = off_ref[0:1, c]
            sum_ref[0, :, c] += jnp.sum(jnp.sum(raw, axis=(1, 2)) * m[:, 0, 0], axis=0)
            sum_ref[1, :, c] += jnp.sum(jnp.sum(raw * raw, axis=(1, 2)) * m[:, 0, 0], axis=0)
            low = raw - offset
            raw_ref[:, :, :, c] = jnp.concatenate([low[0], low[1]], axis=2).astype(BF)

    return call(
        body,
        (slots // 2, half),
        (feats, weight, mask),
        (
            ((2, rows, c_in), lambda c, h: (c, h, 0)),
            whole(weight.shape),
            ((2 * frames, mask.shape[1]), lambda c, h: (c, 0)),
        ),
        (
            ((height, height, slots * frames, middle), BF),
            ((8, middle), F32),
            ((2, frames, middle), F32),
        ),
        (
            ((2, height, 2 * frames, middle), lambda c, h: (h, 0, c, 0)),
            whole((8, middle)),
            whole((2, frames, middle)),
        ),
        flops=2 * feats.size * middle,
        moved=feats.size * 2 + feats.size // c_in * middle * 2,
    )


def exchange_shape(width):
    return (lax.psum(1, AXES), 1, width)


def send_sums(send_ref, sum_ref, last=True):
    def send():
        rows = [jnp.sum(sum_ref[n], axis=0, keepdims=True) for n in range(sum_ref.shape[0])]
        row = jnp.concatenate(rows, axis=1)
        send_ref[...] = jnp.broadcast_to(row[None], send_ref.shape)

    if last is True:
        send()
    else:
        pl.when(last)(send)


def kernel_act(raw_a, stats, mask):
    height, _, batch, middle = raw_a.shape
    block = (2, height, batch, middle), lambda i: (i, 0, 0, 0)

    def body(a_ref, s_ref, m_ref, act_ref):
        m = m_ref[...]
        for c in chunks(middle):
            al, be = s_ref[0:1, c], s_ref[1:2, c]
            for p in range(2):
                for j in range(height):
                    act_ref[p, j, :, c] = (silu_parts(a_ref[p, j, :, c].astype(F32) * al + be)[1] * m).astype(BF)

    return call(
        body,
        (height // 2,),
        (raw_a, stats, mask),
        (block, whole(stats.shape), whole(mask.shape)),
        ((raw_a.shape, BF),),
        (block,),
        flops=10 * raw_a.size,
        moved=raw_a.size * 6,
    )[0]


def kernel_conv_down(act_a, mask, taps):
    height, _, batch, middle = act_a.shape
    half = height // 2
    rows = half * batch

    def body(a_ref, m_ref, *refs):
        w_refs, (raw_ref, send_ref, cols, w_ref, sum_ref) = refs[:9], refs[9:]
        step = pl.program_id(0)
        wide = 3 * middle

        @pl.when(step == 0)
        def _():
            sum_ref[...] = jnp.zeros_like(sum_ref)
            cols[...] = jnp.zeros_like(cols)
            for t in range(9):
                w_ref[t * middle : (t + 1) * middle] = taps[t].of(w_refs[t], 0)

        @pl.when(step > 0)
        def _():
            cols[:, :wide] = cols[:, 2 * wide :]

        m = m_ref[:, :1]
        for p in range(2):
            base = (1 + p) * wide
            for j in range(half):
                for q in range(2):
                    act = a_ref[p, 2 * j + q]
                    lane = base + (1 + q) * middle
                    cols[j * batch : (j + 1) * batch, lane : lane + middle] = act
                    if q == 1 and j + 1 < half:
                        cols[(j + 1) * batch : (j + 2) * batch, base : base + middle] = act
        raw = jnp.dot(cols[...], w_ref[...], preferred_element_type=F32)
        raw = raw.reshape(half, batch, middle)
        raw_ref[0] = raw
        sum_ref[0] += jnp.sum(raw, axis=0) * m
        sum_ref[1] += jnp.sum(raw * raw, axis=0) * m
        send_sums(send_ref, sum_ref, step == half - 1)

    return call(
        body,
        (half,),
        (act_a, mask) + tuple(t.array for t in taps),
        (((2, height, batch, middle), lambda i: (i, 0, 0, 0)), whole(mask.shape))
        + tuple(t.block() for t in taps),
        (
            ((half, half, batch, middle), F32),
            (exchange_shape(2 * middle), F32),
        ),
        (
            ((1, half, batch, middle), lambda i: (i, 0, 0, 0)),
            whole(exchange_shape(2 * middle)),
        ),
        scratch=[pltpu.VMEM((rows, 9 * middle), BF), pltpu.VMEM((9 * middle, middle), BF), pltpu.VMEM((2, batch, middle), F32)],
        flops=2 * half * rows * 9 * middle * middle,
        moved=act_a.size * 2 + 18 * middle * middle,
    )


def kernel_conv_down_weights(act_a, grad, raw_b, stats, mask, dp, fsdp):
    height, _, batch, middle = act_a.shape
    half = height // 2
    split = act_a.reshape(half, 2, half, 2, batch, middle)
    own = middle // (dp * fsdp)
    aligned = own % 16 == 0

    def body(a_ref, n_ref, b_ref, s_ref, m_ref, out_ref, g_ref, cols):
        step = pl.program_id(0)

        @pl.when(step == 0)
        def _():
            for c in chunks(middle):
                scale, mean, shift, spread = (s_ref[n : n + 1, c] for n in range(4))
                m = m_ref[:, : c.stop - c.start]

                @pl.loop(0, half)
                def _(i):
                    for j in range(half):
                        p = i * half + j
                        value = scale * n_ref[p, :, c] - m * (shift + (b_ref[p, :, c] - mean) * spread)
                        g_ref[p, :, c] = value.astype(BF)

        for r in range(3):
            for c in range(3):
                top, left = int(r == 0), int(c == 0)

                @pl.when(step == r * 3 + c)
                def _(r=r, c=c, top=top, left=left):
                    if top:
                        cols[0] = jnp.zeros_like(cols[0])
                    if left:
                        cols[:, 0] = jnp.zeros_like(cols[:, 0])
                    cols[top:, left:] = a_ref[
                        : half - top, int(r != 1), : half - left, int(c != 1)
                    ]

        value = tn(cols[...].reshape(half * half * batch, middle), g_ref[...].reshape(-1, middle)).astype(BF)
        if not aligned:
            out_ref[0] = value
            return
        value = value.reshape(dp, fsdp // 2, 2, own, middle)
        for place, d in enumerate(by_low_bit(dp)):
            for f in range(fsdp // 2):
                for core in range(2):
                    out_ref[core, place, f] = value[d, f, core]

    if aligned:
        out = ((2, dp, fsdp // 2, 9 * own, middle), BF)
        out_block = (2, dp, fsdp // 2, own, middle), lambda t: (0, 0, 0, t, 0)
    else:
        out = ((9, middle, middle), BF)
        out_block = (1, middle, middle), lambda t: (t, 0, 0)
    value, strided_grad = call(
        body,
        (9,),
        (split, grad, raw_b, stats, mask),
        (whole(split.shape), whole(grad.shape), whole(raw_b.shape), whole(stats.shape), whole(mask.shape)),
        (out, (grad.shape, BF)),
        (out_block, whole(grad.shape)),
        scratch=[pltpu.VMEM((half, half, batch, middle), BF)],
        flops=2 * half * half * batch * 9 * middle * middle,
        moved=act_a.size * 2 + grad.size * 10 + 18 * middle * middle,
    )
    if not aligned:
        value = value.reshape(9, dp, fsdp // 2, 2, own, middle).transpose(3, 1, 2, 0, 4, 5)
        value = value.reshape(2, dp, fsdp // 2, 9 * own, middle)[:, jnp.array(by_low_bit(dp))]
    return value, strided_grad


def kernel_conv_down_back(grad, taps, raw_a, stats, mask):
    height, _, batch, middle = raw_a.shape
    half = height // 2
    rows = half * batch

    def body(g_ref, n_ref, a_ref, s_ref, m_ref, *refs):
        w_refs, (out_ref, send_ref, here, below, sum_ref) = refs[:9], refs[9:]
        step = pl.program_id(0)

        @pl.when(step == 0)
        def _():
            sum_ref[...] = jnp.zeros_like(sum_ref)
            here[half] = jnp.zeros_like(here[half])
            below[half] = jnp.zeros_like(below[half])

        here[:half] = g_ref[0]

        @pl.when(step < half - 1)
        def _():
            below[:half] = n_ref[0]

        @pl.when(step == half - 1)
        def _():
            below[:half] = jnp.zeros_like(n_ref[0])

        def tap(ref, right, t):
            return lax.dot_general(
                ref[right : right + half].reshape(rows, middle),
                taps[t].of(w_refs[t], 0),
                (((1,), (1,)), ((), ())),
                preferred_element_type=F32,
            )

        al, be = s_ref[0:1], s_ref[1:2]
        mean, inv = s_ref[2:3], s_ref[3:4]
        m = m_ref[:, :1]
        plans = (
            (0, 0, ((here, 0, 4),)),
            (0, 1, ((here, 0, 5), (here, 1, 3))),
            (1, 0, ((here, 0, 7), (below, 0, 1))),
            (1, 1, ((here, 0, 8), (here, 1, 6), (below, 0, 2), (below, 1, 0))),
        )
        for p, q, parts in plans:
            back = tap(*parts[0])
            for part in parts[1:]:
                back = back + tap(*part)
            raw = a_ref[0, p, :, q].astype(F32)
            norm = raw * al + be
            sig, act = silu_parts(norm)
            slope = sig + act * (1.0 - sig)
            out = back.reshape(half, batch, middle) * slope * m
            out_ref[0, p, :, q] = out.astype(BF)
            sum_ref[0] += jnp.sum(out, axis=0)
            sum_ref[1] += jnp.sum(out * ((raw - mean) * inv), axis=0)
        send_sums(send_ref, sum_ref, step == half - 1)

    return call(
        body,
        (half,),
        (grad, grad, raw_a.reshape(half, 2, half, 2, batch, middle), stats, mask)
        + tuple(t.array for t in taps),
        (
            ((1, half, batch, middle), lambda i: (i, 0, 0, 0)),
            ((1, half, batch, middle), lambda i: (jnp.minimum(i + 1, half - 1), 0, 0, 0)),
            ((1, 2, half, 2, batch, middle), lambda i: (i, 0, 0, 0, 0, 0)),
            whole(stats.shape),
            whole(mask.shape),
        )
        + tuple(t.block() for t in taps),
        (
            ((half, 2, half, 2, batch, middle), BF),
            (exchange_shape(2 * middle), F32),
        ),
        (
            ((1, 2, half, 2, batch, middle), lambda i: (i, 0, 0, 0, 0, 0)),
            whole(exchange_shape(2 * middle)),
        ),
        scratch=[
            pltpu.VMEM((half + 1, batch, middle), BF),
            pltpu.VMEM((half + 1, batch, middle), BF),
            pltpu.VMEM((2, batch, middle), F32),
        ],
        flops=2 * half * rows * 9 * middle * middle,
        moved=raw_a.size * 8 + 18 * middle * middle,
    )


def kernel_first_grad(grad, raw_a, feats, stats, mask, frames):
    height, _, batch, middle = raw_a.shape
    half = height // 2
    rows = half * height * frames
    line = height * frames
    slots, _, c_in = feats.shape

    def body(g_ref, a_ref, x_ref, s_ref, m_ref, out_ref, w_ref, acc):
        first = (pl.program_id(0) == 0) & (pl.program_id(1) == 0)
        last = (pl.program_id(0) == slots // 2 - 1) & (pl.program_id(1) == 1)

        @pl.when(first)
        def _():
            acc[...] = jnp.zeros_like(acc)

        m = m_ref[...]
        for c in chunks(middle):
            scale, mean, shift, spread = (s_ref[n : n + 1, c] for n in range(4))
            for r in range(half):
                raw = a_ref[r, :, :, c].astype(F32)
                value = scale * g_ref[r, :, :, c].astype(F32) - m * (shift + (raw - mean) * spread)
                for clip in range(2):
                    part = value[:, clip * frames : (clip + 1) * frames]
                    out_ref[clip, r * line : (r + 1) * line, c] = part.reshape(line, -1).astype(BF)
        for clip in range(2):
            acc[...] += tn(x_ref[clip], out_ref[clip])

        @pl.when(last)
        def _():
            w_ref[...] = acc[...].astype(BF)

    block = (half, height, 2 * frames, middle), lambda c, h: (h, 0, c, 0)
    return call(
        body,
        (slots // 2, 2),
        (grad.reshape(raw_a.shape), raw_a, feats, stats, mask),
        (
            block,
            block,
            ((2, rows, c_in), lambda c, h: (c, h, 0)),
            whole(stats.shape),
            ((2 * frames, mask.shape[1]), lambda c, h: (c, 0)),
        ),
        (
            ((slots, 2 * rows, middle), BF),
            ((c_in, middle), BF),
        ),
        (
            ((2, rows, middle), lambda c, h: (c, h, 0)),
            whole((c_in, middle)),
        ),
        scratch=[pltpu.VMEM((c_in, middle), F32)],
        flops=2 * raw_a.size * c_in,
        moved=raw_a.size * 6 + feats.size * 2,
    )


def kernel_grad_features(grad, weight, shortcut, project, height, frames, pair, into=None):
    c_in, middle = weight.shape
    slots, all_rows, _ = grad.shape
    half = height // 2
    pixels, batch, wide = shortcut.shape
    size = 256
    parts = c_in // size

    def body(g_ref, w_ref, s_ref, p_ref, *refs):
        out_ref = refs[-1]
        even = None
        for k in range(project.count):
            left = s_ref[:, :, k * middle : (k + 1) * middle].reshape(pixels * 2 * frames, middle)
            part = nt(left, project.of(p_ref, k))
            even = part if even is None else even + part
        even = even.reshape(half, half, 2, frames, size)
        for clip in range(2):
            value = nt(g_ref[clip], w_ref[...]).reshape(half, 2, half, 2, frames, size)
            both = jnp.stack([value[:, 0, :, 0] + even[:, :, clip], value[:, 0, :, 1]], axis=2)
            line = jnp.stack([both, value[:, 1]], axis=1)
            out_ref[clip] = line.reshape(all_rows, size).astype(BF)

    groups, _, _ = project.array.shape
    if groups == 1:
        size_rows = project.rows // parts
        project_block = pl.BlockSpec((1, project.count * project.rows, middle), lambda n: (0, 0, 0))
    else:
        project_block = pl.BlockSpec(
            (groups // parts, project.count * project.rows, middle), lambda n: (n, 0, 0)
        )
    if groups == 1:

        def of(ref, k):
            begin = k * project.rows + pl.program_id(0) * size_rows
            return ref[0, pl.ds(pl.multiple_of(begin, size_rows), size_rows), :]

        project.of = of
    ins = (grad, weight, shortcut, project.array)
    in_specs = [
        pl.BlockSpec((2, all_rows, middle), lambda n: (pair, 0, 0)),
        pl.BlockSpec((size, middle), lambda n: (n, 0)),
        pl.BlockSpec((pixels, 2 * frames, wide), lambda n: (0, pair, 0)),
        project_block,
    ]
    alias = {}
    if into is not None:
        ins += (into,)
        in_specs.append(pl.BlockSpec(memory_space=pl.ANY))
        alias = {4: 0}
    return pl.pallas_call(
        body,
        grid=(parts,),
        in_specs=in_specs,
        out_specs=pl.BlockSpec((2, all_rows, size), lambda n: (pair, 0, n)),
        out_shape=jax.ShapeDtypeStruct((slots, all_rows, c_in), BF),
        input_output_aliases=alias,
        compiler_params=pltpu.CompilerParams(
            vmem_limit_bytes=56 * 1024 * 1024, dimension_semantics=("arbitrary",)
        ),
        cost_estimate=pl.CostEstimate(
            flops=(grad.size + shortcut.size) * c_in,
            bytes_accessed=grad.size + shortcut.size + slots * all_rows * c_in,
            transcendentals=0,
        ),
    )(*ins)


CHUNK = 256


def fold(value):
    return jnp.sum(value.reshape(-1, 8, value.shape[-1]), axis=0)


def chunks(width):
    return [slice(b, min(b + CHUNK, width)) for b in range(0, width, CHUNK)]


def zero_first(*refs):
    @pl.when(pl.program_id(0) == 0)
    def _():
        for ref in refs:
            ref[...] = jnp.zeros_like(ref)


def row_block(half, batch, width):
    return (half, batch, width), lambda i: (i, 0, 0)


class Packed:
    def __init__(self, array, rows, first, count):
        self.array, self.rows, self.first, self.count = array, rows, first, count

    def block(self):
        size, index = self.rows * self.count, self.first // self.count
        return (self.array.shape[0], size, self.array.shape[2]), lambda *_: (0, index, 0)

    def part(self, ref, k, size):
        if self.array.shape[0] == 1:
            return ref[0, k * size : (k + 1) * size, :]
        parts = size // self.rows
        return ref[k * parts : (k + 1) * parts].reshape(size, -1)

    def of(self, ref, k):
        part = ref[:, k * self.rows : (k + 1) * self.rows, :]
        return part.reshape(-1, part.shape[-1])


def nt(left, right):
    return lax.dot_general(left, right, (((1,), (1,)), ((), ())), preferred_element_type=F32)


def tn(left, right):
    return lax.dot_general(left, right, (((0,), (0,)), ((), ())), preferred_element_type=F32)


def nn(left, right):
    return jnp.dot(left, right, preferred_element_type=F32)


def kernel_expand(raw_b, stats, mask, weight, half):
    _, batch, middle = raw_b.shape
    wide = weight.count * middle
    rows = half * batch

    def body(b_ref, s_ref, m_ref, w_ref, act_ref, raw_ref, off_ref, sum_ref):
        zero_first(sum_ref)
        m = m_ref[...]

        for c in chunks(middle):
            al, be = s_ref[0:1, c], s_ref[1:2, c]
            for j in range(half):
                act_ref[j, :, c] = (silu_parts(b_ref[j, :, c] * al + be)[1] * m).astype(BF)


        @pl.when(pl.program_id(0) == 0)
        def _():
            for k in range(weight.count):
                few = nn(act_ref[half // 2], weight.of(w_ref, k))
                off_ref[0:1, k * middle : (k + 1) * middle] = mean_of(few, m_ref[:, :1])

        m = m_ref[:, :1]
        act = act_ref[...].reshape(rows, middle)
        for k in range(weight.count):
            raw = nn(act, weight.of(w_ref, k)).reshape(half, batch, middle)
            span = slice(k * middle, (k + 1) * middle)
            offset = off_ref[0:1, span]
            raw_ref[:, :, span] = (raw - offset).astype(BF)
            sum_ref[0, :, span] += fold(jnp.sum(raw, axis=0) * m)
            sum_ref[1, :, span] += fold(jnp.sum(raw * raw, axis=0) * m)

    pixels = half * half
    return call(
        body,
        (half,),
        (raw_b, stats, mask, weight.array),
        (row_block(half, batch, middle), whole(stats.shape), whole(mask.shape), weight.block()),
        (
            ((pixels, batch, middle), BF),
            ((pixels, batch, wide), BF), ((8, wide), F32),
            ((2, 8, wide), F32),
        ),
        (row_block(half, batch, middle), row_block(half, batch, wide), whole((8, wide)), whole((2, 8, wide))),
        flops=2 * raw_b.size * wide,
        moved=raw_b.size * 6 + pixels * batch * wide * 4,
    )


def kernel_project(sampled, mask, weight):
    pixels, batch, c_in = sampled.shape
    middle = weight.array.shape[2]
    wide = weight.count * middle

    def body(x_ref, m_ref, w_ref, raw_ref, off_ref, sum_ref):
        m = m_ref[:, :1]
        w = w_ref[...].reshape(c_in, middle)
        offset = mean_of(nn(x_ref[pixels // 2], w), m)
        off_ref[...] = jnp.broadcast_to(offset, off_ref.shape)
        part = 7
        first = second = None
        for p in range(0, pixels, part):
            raw = nn(x_ref[p : p + part].reshape(part * batch, c_in), w).reshape(part, batch, middle)
            raw_ref[p : p + part] = (raw - offset).astype(BF)
            one, two = jnp.sum(raw, axis=0), jnp.sum(raw * raw, axis=0)
            first = one if first is None else first + one
            second = two if second is None else second + two
        sum_ref[0] = fold(first * m)
        sum_ref[1] = fold(second * m)

    groups = weight.array.shape[0]
    return call(
        body,
        (weight.count,),
        (sampled, mask, weight.array),
        (
            whole(sampled.shape),
            whole(mask.shape),
            ((groups, weight.rows, middle), lambda k: (0, weight.first + k, 0)),
        ),
        (((pixels, batch, wide), BF), ((8, wide), F32), ((2, 8, wide), F32)),
        (
            ((pixels, batch, middle), lambda k: (0, 0, k)),
            ((8, middle), lambda k: (0, k)),
            ((2, 8, middle), lambda k: (0, 0, k)),
        ),
        flops=2 * sampled.size * wide,
        moved=sampled.size * 2 + pixels * batch * wide * 2,
    )


def kernel_block_one(raw_c, raw_p, stats, mask, weight, half):
    pixels, batch, wide = raw_c.shape
    middle = weight.array.shape[2]

    def body(c_ref, p_ref, s_ref, m_ref, w_ref, one_ref, raw_ref, send_ref, sum_ref):
        zero_first(sum_ref)
        m = m_ref[...]

        raw = None
        for k in range(wide // middle):
            for c in chunks(middle):
                c = slice(k * middle + c.start, k * middle + c.stop)
                al, ap, be = s_ref[0:1, c], s_ref[1:2, c], s_ref[2:3, c]
                for j in range(half):
                    total = c_ref[j, :, c].astype(F32) * al + p_ref[j, :, c].astype(F32) * ap + be
                    one_ref[j, :, c] = (silu_parts(total)[1] * m).astype(BF)
            left = one_ref[:, :, k * middle : (k + 1) * middle].reshape(half * batch, middle)
            part = nn(left, weight.part(w_ref, k, middle))
            raw = part if raw is None else raw + part
        raw = raw.reshape(half, batch, middle)
        m = m_ref[:, :1]
        raw_ref[...] = raw
        sum_ref[0] += fold(jnp.sum(raw, axis=0) * m)
        sum_ref[1] += fold(jnp.sum(raw * raw, axis=0) * m)
        send_sums(send_ref, sum_ref, pl.program_id(0) == half - 1)

    return call(
        body,
        (half,),
        (raw_c, raw_p, stats, mask, weight.array),
        (
            row_block(half, batch, wide),
            row_block(half, batch, wide),
            whole(stats.shape),
            whole(mask.shape),
            weight.block(),
        ),
        (
            ((pixels, batch, wide), BF),
            ((pixels, batch, middle), F32),
            (exchange_shape(2 * middle), F32),
        ),
        (row_block(half, batch, wide), row_block(half, batch, middle), whole(exchange_shape(2 * middle))),
        scratch=[pltpu.VMEM((2, 8, middle), F32)],
        flops=2 * raw_c.size * middle,
        moved=raw_c.size * 10,
    )


def kernel_result(raw_e, block_one, cot, stats, mask, half):
    pixels, batch, wide = raw_e.shape
    slots, _, _, frames, _ = cot.shape

    def body(e_ref, o_ref, g_ref, s_ref, m_ref, res_ref, grad_ref, sum_ref):
        zero_first(sum_ref)
        m = m_ref[...]
        for c in chunks(wide):
            al, be, mean = s_ref[0:1, c], s_ref[1:2, c], s_ref[2:3, c]
            first = second = None
            for j in range(half):
                raw = e_ref[j, :, c].astype(F32)
                sig, act = silu_parts(raw * al + be + o_ref[j, :, c].astype(F32))
                res = act * m
                for s in range(slots):
                    res_ref[s, 0, j, :, c] = res[s * frames : (s + 1) * frames].astype(BF)
                cot = jnp.concatenate([g_ref[s, 0, j, :, c].astype(F32) for s in range(slots)])
                grad = cot * m * (sig + act * (1.0 - sig))
                grad_ref[j, :, c] = grad.astype(BF)
                other = grad * (raw - mean)
                first = grad if first is None else first + grad
                second = other if second is None else second + other
            sum_ref[0, :, c] += fold(first)
            sum_ref[1, :, c] += fold(second)

    outside = (slots, 1, half, frames, wide), lambda i: (0, i, 0, 0, 0)
    return call(
        body,
        (half,),
        (raw_e, block_one, cot, stats, mask),
        (
            row_block(half, batch, wide),
            row_block(half, batch, wide),
            outside,
            whole(stats.shape),
            whole(mask.shape),
        ),
        (
            (cot.shape, BF),
            ((pixels, batch, wide), BF),
            ((2, 8, wide), F32),
        ),
        (outside, row_block(half, batch, wide), whole((2, 8, wide))),
        flops=20 * raw_e.size,
        moved=raw_e.size * 14,
    )


def kernel_block_back(grad_narrow, raw_d, stats_d, weight, grad_total, raw_c, raw_p, stats, mask, half):
    pixels, batch, wide = raw_c.shape
    middle = raw_d.shape[2]

    def body(n_ref, d_ref, sd_ref, w_ref, t_ref, c_ref, p_ref, s_ref, m_ref, nar_ref, one_ref, sum_ref, back):
        zero_first(sum_ref)
        m = m_ref[...]

        for c in chunks(middle):
            scale, mean, shift, spread = (sd_ref[n : n + 1, c] for n in range(4))
            for j in range(half):
                value = scale * n_ref[j, :, c] - m * (shift + (d_ref[j, :, c] - mean) * spread)
                nar_ref[j, :, c] = value.astype(BF)

        left = nar_ref[...].reshape(half * batch, middle)
        for k in range(wide // middle):
            back[k] = nt(left, weight.part(w_ref, k, middle)).reshape(half, batch, middle)
            for d in chunks(middle):
                c = slice(k * middle + d.start, k * middle + d.stop)
                al, ap, be, mean_c, _, mean_p = (s_ref[n : n + 1, c] for n in range(6))
                sums = [None] * 3
                for j in range(half):
                    raw_c, raw_p = c_ref[j, :, c].astype(F32), p_ref[j, :, c].astype(F32)
                    sig, act = silu_parts(raw_c * al + raw_p * ap + be)
                    grad = (t_ref[j, :, c].astype(F32) + back[k, j, :, d]) * m * (sig + act * (1.0 - sig))
                    one_ref[j, :, c] = grad.astype(BF)
                    parts = (grad, grad * (raw_c - mean_c), grad * (raw_p - mean_p))
                    sums = [p if t is None else t + p for t, p in zip(sums, parts)]
                for n in range(3):
                    sum_ref[n, :, c] += fold(sums[n])

    return call(
        body,
        (half,),
        (grad_narrow, raw_d, stats_d, weight.array, grad_total, raw_c, raw_p, stats, mask),
        (
            row_block(half, batch, middle),
            row_block(half, batch, middle),
            whole(stats_d.shape),
            weight.block(),
            row_block(half, batch, wide),
            row_block(half, batch, wide),
            row_block(half, batch, wide),
            whole(stats.shape),
            whole(mask.shape),
        ),
        (
            ((pixels, batch, middle), BF),
            ((pixels, batch, wide), BF),
            ((3, 8, wide), F32),
        ),
        (row_block(half, batch, middle), row_block(half, batch, wide), whole((3, 8, wide))),
        scratch=[pltpu.VMEM((wide // middle, half, batch, middle), F32)],
        flops=2 * raw_c.size * middle,
        moved=raw_c.size * 16,
    )


def kernel_expand_back(grad_one, raw_c, raw_p, stats, weight, raw_b, stats_b, mask, half):
    pixels, batch, wide = raw_c.shape
    middle = raw_b.shape[2]

    def body(g_ref, c_ref, p_ref, s_ref, w_ref, b_ref, sb_ref, m_ref, wid_ref, sho_ref, out_ref, send_ref, sum_ref):
        zero_first(sum_ref)
        m = m_ref[...]
        back = None
        for k in range(weight.count):
            for c in chunks(middle):
                c = slice(k * middle + c.start, k * middle + c.stop)
                rows_s = [s_ref[n : n + 1, c] for n in range(8)]
                for j in range(half):
                    grad = g_ref[j, :, c].astype(F32)
                    for raw_ref, to_ref, n in ((c_ref, wid_ref, 0), (p_ref, sho_ref, 4)):
                        scale, mean, shift, spread = rows_s[n : n + 4]
                        value = scale * grad - m * (shift + (raw_ref[j, :, c].astype(F32) - mean) * spread)
                        to_ref[j, :, c] = value.astype(BF)
            left = wid_ref[:, :, k * middle : (k + 1) * middle].reshape(half * batch, middle)
            part = nt(left, weight.of(w_ref, k))
            back = part if back is None else back + part
        m = m_ref[:, :1]
        raw = b_ref[...]
        sig, act = silu_parts(raw * sb_ref[0:1] + sb_ref[1:2])
        grad = back.reshape(half, batch, middle) * m * (sig + act * (1.0 - sig))
        out_ref[...] = grad
        sum_ref[0] += fold(jnp.sum(grad, axis=0))
        sum_ref[1] += fold(jnp.sum(grad * ((raw - sb_ref[2:3]) * sb_ref[3:4]), axis=0))
        send_sums(send_ref, sum_ref, pl.program_id(0) == half - 1)

    return call(
        body,
        (half,),
        (grad_one, raw_c, raw_p, stats, weight.array, raw_b, stats_b, mask),
        (
            row_block(half, batch, wide),
            row_block(half, batch, wide),
            row_block(half, batch, wide),
            whole(stats.shape),
            weight.block(),
            row_block(half, batch, middle),
            whole(stats_b.shape),
            whole(mask.shape),
        ),
        (
            ((pixels, batch, wide), BF),
            ((pixels, batch, wide), BF),
            ((pixels, batch, middle), F32),
            (exchange_shape(2 * middle), F32),
        ),
        (
            row_block(half, batch, wide),
            row_block(half, batch, wide),
            row_block(half, batch, middle),
            whole(exchange_shape(2 * middle)),
        ),
        scratch=[pltpu.VMEM((2, 8, middle), F32)],
        flops=2 * raw_c.size * middle,
        moved=raw_c.size * 16,
    )


def kernel_join(excited, outputs, raw_g, stats_g, mask, weight, half):
    pixels, batch, middle = excited.shape
    group = middle // 4
    wide = weight.count * middle

    def body(x_ref, o1, o2, r_ref, sg_ref, m_ref, w_ref, join_ref, raw_ref, off_ref, sum_ref):
        zero_first(sum_ref)
        m = m_ref[:, :group]
        join_ref[:, :, :group] = x_ref[...]
        join_ref[:, :, group : 2 * group] = o1[...]
        join_ref[:, :, 2 * group : 3 * group] = o2[...]
        act = silu_parts(r_ref[...] * sg_ref[0:1] + sg_ref[1:2])[1] * m
        join_ref[:, :, 3 * group :] = act.astype(BF)

        @pl.when(pl.program_id(0) == 0)
        def _():
            for k in range(weight.count):
                few = nn(join_ref[half // 2], weight.of(w_ref, k))
                off_ref[0:1, k * middle : (k + 1) * middle] = mean_of(few, m_ref[:, :1])

        left = join_ref[...].reshape(half * batch, middle)
        m = m_ref[:, :1]
        for k in range(weight.count):
            raw = nn(left, weight.of(w_ref, k)).reshape(half, batch, middle)
            span = slice(k * middle, (k + 1) * middle)
            offset = off_ref[0:1, span]
            raw_ref[:, :, span] = (raw - offset).astype(BF)
            sum_ref[0, :, span] += fold(jnp.sum(raw, axis=0) * m)
            sum_ref[1, :, span] += fold(jnp.sum(raw * raw, axis=0) * m)

    part = row_block(half, batch, group)
    return call(
        body,
        (half,),
        (excited, outputs[0], outputs[1], raw_g, stats_g, mask, weight.array),
        (part, part, part, part, whole(stats_g.shape), whole(mask.shape), weight.block()),
        (((pixels, batch, middle), BF), ((pixels, batch, wide), BF), ((8, wide), F32), ((2, 8, wide), F32)),
        (row_block(half, batch, middle), row_block(half, batch, wide), whole((8, wide)), whole((2, 8, wide))),
        flops=2 * excited.size * wide,
        moved=excited.size * 4 + pixels * batch * wide * 4,
    )


def kernel_final_back(grad_total, raw_e, stats, mask, weight, raw_g, stats_g, half):
    pixels, batch, wide = raw_e.shape
    middle = weight.array.shape[2]
    group = middle // 4

    def body(g_ref, e_ref, s_ref, m_ref, w_ref, r_ref, sg_ref, fin_ref, out_ref, pre_ref, send_ref, sum_ref):
        zero_first(sum_ref)
        m = m_ref[...]

        back = None
        for k in range(weight.count):
            for c in chunks(middle):
                c = slice(k * middle + c.start, k * middle + c.stop)
                scale, mean, shift, spread = (s_ref[n : n + 1, c] for n in range(4))
                for j in range(half):
                    value = scale * g_ref[j, :, c].astype(F32) - m * (
                        shift + (e_ref[j, :, c].astype(F32) - mean) * spread
                    )
                    fin_ref[j, :, c] = value.astype(BF)
            left = fin_ref[:, :, k * middle : (k + 1) * middle].reshape(half * batch, middle)
            part = nt(left, weight.of(w_ref, k))
            back = part if back is None else back + part
        back = back.reshape(half, batch, middle)
        out_ref[...] = back
        raw = r_ref[...]
        sig, act = silu_parts(raw * sg_ref[0:1] + sg_ref[1:2])
        pre = back[:, :, 3 * group :] * m_ref[:, :group] * (sig + act * (1.0 - sig))
        pre_ref[...] = pre
        sum_ref[0] += fold(jnp.sum(pre, axis=0))
        sum_ref[1] += fold(jnp.sum(pre * (raw - sg_ref[2:3]), axis=0))
        send_sums(send_ref, sum_ref, pl.program_id(0) == half - 1)

    part = row_block(half, batch, group)
    return call(
        body,
        (half,),
        (grad_total, raw_e, stats, mask, weight.array, raw_g, stats_g),
        (
            row_block(half, batch, wide),
            row_block(half, batch, wide),
            whole(stats.shape),
            whole(mask.shape),
            weight.block(),
            part,
            whole(stats_g.shape),
        ),
        (
            ((pixels, batch, wide), BF),
            ((pixels, batch, middle), F32),
            ((pixels, batch, group), F32),
            (exchange_shape(2 * group), F32),
        ),
        (row_block(half, batch, wide), row_block(half, batch, middle), part, whole(exchange_shape(2 * group))),
        scratch=[pltpu.VMEM((2, 8, group), F32)],
        flops=2 * raw_e.size * middle,
        moved=raw_e.size * 10,
    )


def kernel_weight_grad(left, right, dp, fsdp, rows, first, total, into=None):
    pixels, batch, depth = left.shape
    columns = right.shape[2]
    middle = min(columns, 512)
    owners = dp * fsdp

    def body(*refs):
        a_ref, b_ref, out_ref = refs[0], refs[1], refs[-1]
        value = tn(a_ref[...].reshape(-1, depth), b_ref[...].reshape(-1, middle)).astype(BF)
        value = value.reshape(dp, fsdp, rows, middle)
        for d in range(dp):
            out_ref[:, d] = value[d]

    ins = (left, right)
    in_specs = [
        pl.BlockSpec((pixels, batch, depth), lambda k: (0, 0, 0)),
        pl.BlockSpec((pixels, batch, middle), lambda k: (0, 0, k)),
    ]
    alias = {}
    if into is not None:
        ins += (into,)
        in_specs.append(pl.BlockSpec(memory_space=pl.ANY))
        alias = {2: 0}
    return pl.pallas_call(
        body,
        grid=(columns // middle,),
        in_specs=in_specs,
        out_specs=pl.BlockSpec((fsdp, dp, rows, middle), lambda k: (0, 0, first + k, 0)),
        out_shape=jax.ShapeDtypeStruct((fsdp, dp, total, middle), BF),
        input_output_aliases=alias,
        compiler_params=pltpu.CompilerParams(
            vmem_limit_bytes=56 * 1024 * 1024, dimension_semantics=("arbitrary",)
        ),
        cost_estimate=pl.CostEstimate(
            flops=2 * left.size * columns,
            bytes_accessed=left.size * 2 + right.size * 2 + owners * rows * columns * 2,
            transcendentals=0,
        ),
    )(*ins)


def frame_rows(rows):
    return lax.broadcasted_iota(jnp.int32, (1, rows, 128), 1)


def shift_frames(value, frames):
    shape = value.shape
    value = value.reshape(-1, frames, 128)
    spot = frame_rows(frames)
    before = jnp.where(spot == 0, 0.0, pltpu.roll(value, 1, 1))
    after_ = jnp.where(spot == frames - 1, 0.0, pltpu.roll(value, frames - 1, 1))
    return before.reshape(shape), after_.reshape(shape)


def nine_taps(pad, cols, half, batch):
    for r in range(3):
        for c in range(3):
            lane = (r * 3 + c) * 128
            part = pad[r : r + half, c : c + half]
            cols[:, lane : lane + 128] = part.reshape(half * half * batch, 128)


def clear_border(pad, half):
    pad[0] = jnp.zeros_like(pad[0])
    pad[half + 1] = jnp.zeros_like(pad[0])
    pad[:, 0] = jnp.zeros_like(pad[:, 0])
    pad[:, half + 1] = jnp.zeros_like(pad[:, 0])


def kernel_motion(rows_d, stats, mask, weight, windows, half):
    pixels, batch, middle = rows_d.shape
    narrow = weight.shape[1]

    def body(d_ref, s_ref, m_ref, w_ref, act_ref, raw_ref, win_ref, sq_ref):
        for c in chunks(middle):
            al, be, m = s_ref[0:1, c], s_ref[1:2, c], m_ref[...]

            @pl.loop(0, half)
            def _(i):
                for j in range(half):
                    act = silu_parts(d_ref[i * half + j, :, c] * al + be)[1] * m
                    act_ref[i * half + j, :, c] = act.astype(BF)

        raw = nn(act_ref[...].reshape(pixels * batch, middle), w_ref[...])
        raw_ref[...] = raw.reshape(pixels, batch, narrow)
        square = jnp.zeros((batch, narrow), F32)
        sums = [jnp.zeros((batch, narrow), F32) for _ in range(9)]
        for p in range(pixels):
            value = raw_ref[p]
            square = square + value * value
            for t in range(9):
                if windows[p // half][p % half][t]:
                    sums[t] = sums[t] + value
        for t in range(9):
            win_ref[t] = sums[t]
        sq_ref[...] = square

    return call(
        body,
        (1,),
        (rows_d, stats, mask, weight),
        (whole(rows_d.shape), whole(stats.shape), whole(mask.shape), whole(weight.shape)),
        (
            (rows_d.shape, BF),
            ((pixels, batch, narrow), F32),
            ((9, batch, narrow), F32),
            ((batch, narrow), F32),
        ),
        (
            whole(rows_d.shape),
            whole((pixels, batch, narrow)),
            whole((9, batch, narrow)),
            whole((batch, narrow)),
        ),
        flops=2 * rows_d.size * narrow,
        moved=rows_d.size * 6,
    )


def kernel_group(source, extra, taps, weight, mask, index, half, frames):
    pixels, batch, middle = source.shape
    group = 128

    def body(*refs):
        if index == 1:
            x_ref, e_ref, t_ref, w_ref, m_ref, first_ref, pad_ref, raw_ref, send_ref, cols, sum_ref = refs
            excited = (x_ref[...].astype(F32) * e_ref[...]).astype(BF)
            first_ref[...] = excited
            piece = first_ref[:, :, group : 2 * group].astype(F32)
        else:
            x_ref, r_ref, s_ref, t_ref, w_ref, m_ref, first_ref, pad_ref, raw_ref, send_ref, cols, sum_ref = refs
            act = silu_parts(r_ref[...] * s_ref[0:1] + s_ref[1:2])[1] * m_ref[:, :group]
            first_ref[...] = act.astype(BF)
            piece = x_ref[...].astype(F32) + first_ref[...].astype(F32)
        before, after_ = shift_frames(piece, frames)
        value = t_ref[0:1] * before + t_ref[1:2] * piece + t_ref[2:3] * after_
        clear_border(pad_ref, half)
        pad_ref[1 : half + 1, 1 : half + 1] = value.astype(BF).reshape(half, half, batch, group)
        nine_taps(pad_ref, cols, half, batch)
        raw = nn(cols[...], w_ref[...]).reshape(pixels, batch, group)
        raw_ref[...] = raw
        m = m_ref[:, :group]
        sum_ref[0] = fold(jnp.sum(raw, axis=0) * m)
        sum_ref[1] = fold(jnp.sum(raw * raw, axis=0) * m)
        send_sums(send_ref, sum_ref)

    block = (pixels, batch, group)
    if index == 1:
        ins = (source, extra, taps, weight, mask)
        first = (source.shape, BF)
        specs = tuple(whole(a.shape) for a in ins)
    else:
        ins = (source, extra[0], extra[1], taps, weight, mask)
        first = (block, BF)
        specs = ((block, lambda i: (0, 0, index)),) + tuple(whole(a.shape) for a in ins[1:])
    outs = (
        first,
        ((half + 2, half + 2, batch, group), BF),
        (block, F32),
        (exchange_shape(2 * group), F32),
    )
    return call(
        body,
        (1,),
        ins,
        specs,
        outs,
        tuple(whole(o[0]) for o in outs),
        scratch=[pltpu.VMEM((pixels * batch, 9 * group), BF), pltpu.VMEM((2, 8, group), F32)],
        flops=2 * pixels * batch * 9 * group * group,
        moved=pixels * batch * group * 12,
    )


def kernel_group_weights(pad, grad, half):
    pixels, batch, group = grad.shape

    def body(p_ref, g_ref, out_ref, cols):
        nine_taps(p_ref, cols, half, batch)
        out_ref[...] = tn(cols[...], g_ref[...].reshape(pixels * batch, group)).astype(BF)

    return call(
        body,
        (1,),
        (pad, grad),
        (whole(pad.shape), whole(grad.shape)),
        (((9 * group, group), BF),),
        (whole((9 * group, group)),),
        scratch=[pltpu.VMEM((pixels * batch, 9 * group), BF)],
        flops=2 * grad.size * 9 * group,
        moved=grad.size * 6,
    )[0]


def kernel_group_back(
    grad, raw, stats, weight, taps, excited, previous, joined, lower, mask, index, half, frames
):
    pixels, batch, group = grad.shape
    block = (pixels, batch, group)
    rows = pixels * batch

    def body(*refs):
        g_ref, r_ref, s_ref, w_ref, t_ref, x_ref, j_ref, m_ref = refs[:8]
        pad, cols, sum_ref = refs[-3:]
        m = m_ref[:, :group]
        raw = r_ref[...]
        value = s_ref[0:1] * g_ref[...] - m * (s_ref[2:3] + (raw - s_ref[1:2]) * s_ref[3:4])
        if index > 1:
            p_ref, l_ref, ls_ref, gg_ref, gp_ref, tg_ref, pre_ref, send_ref = refs[8:16]
        else:
            g2_ref, g3_ref, d_ref, gg_ref, gp_ref, tg_ref, at_ref = refs[8:15]
        gg_ref[...] = value.astype(BF)
        clear_border(pad, half)
        pad[1 : half + 1, 1 : half + 1] = gg_ref[...].reshape(half, half, batch, group)
        nine_taps(pad, cols, half, batch)
        back = nn(cols[...], w_ref[...]).reshape(block)
        before, after_ = shift_frames(back, frames)
        below = t_ref[0:1] * after_ + t_ref[1:2] * back + t_ref[2:3] * before
        gp_ref[...] = below
        piece = x_ref[...].astype(F32)
        if index > 1:
            piece = piece + p_ref[...].astype(F32)
        tg_ref[0] = fold(jnp.sum(after_ * piece, axis=0))
        tg_ref[1] = fold(jnp.sum(back * piece, axis=0))
        tg_ref[2] = fold(jnp.sum(before * piece, axis=0))
        if index > 1:
            raw = l_ref[...]
            sig, act = silu_parts(raw * ls_ref[0:1] + ls_ref[1:2])
            pre = (j_ref[...] + below) * m * (sig + act * (1.0 - sig))
            pre_ref[...] = pre
            sum_ref[0] = fold(jnp.sum(pre, axis=0))
            sum_ref[1] = fold(jnp.sum(pre * (raw - ls_ref[2:3]), axis=0))
            send_sums(send_ref, sum_ref)
        else:
            for k, source in enumerate((j_ref, gp_ref, g2_ref, g3_ref)):
                span = slice(k * group, (k + 1) * group)
                at_ref[:, span] = jnp.sum(source[...] * d_ref[:, :, span].astype(F32), axis=0)

    column = lambda k: (block, lambda i: (0, 0, k))
    ins = [grad, raw, stats, weight, taps, excited, joined, mask]
    specs = [whole(a.shape) for a in ins]
    specs[5] = column(index)
    specs[6] = column(index - 1)
    outs = [(block, BF), (block, F32), ((3, 8, group), F32)]
    if index > 1:
        more = [previous, lower[0], lower[1]]
        outs += [(block, F32), (exchange_shape(2 * group), F32)]
    else:
        more = list(previous)
        outs += [((batch, 4 * group), F32)]
    return call(
        body,
        (1,),
        ins + more,
        specs + [whole(a.shape) for a in more],
        outs,
        [whole(o[0]) for o in outs],
        scratch=[
            pltpu.VMEM((half + 2, half + 2, batch, group), BF),
            pltpu.VMEM((rows, 9 * group), BF),
            pltpu.VMEM((2, 8, group), F32),
        ],
        flops=2 * rows * 9 * group * group,
        moved=rows * group * 24,
    )


def kernel_motion_back(
    joined, pieces, attend, rows_d, stats_d, raw_m, kmap, change, stats_m, weight, mask, half
):
    pixels, batch, middle = rows_d.shape
    narrow = raw_m.shape[2]
    group = middle // 4

    def body(j_ref, p1, p2, p3, e_ref, d_ref, sd_ref, r_ref, k_ref, c_ref, sm_ref, w_ref, m_ref, out_ref, mg_ref, send_ref, sum_ref):
        zero_first(sum_ref)
        mn = m_ref[:, :narrow]
        grad = (k_ref[...] * c_ref[0] - c_ref[1]) * mn
        value = sm_ref[0:1] * grad - mn * (sm_ref[2:3] + (r_ref[...] - sm_ref[1:2]) * sm_ref[3:4])
        mg_ref[...] = value.astype(BF)
        back = nt(mg_ref[...].reshape(half * batch, narrow), w_ref[...])
        back = back.reshape(half, batch, middle)
        m = m_ref[:, :group]
        for k, ref in enumerate((j_ref, p1, p2, p3)):
            c = slice(k * group, (k + 1) * group)
            raw = d_ref[:, :, c]
            sig, act = silu_parts(raw * sd_ref[0:1, c] + sd_ref[1:2, c])
            out = (ref[...] * e_ref[:, c] + back[:, :, c]) * m * (sig + act * (1.0 - sig))
            out_ref[:, :, c] = out
            sum_ref[0, :, c] += fold(jnp.sum(out, axis=0))
            sum_ref[1, :, c] += fold(jnp.sum(out * (raw - sd_ref[2:3, c]), axis=0))
        send_sums(send_ref, sum_ref, pl.program_id(0) == half - 1)

    part = row_block(half, batch, group)
    ins = (joined,) + tuple(pieces)
    ins += (attend, rows_d, stats_d, raw_m, kmap, change, stats_m, weight, mask)
    return call(
        body,
        (half,),
        ins,
        (
            part,
            part,
            part,
            part,
            whole(attend.shape),
            row_block(half, batch, middle),
            whole(stats_d.shape),
            row_block(half, batch, narrow),
            ((half, 1, narrow), lambda i: (i, 0, 0)),
            whole(change.shape),
            whole(stats_m.shape),
            whole(weight.shape),
            whole(mask.shape),
        ),
        (
            ((pixels, batch, middle), F32),
            ((pixels, batch, narrow), BF),
            (exchange_shape(2 * middle), F32),
        ),
        (row_block(half, batch, middle), row_block(half, batch, narrow), whole(exchange_shape(2 * middle))),
        scratch=[pltpu.VMEM((2, 8, middle), F32)],
        flops=2 * rows_d.size * narrow,
        moved=rows_d.size * 12,
    )


class Sums:
    def __init__(self, dp, fsdp):
        self.devices = dp * fsdp
        half = self.devices // 2
        self.groups = [[2 * i + c for i in range(half)] for c in range(2)]
        self.swap = [(i, i ^ 1) for i in range(self.devices)]

    def flat(self, values):
        size = values.shape[0]
        if size <= 2048:
            copies = jnp.broadcast_to(values[None], (self.devices, size))
            return jnp.sum(lax.all_to_all(copies, AXES, 0, 0), axis=0)
        core = lax.axis_index("fsdp") % 2
        halves = values.reshape(2, size // 2)
        mine = lax.dynamic_index_in_dim(halves, core, 0, False)
        other = lax.dynamic_index_in_dim(halves, 1 - core, 0, False)
        mine = mine + lax.ppermute(other, AXES, self.swap)
        copies = jnp.broadcast_to(mine[None], (self.devices // 2, size // 2))
        mine = jnp.sum(lax.all_to_all(copies, AXES, 0, 0, axis_index_groups=self.groups), axis=0)
        other = lax.ppermute(mine, AXES, self.swap)
        low = jnp.where(core == 0, mine, other)
        high = jnp.where(core == 0, other, mine)
        return jnp.concatenate([low, high])

    def ready(self, copies, count):
        total = jnp.sum(lax.all_to_all(copies, AXES, 0, 0, tiled=True), axis=(0, 1))
        return list(total.reshape(count, -1))

    def __call__(self, *arrays):
        sizes = [a.size for a in arrays]
        extra = -sum(sizes) % 256
        parts = [a.reshape(-1) for a in arrays]
        if extra:
            parts.append(jnp.zeros((extra,), F32))
        merged = self.flat(jnp.concatenate(parts))
        out, begin = [], 0
        for a, size in zip(arrays, sizes):
            out.append(merged[begin : begin + size].reshape(a.shape))
            begin += size
        return out


def pairs_of(dp, fsdp):
    return [(i, i ^ 1) for i in range(dp * fsdp)]


def same_core(fsdp):
    return [[2 * i + c for i in range(fsdp // 2)] for c in range(2)]


def quick_gather(dp, fsdp, value):
    value = lax.all_to_all(jnp.broadcast_to(value[None], (dp,) + value.shape), "dp", 0, 0)
    value = lax.all_to_all(
        jnp.broadcast_to(value[None], (fsdp // 2,) + value.shape),
        "fsdp",
        0,
        0,
        axis_index_groups=same_core(fsdp),
    )
    other = lax.ppermute(value, AXES, pairs_of(dp, fsdp))
    core = lax.axis_index("fsdp") % 2
    low = jnp.where(core == 0, value, other)
    high = jnp.where(core == 0, other, value)
    both = jnp.stack([low, high], axis=2).swapaxes(0, 1)
    return both.reshape((dp * fsdp,) + both.shape[3:])


def scatter_cores(dp, fsdp, value):
    core = lax.axis_index("fsdp") % 2
    mine = lax.dynamic_index_in_dim(value, core, 0, False)
    other = lax.dynamic_index_in_dim(value, 1 - core, 0, False)
    other = lax.ppermute(other, AXES, pairs_of(dp, fsdp))
    return (mine.astype(F32) + other.astype(F32)).astype(BF)


def scatter_halves(dp, value, bit):
    mine = (lax.axis_index("dp") >> bit) & 1
    other = lax.dynamic_index_in_dim(value, 1 - mine, 0, False)
    other = lax.ppermute(other, "dp", [(i, i ^ (1 << bit)) for i in range(dp)])
    mine = lax.dynamic_index_in_dim(value, mine, 0, False)
    return (mine.astype(F32) + other.astype(F32)).astype(BF)


def scatter_fsdp(fsdp, value):
    value = lax.all_to_all(value, "fsdp", 0, 0, axis_index_groups=same_core(fsdp))
    return jnp.sum(value.astype(F32), axis=0)


def scatter_dp(value):
    return jnp.sum(lax.all_to_all(value, "dp", 0, 0).astype(F32), axis=0)


def by_low_bit(count):
    order = [0]
    while len(order) < count:
        order = [2 * i for i in order] + [2 * i + 1 for i in order]
    return order


def after(value, *others):
    return lax.optimization_barrier((value, others))[0]


def affine(total, square, count, gain, bias, offset=0.0):
    mean = total / count
    inv = lax.rsqrt(square / count - mean * mean + EPSILON)
    alpha = gain * inv
    mean = mean - offset
    return mean, inv, alpha, bias - mean * alpha


def local(
    dp,
    fsdp,
    clip_count,
    frame_count,
    frame_mask,
    features,
    w_reduce1,
    w_spatial1,
    w_expand1,
    w_project1,
    w_reduce2,
    w_motion_in,
    w_motion_out,
    w_spatial2,
    w_expand2,
    gains,
    biases,
    motion_taps,
    temporal_taps,
    cotangent,
):
    devices = dp * fsdp
    sums = Sums(dp, fsdp)
    slots, frames, height = features.shape[:3]
    half = height // 2
    area = half * half
    c_in = features.shape[-1]
    middle = w_reduce1.shape[1]
    group = middle // 4
    wide = w_expand1.shape[1]
    narrow = w_motion_in.shape[1]
    valid = (
        (jnp.arange(slots)[:, None] < clip_count[0])
        & (jnp.arange(frames)[None, :] < frame_count[:, None])
        & (frame_mask == 1)
    ).astype(F32)
    mask = valid[None, None, :, :, None]
    mask_rows = jnp.broadcast_to(valid.reshape(-1, 1), (slots * frames, 256))
    fmask = valid[:, :, None]
    widths = [middle, middle, wide, wide, middle, narrow, middle, group, group, group, wide]
    starts = [sum(widths[:k]) for k in range(len(widths))]
    gain = [gains[s : s + w] for s, w in zip(starts, widths)]
    bias = [biases[s : s + w] for s, w in zip(starts, widths)]

    feats = features.transpose(0, 2, 3, 1, 4).reshape(slots, -1, c_in)

    def gather(value):
        return lax.all_gather(value, AXES, axis=0, tiled=False)

    def rows_of(value):
        return jnp.pad(value, ((0, 0), (0, -value.shape[1] % middle))).reshape(
            value.shape[0], -1, middle
        )

    def columns_of(value):
        rows = value.shape[0]
        return value.reshape(rows, -1, middle).swapaxes(0, 1).reshape(-1, middle)

    own = middle // devices
    full_reduce1 = quick_gather(dp, fsdp, w_reduce1).reshape(c_in, middle)
    rows1, rowsp, rows2 = w_expand1.shape[0], w_project1.shape[0], w_reduce2.shape[0]
    blocks = wide // middle
    aligned = own % 16 == 0

    def gather_packed(*parts):
        value = gather(jnp.concatenate([part[0] for part in parts]))
        begin, flat, places = 0, [], []
        for part, rows, count in parts:
            places.append((rows * (1 if aligned else devices), begin // rows, count))
            mine = value[:, begin : begin + part.shape[0]]
            flat.append(mine.reshape(devices, -1, rows, middle).swapaxes(0, 1).reshape(-1, middle))
            begin += part.shape[0]
        array = value if aligned else jnp.concatenate(flat)[None]
        return [Packed(array, *place) for place in places]

    project1, expand1, reduce2, spatial1 = gather_packed(
        (columns_of(w_project1), rowsp, blocks),
        (columns_of(w_expand1), rows1, blocks),
        (w_reduce2, rows2, 1),
        (w_spatial1.reshape(-1, middle), own, 1),
    )
    taps1 = [Packed(spatial1.array, spatial1.rows, spatial1.first + t, 1) for t in range(9)]
    smalls = jnp.concatenate(
        [w_spatial2.reshape(1, -1), w_motion_in.reshape(1, -1), w_motion_out.reshape(1, -1)], axis=1
    )
    rowse = w_expand2.shape[0]
    late_rows = columns_of(w_expand2).shape[0]
    smalls = rows_of(smalls)[0]
    expand2, tail = gather_packed(
        (columns_of(w_expand2), rowse, blocks), (smalls, 1, smalls.shape[0])
    )
    if aligned:
        flat_small = tail.array[:, late_rows:].reshape(devices, -1)
    else:
        flat_small = (
            tail.array[0, late_rows * devices :]
            .reshape(-1, devices, middle)
            .swapaxes(0, 1)
            .reshape(devices, -1)
        )
    batch = slots * frames
    pixel_rows = (area, batch)
    size_s, size_m = w_spatial2.size, w_motion_in.size
    kernels = (
        flat_small[:, :size_s].reshape(devices, 27, -1).swapaxes(0, 1).reshape(3, 9, group, group)
    )
    small = flat_small[:, size_s : size_s + 2 * size_m].reshape(devices, 2, own, narrow)
    full_motion_in = small[:, 0].reshape(middle, narrow)
    full_motion_out = small[:, 1].reshape(middle, narrow).astype(F32)

    raw_a, off_a, sums_a = kernel_reduce1(feats, full_reduce1, mask_rows, height, frames)
    sum_a, square_a, frame_total, pairs = sums(
        jnp.sum(sums_a[0], axis=0),
        jnp.sum(sums_a[1], axis=0),
        jnp.sum(valid),
        jnp.sum(valid[:, :-1] * valid[:, 1:]),
    )
    count_big = frame_total * (height * height)
    count = frame_total * area
    mean_a, inv_a, alpha_a, beta_a = affine(
        sum_a, square_a, count_big, gain[0], bias[0], off_a[0]
    )
    act_a = kernel_act(raw_a, jnp.stack([alpha_a, beta_a]), mask_rows)
    raw_b, sums_b = kernel_conv_down(act_a, mask_rows, taps1)
    raw_b = raw_b.reshape(area, batch, middle)
    sampled = (
        features.reshape(slots, frames, half, 2, half, 2, c_in)[:, :, :, 0, :, 0]
        .transpose(2, 3, 0, 1, 4)
        .reshape(area, batch, c_in)
    )
    raw_p, off_p, sums_p = kernel_project(sampled, mask_rows, project1)

    def moments(raw):
        return total_over(raw * mask), total_over(raw * raw * mask)

    sum_b, square_b = sums.ready(sums_b, 2)
    mean_b, inv_b, alpha_b, beta_b = affine(sum_b, square_b, count, gain[1], bias[1])
    act_b, raw_c, off_c, sums_c = kernel_expand(
        raw_b, jnp.stack([alpha_b, beta_b]), mask_rows, expand1, half
    )
    sums_c, sums_p = jnp.sum(sums_c, axis=1), jnp.sum(sums_p, axis=1)
    sum_c, square_c, sum_p, square_p = sums(sums_c[0], sums_c[1], sums_p[0], sums_p[1])
    mean_c, inv_c, alpha_c, beta_c = affine(sum_c, square_c, count, gain[2], bias[2], off_c[0])
    mean_p, inv_p, alpha_p, beta_p = affine(sum_p, square_p, count, gain[3], bias[3], off_p[0])
    stats_one = jnp.stack(
        [alpha_c, alpha_p, beta_c + beta_p, mean_c, inv_c, mean_p, inv_p, jnp.zeros_like(mean_p)]
    )
    block_one, rows_d, sums_d = kernel_block_one(
        raw_c, raw_p, stats_one, mask_rows, reduce2, half
    )

    sum_d, square_d = sums.ready(sums_d, 2)
    mean_d, inv_d, alpha_d, beta_d = affine(sum_d, square_d, count, gain[4], bias[4])
    inside = [
        [
            [int(0 <= y - r + 1 < half and 0 <= x - c + 1 < half) for r in range(3) for c in range(3)]
            for x in range(half)
        ]
        for y in range(half)
    ]
    windows = jnp.array(inside, F32)
    act_d, raw_m, in_window, square_rows = kernel_motion(
        rows_d, jnp.stack([alpha_d, beta_d]), mask_rows, full_motion_in, inside, half
    )
    in_window = in_window.reshape(9, slots, frames, narrow)
    kmap = jnp.sum(windows[..., None] * motion_taps, axis=2)
    ksum = jnp.sum(kmap, axis=(0, 1))
    mapped = jnp.sum(in_window * motion_taps[:, None, None, :], axis=0)
    plain = in_window[4]
    vnext = later(fmask)
    pool_raw = (vnext / area) * (later(mapped * fmask) - fmask * plain)
    pool_one = (vnext / area) * (later(fmask) * ksum - fmask * area)
    flat_raw = pool_raw.reshape(-1, narrow)
    flat_valid = valid.reshape(-1, 1)
    gram = lax.dot_general(
        flat_raw * flat_valid, flat_raw, (((0,), (0,)), ((), ())), precision=HIGHEST
    )
    sum_m, square_m, pool_a, gram_aa = sums(
        total_over(plain * fmask),
        total_over(square_rows.reshape(plain.shape) * fmask),
        jnp.sum(flat_raw * flat_valid, axis=0), gram
    )
    mean_m, inv_m, alpha_m, beta_m = affine(sum_m, square_m, count, gain[5], bias[5])
    step = ksum / area - 1.0
    pool_b = pairs * step
    gram_ab = pool_a[:, None] * step[None, :]
    gram_bb = pairs * step[:, None] * step[None, :]
    pooled = alpha_m * pool_raw + beta_m * pool_one
    lifted = jnp.einsum("cfr,or->cfo", pooled, full_motion_out, precision=HIGHEST)
    gram_p = (
        alpha_m[:, None] * alpha_m * gram_aa
        + alpha_m[:, None] * beta_m * gram_ab
        + beta_m[:, None] * alpha_m * gram_ab.T
        + beta_m[:, None] * beta_m * gram_bb
    )
    sum_x = jnp.dot(full_motion_out, alpha_m * pool_a + beta_m * pool_b, precision=HIGHEST)
    square_x = jnp.sum(jnp.dot(full_motion_out, gram_p, precision=HIGHEST) * full_motion_out, axis=1)
    mean_x, inv_x, alpha_x, beta_x = affine(sum_x, square_x, frame_total, gain[6], bias[6])
    sigma = jax.nn.sigmoid(lifted * alpha_x + beta_x)
    attend1 = 2.0 * sigma
    attend_rows = attend1.reshape(batch, middle)
    tap_rows = [temporal_taps[k] for k in range(3)]
    excited, pad, raw, partial = kernel_group(
        act_d, attend_rows, tap_rows[0], kernels[0].reshape(-1, group), mask_rows, 1, half, frames
    )
    pads, raws, stats, outputs = [pad], [raw], [], []
    for k in range(3):
        stats.append(affine(*sums.ready(partial, 2), count, gain[7 + k], bias[7 + k]))
        if k < 2:
            out, pad, raw, partial = kernel_group(
                excited,
                (raws[k], jnp.stack(stats[k][2:])),
                tap_rows[k + 1],
                kernels[k + 1].reshape(-1, group),
                mask_rows,
                k + 2,
                half,
                frames,
            )
            pads.append(pad)
            raws.append(raw)
            outputs.append(out)
    joined, raw_e, off_e, sums_e = kernel_join(
        excited, outputs, raws[2], jnp.stack(stats[2][2:]), mask_rows, expand2, half
    )
    sums_e = jnp.sum(sums_e, axis=1)
    mean_e, inv_e, alpha_e, beta_e = affine(
        *sums(sums_e[0], sums_e[1]), count, gain[10], bias[10], off_e[0]
    )
    def by_owner(values, number):
        return (
            values.astype(BF)
            .reshape(dp, fsdp, -1, number, middle)
            .transpose(1, 0, 3, 2, 4)
            .reshape(fsdp, dp, -1, middle)
        )

    shifts = [None] * 11
    spreads = [None] * 11

    result, grad_total, sums_e = kernel_result(
        raw_e,
        block_one,
        cotangent.transpose(0, 2, 3, 1, 4),
        jnp.stack([alpha_e, beta_e, mean_e]),
        mask_rows,
        half,
    )
    sums_e = jnp.sum(sums_e, axis=1)
    shifts[10], spreads[10] = sums(sums_e[0], sums_e[1] * inv_e)

    def back_stats(index, mean, inv):
        scale = gain[index] * inv
        return [scale, mean, scale * shifts[index] / count, scale * inv * spreads[index] / count]

    def lower(k):
        return raws[k], jnp.stack([stats[k][2], stats[k][3], stats[k][0]])

    flipped = [kernels[k][::-1].transpose(0, 2, 1).reshape(9 * group, group) for k in range(3)]
    final_grad, grad_joined, grad_pre, partial = kernel_final_back(
        grad_total,
        raw_e,
        jnp.stack(back_stats(10, mean_e, inv_e)),
        mask_rows,
        expand2,
        *lower(2),
        half,
    )
    kernel_grads = [None] * 3
    temporal_grads = [None] * 3
    grad_pieces = [None] * 3
    for k in (2, 1, 0):
        mean, inv, alpha, _ = stats[k]
        shifts[7 + k], spreads[7 + k] = sums.ready(partial, 2)
        spreads[7 + k] = spreads[7 + k] * inv
        got = kernel_group_back(
            grad_pre,
            raws[k],
            jnp.stack(
                [alpha, mean, alpha * shifts[7 + k] / count, alpha * inv * spreads[7 + k] / count]
            ),
            flipped[k],
            tap_rows[k],
            excited,
            outputs[k - 1] if k else (grad_pieces[1], grad_pieces[2], act_d),
            grad_joined,
            lower(k - 1) if k else None,
            mask_rows,
            k + 1,
            half,
            frames,
        )
        group_grad, grad_pieces[k], sums_t = got[:3]
        if k:
            grad_pre, partial = got[3:]
        else:
            grad_attend = got[3].reshape(slots, frames, middle)
        temporal_grads[k] = jnp.sum(sums_t, axis=1)
        kernel_grads[k] = kernel_group_weights(pads[k], group_grad, half)
    grad_kernels = rows_of(
        jnp.stack(kernel_grads).reshape(27, devices, -1).swapaxes(0, 1).astype(BF).reshape(devices, -1)
    )
    total_a = blocks * rowse + grad_kernels.shape[1]
    total_a += -total_a % 16
    if aligned:
        packed_a = kernel_weight_grad(joined, final_grad, dp, fsdp, rowse, 0, blocks * rowse)
        rest = grad_kernels.reshape(dp, fsdp, -1, middle).swapaxes(0, 1)
        rest = jnp.pad(rest, ((0, 0), (0, 0), (0, -rest.shape[2] % 16), (0, 0)))
        packed_a = jnp.concatenate([packed_a, rest], axis=2)
    else:
        packed_a = jnp.concatenate(
            [
                by_owner(weight_grad(joined, final_grad), blocks),
                grad_kernels.reshape(dp, fsdp, -1, middle).swapaxes(0, 1),
            ],
            axis=2,
        )
        packed_a = jnp.pad(
            packed_a, ((0, 0), (0, 0), (0, total_a - packed_a.shape[2]), (0, 0))
        )
    grad_x = grad_attend * 2.0 * sigma * (1.0 - sigma)
    unit_x = (lifted - mean_x) * inv_x
    pool_unit = (pool_raw - mean_m * pool_one) * inv_m
    grad_e = jnp.einsum("cfo,or->cfr", grad_x, full_motion_out * alpha_x[:, None], precision=HIGHEST)
    shifts[6], spreads[6], first_t, second_t = sums(
        jnp.sum(grad_x, axis=(0, 1)),
        jnp.sum(grad_x * unit_x, axis=(0, 1)),
        jnp.sum(grad_e * pool_one, axis=(0, 1)),
        jnp.sum(grad_e * pool_unit, axis=(0, 1)),
    )
    shifts[6], packed_a = lax.optimization_barrier((shifts[6], packed_a))
    mine_a = lax.psum_scatter(
        packed_a.reshape(-1, middle), "fsdp", scatter_dimension=0, tiled=True
    )
    lift_b = jnp.dot(
        full_motion_out, alpha_m[:, None] * gram_ab + beta_m[:, None] * gram_bb, precision=HIGHEST
    )
    lift_a = jnp.dot(
        full_motion_out, alpha_m[:, None] * gram_aa + beta_m[:, None] * gram_ab.T, precision=HIGHEST
    )
    unit_b = inv_x[:, None] * (lift_b - mean_x[:, None] * pool_b)
    unit_a = inv_x[:, None] * (lift_a - mean_x[:, None] * pool_a)
    unit_u = (unit_a - unit_b * mean_m) * inv_m
    pool_u = (pool_a - pool_b * mean_m) * inv_m
    back_x = full_motion_out * alpha_x[:, None]
    shifts[5] = first_t - jnp.sum(
        back_x * (shifts[6][:, None] * pool_b + spreads[6][:, None] * unit_b), axis=0
    ) / frame_total
    spreads[5] = second_t - jnp.sum(
        back_x * (shifts[6][:, None] * pool_u + spreads[6][:, None] * unit_u), axis=0
    ) / frame_total
    grad_lifted = alpha_x * (grad_x - fmask * (shifts[6] + unit_x * spreads[6]) / frame_total)
    grad_motion_out = jnp.einsum("cfo,cfr->or", grad_lifted, pooled, precision=HIGHEST)
    grad_pooled = jnp.einsum("cfo,or->cfr", grad_lifted, full_motion_out, precision=HIGHEST)
    grad_change = grad_pooled * vnext / area
    reduced_windows = later(
        fmask * (alpha_m * in_window + beta_m * jnp.sum(windows, axis=(0, 1))[:, None, None, None])
    )
    motion_tap_grad = jnp.sum(grad_change * reduced_windows, axis=(1, 2))
    grad_narrow, motion_grad, sums_narrow = kernel_motion_back(
        grad_joined,
        grad_pieces,
        attend_rows,
        rows_d,
        jnp.stack([alpha_d, beta_d, mean_d]),
        raw_m,
        kmap.reshape(area, 1, narrow),
        jnp.stack([earlier(grad_change), grad_change]).reshape(2, batch, narrow),
        jnp.stack(
            [alpha_m, mean_m, alpha_m * shifts[5] / count, alpha_m * inv_m * spreads[5] / count]
        ),
        full_motion_in,
        mask_rows,
        half,
    )
    grad_motion_in = weight_grad(act_d, motion_grad)
    shifts[4], spreads[4] = sums.ready(sums_narrow, 2)
    spreads[4] = spreads[4] * inv_d
    small_grads = jnp.concatenate(
        [grad_motion_in.reshape(devices, -1), grad_motion_out.reshape(devices, -1)], axis=1
    )
    narrow_grad, grad_one, sums_one = kernel_block_back(
        grad_narrow,
        rows_d,
        jnp.stack(back_stats(4, mean_d, inv_d)),
        reduce2,
        grad_total,
        raw_c,
        raw_p,
        stats_one,
        mask_rows,
        half,
    )
    sums_one, mine_a = lax.optimization_barrier((sums_one, mine_a))
    mine_a = lax.psum_scatter(mine_a, "dp", scatter_dimension=0, tiled=True)
    sums_one = jnp.sum(sums_one, axis=1)
    shifts[2], spreads[2], spreads[3], motion_total, temporal_total = sums(
        sums_one[0],
        sums_one[1] * inv_c,
        sums_one[2] * inv_p,
        motion_tap_grad,
        jnp.stack(temporal_grads),
    )
    shifts[3] = shifts[2]
    stats_two = jnp.stack(back_stats(2, mean_c, inv_c) + back_stats(3, mean_p, inv_p))
    total = blocks * (rowsp + rows1)
    if aligned:
        packed_r = kernel_weight_grad(block_one, narrow_grad, dp, fsdp, rows2, 0, rows2)
    else:
        packed_r = by_owner(weight_grad(block_one, narrow_grad), 1)
    stats_two, packed_r = lax.optimization_barrier((stats_two, packed_r))
    mine_r = lax.psum_scatter(
        packed_r.reshape(-1, middle), "fsdp", scatter_dimension=0, tiled=True
    )
    widen_grad, shortcut_grad, grad_strided, sums_strided = kernel_expand_back(
        grad_one,
        raw_c,
        raw_p,
        stats_two,
        expand1,
        raw_b,
        jnp.stack([alpha_b, beta_b, mean_b, inv_b]),
        mask_rows,
        half,
    )
    if aligned:
        packed_b = kernel_weight_grad(
            act_b, widen_grad, dp, fsdp, rows1, blocks * rowsp // rows1, total
        )
        packed_b = kernel_weight_grad(
            sampled, shortcut_grad, dp, fsdp, rowsp, 0, total, packed_b
        )
    else:
        packed_b = jnp.concatenate(
            [
                by_owner(weight_grad(sampled, shortcut_grad), blocks),
                by_owner(weight_grad(act_b, widen_grad), blocks),
            ],
            axis=2,
        )
    shifts[1], spreads[1] = sums.ready(sums_strided, 2)
    shifts[1], spreads[1], packed_b, mine_a, mine_r = lax.optimization_barrier(
        (shifts[1], spreads[1], packed_b, mine_a, mine_r)
    )

    def columns_back(value, rows):
        return value.reshape(blocks, rows, middle).swapaxes(0, 1).reshape(rows, wide)

    mine_a = mine_a.astype(F32)
    own_expand2 = columns_back(mine_a[: blocks * rowse], rowse)
    own_kernels = mine_a[blocks * rowse :].reshape(-1)[:size_s]
    mine_b = packed_b.reshape(-1, middle)
    mine_b = lax.psum_scatter(mine_b, "fsdp", scatter_dimension=0, tiled=True)
    grad_spatial1, strided_grad = kernel_conv_down_weights(
        act_a, grad_strided, raw_b, jnp.stack(back_stats(1, mean_b, inv_b)), mask_rows, dp, fsdp
    )
    strided_grad = strided_grad.reshape(half, half, batch, middle)
    sum_c1 = scatter_cores(dp, fsdp, grad_spatial1)
    strided_grad, sum_c1 = lax.optimization_barrier((strided_grad, sum_c1))
    sum_c = scatter_halves(dp, sum_c1.reshape((2, -1) + sum_c1.shape[1:]), 0)
    grad_first, sums_first = kernel_conv_down_back(
        strided_grad,
        taps1,
        raw_a,
        jnp.stack([alpha_a, beta_a, mean_a, inv_a]),
        mask_rows,
    )
    shifts[0], spreads[0] = sums.ready(sums_first, 2)
    stats_first = jnp.stack(
        [
            alpha_a,
            mean_a,
            alpha_a * shifts[0] / count_big,
            alpha_a * inv_a * spreads[0] / count_big,
        ]
    )
    stats_first, sum_c, mine_b = lax.optimization_barrier((stats_first, sum_c, mine_b))
    mine_b = jnp.concatenate([mine_b.reshape(dp, -1, middle), mine_r.reshape(dp, -1, middle)], axis=1)
    mine_b = mine_b.reshape(-1, middle)
    mine_b = lax.psum_scatter(mine_b, "dp", scatter_dimension=0, tiled=True).astype(F32)
    cut1 = blocks * rowsp
    cut2 = cut1 + blocks * rows1
    own_project1 = columns_back(mine_b[:cut1], rowsp)
    own_expand1 = columns_back(mine_b[cut1:cut2], rows1)
    own_reduce2 = mine_b[cut2:]
    for bit in range(1, dp.bit_length() - 1):
        sum_c = scatter_halves(dp, sum_c.reshape((2, -1) + sum_c.shape[1:]), bit)
    sum_c = sum_c.reshape(fsdp // 2, -1, middle)
    first_grad, grad_reduce1 = kernel_first_grad(
        grad_first, raw_a, feats, stats_first, mask_rows, frames
    )
    grad_reduce1, sum_c = lax.optimization_barrier((grad_reduce1, sum_c))
    sum_d = jnp.concatenate(
        [grad_reduce1.reshape(devices, -1, middle), rows_of(small_grads.astype(BF))], axis=1
    )
    rows_d = sum_d.shape[1]
    sum_d = sum_d.reshape((dp, fsdp // 2, 2) + sum_d.shape[1:]).transpose(2, 1, 0, 3, 4)
    sum_d = scatter_cores(dp, fsdp, sum_d).reshape(fsdp // 2, -1, middle)
    both = scatter_fsdp(fsdp, jnp.concatenate([sum_d, sum_c], axis=1))
    grad_features = None
    for pair in range(slots // 2):
        grad_features = kernel_grad_features(
            first_grad, full_reduce1, shortcut_grad, project1, height, frames, pair, grad_features
        )
        if pair == 0:
            grad_features, both = lax.optimization_barrier((grad_features, both))
    own_spatial1 = both[dp * rows_d :]
    sum_d = scatter_dp(both[: dp * rows_d].astype(BF).reshape(dp, rows_d, middle))
    rows_first = c_in // devices
    own_reduce1 = sum_d[:rows_first]
    own_motion = sum_d[rows_first:].reshape(-1)[: 2 * size_m].reshape(2, own, narrow)
    grad_features = grad_features.reshape(slots, height, height, frames, c_in)
    return (
        result.transpose(0, 3, 1, 2, 4),
        grad_features.transpose(0, 3, 1, 2, 4),
        own_reduce1,
        own_spatial1.reshape(9, own * middle),
        own_expand1,
        own_project1,
        own_reduce2,
        own_motion[0],
        own_motion[1],
        own_kernels.reshape(27, -1),
        own_expand2,
        jnp.concatenate(spreads),
        jnp.concatenate(shifts),
        motion_total,
        temporal_total,
    )


def solution(mesh):
    dp, fsdp = mesh.shape["dp"], mesh.shape["fsdp"]

    def run(*arrays):
        return local(dp, fsdp, *arrays)

    rows = P(AXES, None)
    columns = P(None, AXES)
    clips = P(AXES, None, None, None, None)
    return jax.shard_map(
        run,
        mesh=mesh,
        in_specs=(
            P(AXES),
            P(AXES),
            rows,
            clips,
            rows,
            columns,
            rows,
            rows,
            rows,
            rows,
            rows,
            columns,
            rows,
            P(),
            P(),
            P(),
            P(),
            clips,
        ),
        out_specs=(
            clips,
            clips,
            rows,
            columns,
            rows,
            rows,
            rows,
            rows,
            rows,
            columns,
            rows,
            P(),
            P(),
            P(),
            P(),
        ),
        check_vma=False,
    )
```

```python
import jax
import jax.numpy as jnp
from jax import lax
from jax.experimental import pallas as pl
from jax.experimental.pallas import tpu as pltpu
from jax.sharding import PartitionSpec as P

EPSILON = 1e-05
HIGHEST = lax.Precision.HIGHEST
AXES = ("dp", "fsdp")
BF = jnp.bfloat16
F32 = jnp.float32


def by_clip(values, frames):
    return values.reshape(values.shape[:-2] + (-1, frames, values.shape[-1]))


def earlier(values):
    return jnp.concatenate([jnp.zeros_like(values[..., :1, :]), values[..., :-1, :]], axis=-2)


def later(values):
    return jnp.concatenate([values[..., 1:, :], jnp.zeros_like(values[..., :1, :])], axis=-2)


def taps_of(values, size):
    padded = jnp.pad(values, ((1, 1), (1, 1), (0, 0), (0, 0), (0, 0)))
    return [padded[r : r + size, c : c + size] for r in range(3) for c in range(3)]


def dot(left, weight):
    shape = left.shape
    flat = jnp.dot(left.reshape(-1, shape[-1]), weight, preferred_element_type=F32)
    return flat.reshape(shape[:-1] + (weight.shape[1],))


def dot_t(grad, weight):
    shape = grad.shape
    flat = lax.dot_general(
        grad.reshape(-1, shape[-1]), weight, (((1,), (1,)), ((), ())), preferred_element_type=F32
    )
    return flat.reshape(shape[:-1] + (weight.shape[0],))


def weight_grad(left, grad):
    return lax.dot_general(
        left.reshape(-1, left.shape[-1]),
        grad.reshape(-1, grad.shape[-1]),
        (((0,), (0,)), ((), ())),
        preferred_element_type=F32,
    )


def silu_slope(values):
    sig = jax.nn.sigmoid(values)
    return sig * (1.0 + values * (1.0 - sig))


def total_over(values):
    return jnp.sum(values, axis=tuple(range(values.ndim - 1)))


def silu_parts(norm):
    sig = 0.5 * jnp.tanh(0.5 * norm) + 0.5
    return sig, norm * sig


def call(body, grid, ins, in_blocks, outs, out_blocks, scratch=(), limit=56, flops=0, moved=0):
    def spec(block):
        if block is None:
            return pl.BlockSpec(memory_space=pltpu.VMEM)
        return pl.BlockSpec(block[0], block[1])

    return pl.pallas_call(
        body,
        grid=grid,
        in_specs=[spec(b) for b in in_blocks],
        out_specs=[spec(b) for b in out_blocks],
        out_shape=[jax.ShapeDtypeStruct(s, d) for s, d in outs],
        scratch_shapes=list(scratch),
        compiler_params=pltpu.CompilerParams(
            vmem_limit_bytes=limit * 1024 * 1024,
            dimension_semantics=("arbitrary",) * len(grid),
        ),
        cost_estimate=pl.CostEstimate(flops=flops, bytes_accessed=moved, transcendentals=0),
    )(*ins)


def whole(shape):
    return shape, lambda *_: (0,) * len(shape)


def mean_of(raw, weight):
    return jnp.sum(raw * weight, axis=0, keepdims=True) / jnp.maximum(jnp.sum(weight), 1.0)


def kernel_reduce1(feats, weight, mask, height, frames):
    c_in, middle = weight.shape
    slots = feats.shape[0]
    half = height // 2
    rows = 2 * height * frames

    def body(x_ref, w_ref, m_ref, raw_ref, off_ref, sum_ref):
        first = (pl.program_id(0) == 0) & (pl.program_id(1) == 0)

        @pl.when(first)
        def _():
            sum_ref[...] = jnp.zeros_like(sum_ref)
            few = nn(x_ref[0, : height * frames], w_ref[...]).reshape(height, frames, middle)
            off_ref[0:1] = mean_of(jnp.sum(few, axis=0) * (1.0 / height), m_ref[:frames, :1])

        left = x_ref[...].reshape(2 * rows, c_in)
        m = m_ref[:, :1].reshape(2, 1, 1, frames, 1)
        for c in chunks(middle):
            raw = nn(left, w_ref[:, c]).reshape(2, 2, height, frames, -1)
            offset = off_ref[0:1, c]
            sum_ref[0, :, c] += jnp.sum(jnp.sum(raw, axis=(1, 2)) * m[:, 0, 0], axis=0)
            sum_ref[1, :, c] += jnp.sum(jnp.sum(raw * raw, axis=(1, 2)) * m[:, 0, 0], axis=0)
            low = raw - offset
            raw_ref[:, :, :, c] = jnp.concatenate([low[0], low[1]], axis=2).astype(BF)

    return call(
        body,
        (slots // 2, half),
        (feats, weight, mask),
        (
            ((2, rows, c_in), lambda c, h: (c, h, 0)),
            whole(weight.shape),
            ((2 * frames, mask.shape[1]), lambda c, h: (c, 0)),
        ),
        (
            ((height, height, slots * frames, middle), BF),
            ((8, middle), F32),
            ((2, frames, middle), F32),
        ),
        (
            ((2, height, 2 * frames, middle), lambda c, h: (h, 0, c, 0)),
            whole((8, middle)),
            whole((2, frames, middle)),
        ),
        flops=2 * feats.size * middle,
        moved=feats.size * 2 + feats.size // c_in * middle * 2,
    )


def exchange_shape(width):
    return (lax.psum(1, AXES), 1, width)


def send_sums(send_ref, sum_ref, last=True):
    def send():
        rows = [jnp.sum(sum_ref[n], axis=0, keepdims=True) for n in range(sum_ref.shape[0])]
        row = jnp.concatenate(rows, axis=1)
        send_ref[...] = jnp.broadcast_to(row[None], send_ref.shape)

    if last is True:
        send()
    else:
        pl.when(last)(send)


def kernel_act(raw_a, stats, mask):
    height, _, batch, middle = raw_a.shape
    block = (2, height, batch, middle), lambda i: (i, 0, 0, 0)

    def body(a_ref, s_ref, m_ref, act_ref):
        m = m_ref[...]
        for c in chunks(middle):
            al, be = s_ref[0:1, c], s_ref[1:2, c]
            for p in range(2):
                for j in range(height):
                    act_ref[p, j, :, c] = (silu_parts(a_ref[p, j, :, c].astype(F32) * al + be)[1] * m).astype(BF)

    return call(
        body,
        (height // 2,),
        (raw_a, stats, mask),
        (block, whole(stats.shape), whole(mask.shape)),
        ((raw_a.shape, BF),),
        (block,),
        flops=10 * raw_a.size,
        moved=raw_a.size * 6,
    )[0]


def kernel_conv_down(act_a, mask, taps):
    height, _, batch, middle = act_a.shape
    half = height // 2
    rows = half * batch

    def body(a_ref, m_ref, *refs):
        w_refs, (raw_ref, send_ref, cols, w_ref, sum_ref) = refs[:9], refs[9:]
        step = pl.program_id(0)
        wide = 3 * middle

        @pl.when(step == 0)
        def _():
            sum_ref[...] = jnp.zeros_like(sum_ref)
            cols[...] = jnp.zeros_like(cols)
            for t in range(9):
                w_ref[t * middle : (t + 1) * middle] = taps[t].of(w_refs[t], 0)

        @pl.when(step > 0)
        def _():
            cols[:, :wide] = cols[:, 2 * wide :]

        m = m_ref[:, :1]
        for p in range(2):
            base = (1 + p) * wide
            for j in range(half):
                for q in range(2):
                    act = a_ref[p, 2 * j + q]
                    lane = base + (1 + q) * middle
                    cols[j * batch : (j + 1) * batch, lane : lane + middle] = act
                    if q == 1 and j + 1 < half:
                        cols[(j + 1) * batch : (j + 2) * batch, base : base + middle] = act
        raw = jnp.dot(cols[...], w_ref[...], preferred_element_type=F32)
        raw = raw.reshape(half, batch, middle)
        raw_ref[0] = raw
        sum_ref[0] += jnp.sum(raw, axis=0) * m
        sum_ref[1] += jnp.sum(raw * raw, axis=0) * m
        send_sums(send_ref, sum_ref, step == half - 1)

    return call(
        body,
        (half,),
        (act_a, mask) + tuple(t.array for t in taps),
        (((2, height, batch, middle), lambda i: (i, 0, 0, 0)), whole(mask.shape))
        + tuple(t.block() for t in taps),
        (
            ((half, half, batch, middle), F32),
            (exchange_shape(2 * middle), F32),
        ),
        (
            ((1, half, batch, middle), lambda i: (i, 0, 0, 0)),
            whole(exchange_shape(2 * middle)),
        ),
        scratch=[pltpu.VMEM((rows, 9 * middle), BF), pltpu.VMEM((9 * middle, middle), BF), pltpu.VMEM((2, batch, middle), F32)],
        flops=2 * half * rows * 9 * middle * middle,
        moved=act_a.size * 2 + 18 * middle * middle,
    )


def kernel_conv_down_weights(act_a, grad, raw_b, stats, mask, dp, fsdp):
    height, _, batch, middle = act_a.shape
    half = height // 2
    split = act_a.reshape(half, 2, half, 2, batch, middle)
    own = middle // (dp * fsdp)
    aligned = own % 16 == 0

    def body(a_ref, n_ref, b_ref, s_ref, m_ref, out_ref, g_ref, cols):
        step = pl.program_id(0)

        @pl.when(step == 0)
        def _():
            for c in chunks(middle):
                scale, mean, shift, spread = (s_ref[n : n + 1, c] for n in range(4))
                m = m_ref[:, : c.stop - c.start]

                @pl.loop(0, half)
                def _(i):
                    for j in range(half):
                        p = i * half + j
                        value = scale * n_ref[p, :, c] - m * (shift + (b_ref[p, :, c] - mean) * spread)
                        g_ref[p, :, c] = value.astype(BF)

        for r in range(3):
            for c in range(3):
                top, left = int(r == 0), int(c == 0)

                @pl.when(step == r * 3 + c)
                def _(r=r, c=c, top=top, left=left):
                    if top:
                        cols[0] = jnp.zeros_like(cols[0])
                    if left:
                        cols[:, 0] = jnp.zeros_like(cols[:, 0])
                    cols[top:, left:] = a_ref[
                        : half - top, int(r != 1), : half - left, int(c != 1)
                    ]

        value = tn(cols[...].reshape(half * half * batch, middle), g_ref[...].reshape(-1, middle)).astype(BF)
        if not aligned:
            out_ref[0] = value
            return
        value = value.reshape(dp, fsdp // 2, 2, own, middle)
        for place, d in enumerate(by_low_bit(dp)):
            for f in range(fsdp // 2):
                for core in range(2):
                    out_ref[core, place, f] = value[d, f, core]

    if aligned:
        out = ((2, dp, fsdp // 2, 9 * own, middle), BF)
        out_block = (2, dp, fsdp // 2, own, middle), lambda t: (0, 0, 0, t, 0)
    else:
        out = ((9, middle, middle), BF)
        out_block = (1, middle, middle), lambda t: (t, 0, 0)
    value, strided_grad = call(
        body,
        (9,),
        (split, grad, raw_b, stats, mask),
        (whole(split.shape), whole(grad.shape), whole(raw_b.shape), whole(stats.shape), whole(mask.shape)),
        (out, (grad.shape, BF)),
        (out_block, whole(grad.shape)),
        scratch=[pltpu.VMEM((half, half, batch, middle), BF)],
        flops=2 * half * half * batch * 9 * middle * middle,
        moved=act_a.size * 2 + grad.size * 10 + 18 * middle * middle,
    )
    if not aligned:
        value = value.reshape(9, dp, fsdp // 2, 2, own, middle).transpose(3, 1, 2, 0, 4, 5)
        value = value.reshape(2, dp, fsdp // 2, 9 * own, middle)[:, jnp.array(by_low_bit(dp))]
    return value, strided_grad


def kernel_conv_down_back(grad, taps, raw_a, stats, mask):
    height, _, batch, middle = raw_a.shape
    half = height // 2
    rows = half * batch

    def body(g_ref, n_ref, a_ref, s_ref, m_ref, *refs):
        w_refs, (out_ref, send_ref, here, below, sum_ref) = refs[:9], refs[9:]
        step = pl.program_id(0)

        @pl.when(step == 0)
        def _():
            sum_ref[...] = jnp.zeros_like(sum_ref)
            here[half] = jnp.zeros_like(here[half])
            below[half] = jnp.zeros_like(below[half])

        here[:half] = g_ref[0]

        @pl.when(step < half - 1)
        def _():
            below[:half] = n_ref[0]

        @pl.when(step == half - 1)
        def _():
            below[:half] = jnp.zeros_like(n_ref[0])

        def tap(ref, right, t):
            return lax.dot_general(
                ref[right : right + half].reshape(rows, middle),
                taps[t].of(w_refs[t], 0),
                (((1,), (1,)), ((), ())),
                preferred_element_type=F32,
            )

        al, be = s_ref[0:1], s_ref[1:2]
        mean, inv = s_ref[2:3], s_ref[3:4]
        m = m_ref[:, :1]
        plans = (
            (0, 0, ((here, 0, 4),)),
            (0, 1, ((here, 0, 5), (here, 1, 3))),
            (1, 0, ((here, 0, 7), (below, 0, 1))),
            (1, 1, ((here, 0, 8), (here, 1, 6), (below, 0, 2), (below, 1, 0))),
        )
        for p, q, parts in plans:
            back = tap(*parts[0])
            for part in parts[1:]:
                back = back + tap(*part)
            raw = a_ref[0, p, :, q].astype(F32)
            norm = raw * al + be
            sig, act = silu_parts(norm)
            slope = sig + act * (1.0 - sig)
            out = back.reshape(half, batch, middle) * slope * m
            out_ref[0, p, :, q] = out.astype(BF)
            sum_ref[0] += jnp.sum(out, axis=0)
            sum_ref[1] += jnp.sum(out * ((raw - mean) * inv), axis=0)
        send_sums(send_ref, sum_ref, step == half - 1)

    return call(
        body,
        (half,),
        (grad, grad, raw_a.reshape(half, 2, half, 2, batch, middle), stats, mask)
        + tuple(t.array for t in taps),
        (
            ((1, half, batch, middle), lambda i: (i, 0, 0, 0)),
            ((1, half, batch, middle), lambda i: (jnp.minimum(i + 1, half - 1), 0, 0, 0)),
            ((1, 2, half, 2, batch, middle), lambda i: (i, 0, 0, 0, 0, 0)),
            whole(stats.shape),
            whole(mask.shape),
        )
        + tuple(t.block() for t in taps),
        (
            ((half, 2, half, 2, batch, middle), BF),
            (exchange_shape(2 * middle), F32),
        ),
        (
            ((1, 2, half, 2, batch, middle), lambda i: (i, 0, 0, 0, 0, 0)),
            whole(exchange_shape(2 * middle)),
        ),
        scratch=[
            pltpu.VMEM((half + 1, batch, middle), BF),
            pltpu.VMEM((half + 1, batch, middle), BF),
            pltpu.VMEM((2, batch, middle), F32),
        ],
        flops=2 * half * rows * 9 * middle * middle,
        moved=raw_a.size * 8 + 18 * middle * middle,
    )


def kernel_first_grad(grad, raw_a, feats, stats, mask, frames):
    height, _, batch, middle = raw_a.shape
    half = height // 2
    rows = half * height * frames
    line = height * frames
    slots, _, c_in = feats.shape

    def body(g_ref, a_ref, x_ref, s_ref, m_ref, out_ref, w_ref, acc):
        first = (pl.program_id(0) == 0) & (pl.program_id(1) == 0)
        last = (pl.program_id(0) == slots // 2 - 1) & (pl.program_id(1) == 1)

        @pl.when(first)
        def _():
            acc[...] = jnp.zeros_like(acc)

        m = m_ref[...]
        for c in chunks(middle):
            scale, mean, shift, spread = (s_ref[n : n + 1, c] for n in range(4))
            for r in range(half):
                raw = a_ref[r, :, :, c].astype(F32)
                value = scale * g_ref[r, :, :, c].astype(F32) - m * (shift + (raw - mean) * spread)
                for clip in range(2):
                    part = value[:, clip * frames : (clip + 1) * frames]
                    out_ref[clip, r * line : (r + 1) * line, c] = part.reshape(line, -1).astype(BF)
        for clip in range(2):
            acc[...] += tn(x_ref[clip], out_ref[clip])

        @pl.when(last)
        def _():
            w_ref[...] = acc[...].astype(BF)

    block = (half, height, 2 * frames, middle), lambda c, h: (h, 0, c, 0)
    return call(
        body,
        (slots // 2, 2),
        (grad.reshape(raw_a.shape), raw_a, feats, stats, mask),
        (
            block,
            block,
            ((2, rows, c_in), lambda c, h: (c, h, 0)),
            whole(stats.shape),
            ((2 * frames, mask.shape[1]), lambda c, h: (c, 0)),
        ),
        (
            ((slots, 2 * rows, middle), BF),
            ((c_in, middle), BF),
        ),
        (
            ((2, rows, middle), lambda c, h: (c, h, 0)),
            whole((c_in, middle)),
        ),
        scratch=[pltpu.VMEM((c_in, middle), F32)],
        flops=2 * raw_a.size * c_in,
        moved=raw_a.size * 6 + feats.size * 2,
    )


def kernel_grad_features(grad, weight, shortcut, project, height, frames, pair, into=None):
    c_in, middle = weight.shape
    slots, all_rows, _ = grad.shape
    half = height // 2
    pixels, batch, wide = shortcut.shape
    size = 256
    parts = c_in // size

    def body(g_ref, w_ref, s_ref, p_ref, *refs):
        out_ref = refs[-1]
        even = None
        for k in range(project.count):
            left = s_ref[:, :, k * middle : (k + 1) * middle].reshape(pixels * 2 * frames, middle)
            part = nt(left, project.of(p_ref, k))
            even = part if even is None else even + part
        even = even.reshape(half, half, 2, frames, size)
        for clip in range(2):
            value = nt(g_ref[clip], w_ref[...]).reshape(half, 2, half, 2, frames, size)
            both = jnp.stack([value[:, 0, :, 0] + even[:, :, clip], value[:, 0, :, 1]], axis=2)
            line = jnp.stack([both, value[:, 1]], axis=1)
            out_ref[clip] = line.reshape(all_rows, size).astype(BF)

    groups, _, _ = project.array.shape
    if groups == 1:
        size_rows = project.rows // parts
        project_block = pl.BlockSpec((1, project.count * project.rows, middle), lambda n: (0, 0, 0))
    else:
        project_block = pl.BlockSpec(
            (groups // parts, project.count * project.rows, middle), lambda n: (n, 0, 0)
        )
    if groups == 1:

        def of(ref, k):
            begin = k * project.rows + pl.program_id(0) * size_rows
            return ref[0, pl.ds(pl.multiple_of(begin, size_rows), size_rows), :]

        project.of = of
    ins = (grad, weight, shortcut, project.array)
    in_specs = [
        pl.BlockSpec((2, all_rows, middle), lambda n: (pair, 0, 0)),
        pl.BlockSpec((size, middle), lambda n: (n, 0)),
        pl.BlockSpec((pixels, 2 * frames, wide), lambda n: (0, pair, 0)),
        project_block,
    ]
    alias = {}
    if into is not None:
        ins += (into,)
        in_specs.append(pl.BlockSpec(memory_space=pl.ANY))
        alias = {4: 0}
    return pl.pallas_call(
        body,
        grid=(parts,),
        in_specs=in_specs,
        out_specs=pl.BlockSpec((2, all_rows, size), lambda n: (pair, 0, n)),
        out_shape=jax.ShapeDtypeStruct((slots, all_rows, c_in), BF),
        input_output_aliases=alias,
        compiler_params=pltpu.CompilerParams(
            vmem_limit_bytes=56 * 1024 * 1024, dimension_semantics=("arbitrary",)
        ),
        cost_estimate=pl.CostEstimate(
            flops=(grad.size + shortcut.size) * c_in,
            bytes_accessed=grad.size + shortcut.size + slots * all_rows * c_in,
            transcendentals=0,
        ),
    )(*ins)


CHUNK = 256


def fold(value):
    return jnp.sum(value.reshape(-1, 8, value.shape[-1]), axis=0)


def chunks(width):
    return [slice(b, min(b + CHUNK, width)) for b in range(0, width, CHUNK)]


def zero_first(*refs):
    @pl.when(pl.program_id(0) == 0)
    def _():
        for ref in refs:
            ref[...] = jnp.zeros_like(ref)


def row_block(half, batch, width):
    return (half, batch, width), lambda i: (i, 0, 0)


class Packed:
    def __init__(self, array, rows, first, count):
        self.array, self.rows, self.first, self.count = array, rows, first, count

    def block(self):
        size, index = self.rows * self.count, self.first // self.count
        return (self.array.shape[0], size, self.array.shape[2]), lambda *_: (0, index, 0)

    def part(self, ref, k, size):
        if self.array.shape[0] == 1:
            return ref[0, k * size : (k + 1) * size, :]
        parts = size // self.rows
        return ref[k * parts : (k + 1) * parts].reshape(size, -1)

    def of(self, ref, k):
        part = ref[:, k * self.rows : (k + 1) * self.rows, :]
        return part.reshape(-1, part.shape[-1])


def nt(left, right):
    return lax.dot_general(left, right, (((1,), (1,)), ((), ())), preferred_element_type=F32)


def tn(left, right):
    return lax.dot_general(left, right, (((0,), (0,)), ((), ())), preferred_element_type=F32)


def nn(left, right):
    return jnp.dot(left, right, preferred_element_type=F32)


def kernel_expand(raw_b, stats, mask, weight, half):
    _, batch, middle = raw_b.shape
    wide = weight.count * middle
    rows = half * batch

    def body(b_ref, s_ref, m_ref, w_ref, act_ref, raw_ref, off_ref, sum_ref):
        zero_first(sum_ref)
        m = m_ref[...]

        for c in chunks(middle):
            al, be = s_ref[0:1, c], s_ref[1:2, c]
            for j in range(half):
                act_ref[j, :, c] = (silu_parts(b_ref[j, :, c] * al + be)[1] * m).astype(BF)


        @pl.when(pl.program_id(0) == 0)
        def _():
            for k in range(weight.count):
                few = nn(act_ref[half // 2], weight.of(w_ref, k))
                off_ref[0:1, k * middle : (k + 1) * middle] = mean_of(few, m_ref[:, :1])

        m = m_ref[:, :1]
        act = act_ref[...].reshape(rows, middle)
        for k in range(weight.count):
            raw = nn(act, weight.of(w_ref, k)).reshape(half, batch, middle)
            span = slice(k * middle, (k + 1) * middle)
            offset = off_ref[0:1, span]
            raw_ref[:, :, span] = (raw - offset).astype(BF)
            sum_ref[0, :, span] += fold(jnp.sum(raw, axis=0) * m)
            sum_ref[1, :, span] += fold(jnp.sum(raw * raw, axis=0) * m)

    pixels = half * half
    return call(
        body,
        (half,),
        (raw_b, stats, mask, weight.array),
        (row_block(half, batch, middle), whole(stats.shape), whole(mask.shape), weight.block()),
        (
            ((pixels, batch, middle), BF),
            ((pixels, batch, wide), BF), ((8, wide), F32),
            ((2, 8, wide), F32),
        ),
        (row_block(half, batch, middle), row_block(half, batch, wide), whole((8, wide)), whole((2, 8, wide))),
        flops=2 * raw_b.size * wide,
        moved=raw_b.size * 6 + pixels * batch * wide * 4,
    )


def kernel_project(sampled, mask, weight):
    pixels, batch, c_in = sampled.shape
    middle = weight.array.shape[2]
    wide = weight.count * middle

    def body(x_ref, m_ref, w_ref, raw_ref, off_ref, sum_ref):
        m = m_ref[:, :1]
        w = w_ref[...].reshape(c_in, middle)
        offset = mean_of(nn(x_ref[pixels // 2], w), m)
        off_ref[...] = jnp.broadcast_to(offset, off_ref.shape)
        part = 7
        first = second = None
        for p in range(0, pixels, part):
            raw = nn(x_ref[p : p + part].reshape(part * batch, c_in), w).reshape(part, batch, middle)
            raw_ref[p : p + part] = (raw - offset).astype(BF)
            one, two = jnp.sum(raw, axis=0), jnp.sum(raw * raw, axis=0)
            first = one if first is None else first + one
            second = two if second is None else second + two
        sum_ref[0] = fold(first * m)
        sum_ref[1] = fold(second * m)

    groups = weight.array.shape[0]
    return call(
        body,
        (weight.count,),
        (sampled, mask, weight.array),
        (
            whole(sampled.shape),
            whole(mask.shape),
            ((groups, weight.rows, middle), lambda k: (0, weight.first + k, 0)),
        ),
        (((pixels, batch, wide), BF), ((8, wide), F32), ((2, 8, wide), F32)),
        (
            ((pixels, batch, middle), lambda k: (0, 0, k)),
            ((8, middle), lambda k: (0, k)),
            ((2, 8, middle), lambda k: (0, 0, k)),
        ),
        flops=2 * sampled.size * wide,
        moved=sampled.size * 2 + pixels * batch * wide * 2,
    )


def kernel_block_one(raw_c, raw_p, stats, mask, weight, half):
    pixels, batch, wide = raw_c.shape
    middle = weight.array.shape[2]

    def body(c_ref, p_ref, s_ref, m_ref, w_ref, one_ref, raw_ref, send_ref, sum_ref):
        zero_first(sum_ref)
        m = m_ref[...]

        raw = None
        for k in range(wide // middle):
            for c in chunks(middle):
                c = slice(k * middle + c.start, k * middle + c.stop)
                al, ap, be = s_ref[0:1, c], s_ref[1:2, c], s_ref[2:3, c]
                for j in range(half):
                    total = c_ref[j, :, c].astype(F32) * al + p_ref[j, :, c].astype(F32) * ap + be
                    one_ref[j, :, c] = (silu_parts(total)[1] * m).astype(BF)
            left = one_ref[:, :, k * middle : (k + 1) * middle].reshape(half * batch, middle)
            part = nn(left, weight.part(w_ref, k, middle))
            raw = part if raw is None else raw + part
        raw = raw.reshape(half, batch, middle)
        m = m_ref[:, :1]
        raw_ref[...] = raw
        sum_ref[0] += fold(jnp.sum(raw, axis=0) * m)
        sum_ref[1] += fold(jnp.sum(raw * raw, axis=0) * m)
        send_sums(send_ref, sum_ref, pl.program_id(0) == half - 1)

    return call(
        body,
        (half,),
        (raw_c, raw_p, stats, mask, weight.array),
        (
            row_block(half, batch, wide),
            row_block(half, batch, wide),
            whole(stats.shape),
            whole(mask.shape),
            weight.block(),
        ),
        (
            ((pixels, batch, wide), BF),
            ((pixels, batch, middle), F32),
            (exchange_shape(2 * middle), F32),
        ),
        (row_block(half, batch, wide), row_block(half, batch, middle), whole(exchange_shape(2 * middle))),
        scratch=[pltpu.VMEM((2, 8, middle), F32)],
        flops=2 * raw_c.size * middle,
        moved=raw_c.size * 10,
    )


def kernel_result(raw_e, block_one, cot, stats, mask, half):
    pixels, batch, wide = raw_e.shape
    slots, _, _, frames, _ = cot.shape

    def body(e_ref, o_ref, g_ref, s_ref, m_ref, res_ref, grad_ref, sum_ref):
        zero_first(sum_ref)
        m = m_ref[...]
        for c in chunks(wide):
            al, be, mean = s_ref[0:1, c], s_ref[1:2, c], s_ref[2:3, c]
            first = second = None
            for j in range(half):
                raw = e_ref[j, :, c].astype(F32)
                sig, act = silu_parts(raw * al + be + o_ref[j, :, c].astype(F32))
                res = act * m
                for s in range(slots):
                    res_ref[s, 0, j, :, c] = res[s * frames : (s + 1) * frames].astype(BF)
                cot = jnp.concatenate([g_ref[s, 0, j, :, c].astype(F32) for s in range(slots)])
                grad = cot * m * (sig + act * (1.0 - sig))
                grad_ref[j, :, c] = grad.astype(BF)
                other = grad * (raw - mean)
                first = grad if first is None else first + grad
                second = other if second is None else second + other
            sum_ref[0, :, c] += fold(first)
            sum_ref[1, :, c] += fold(second)

    outside = (slots, 1, half, frames, wide), lambda i: (0, i, 0, 0, 0)
    return call(
        body,
        (half,),
        (raw_e, block_one, cot, stats, mask),
        (
            row_block(half, batch, wide),
            row_block(half, batch, wide),
            outside,
            whole(stats.shape),
            whole(mask.shape),
        ),
        (
            (cot.shape, BF),
            ((pixels, batch, wide), BF),
            ((2, 8, wide), F32),
        ),
        (outside, row_block(half, batch, wide), whole((2, 8, wide))),
        flops=20 * raw_e.size,
        moved=raw_e.size * 14,
    )


def kernel_block_back(grad_narrow, raw_d, stats_d, weight, grad_total, raw_c, raw_p, stats, mask, half):
    pixels, batch, wide = raw_c.shape
    middle = raw_d.shape[2]

    def body(n_ref, d_ref, sd_ref, w_ref, t_ref, c_ref, p_ref, s_ref, m_ref, nar_ref, one_ref, sum_ref, back):
        zero_first(sum_ref)
        m = m_ref[...]

        for c in chunks(middle):
            scale, mean, shift, spread = (sd_ref[n : n + 1, c] for n in range(4))
            for j in range(half):
                value = scale * n_ref[j, :, c] - m * (shift + (d_ref[j, :, c] - mean) * spread)
                nar_ref[j, :, c] = value.astype(BF)

        left = nar_ref[...].reshape(half * batch, middle)
        for k in range(wide // middle):
            back[k] = nt(left, weight.part(w_ref, k, middle)).reshape(half, batch, middle)
            for d in chunks(middle):
                c = slice(k * middle + d.start, k * middle + d.stop)
                al, ap, be, mean_c, _, mean_p = (s_ref[n : n + 1, c] for n in range(6))
                sums = [None] * 3
                for j in range(half):
                    raw_c, raw_p = c_ref[j, :, c].astype(F32), p_ref[j, :, c].astype(F32)
                    sig, act = silu_parts(raw_c * al + raw_p * ap + be)
                    grad = (t_ref[j, :, c].astype(F32) + back[k, j, :, d]) * m * (sig + act * (1.0 - sig))
                    one_ref[j, :, c] = grad.astype(BF)
                    parts = (grad, grad * (raw_c - mean_c), grad * (raw_p - mean_p))
                    sums = [p if t is None else t + p for t, p in zip(sums, parts)]
                for n in range(3):
                    sum_ref[n, :, c] += fold(sums[n])

    return call(
        body,
        (half,),
        (grad_narrow, raw_d, stats_d, weight.array, grad_total, raw_c, raw_p, stats, mask),
        (
            row_block(half, batch, middle),
            row_block(half, batch, middle),
            whole(stats_d.shape),
            weight.block(),
            row_block(half, batch, wide),
            row_block(half, batch, wide),
            row_block(half, batch, wide),
            whole(stats.shape),
            whole(mask.shape),
        ),
        (
            ((pixels, batch, middle), BF),
            ((pixels, batch, wide), BF),
            ((3, 8, wide), F32),
        ),
        (row_block(half, batch, middle), row_block(half, batch, wide), whole((3, 8, wide))),
        scratch=[pltpu.VMEM((wide // middle, half, batch, middle), F32)],
        flops=2 * raw_c.size * middle,
        moved=raw_c.size * 16,
    )


def kernel_expand_back(grad_one, raw_c, raw_p, stats, weight, raw_b, stats_b, mask, half):
    pixels, batch, wide = raw_c.shape
    middle = raw_b.shape[2]

    def body(g_ref, c_ref, p_ref, s_ref, w_ref, b_ref, sb_ref, m_ref, wid_ref, sho_ref, out_ref, send_ref, sum_ref):
        zero_first(sum_ref)
        m = m_ref[...]
        back = None
        for k in range(weight.count):
            for c in chunks(middle):
                c = slice(k * middle + c.start, k * middle + c.stop)
                rows_s = [s_ref[n : n + 1, c] for n in range(8)]
                for j in range(half):
                    grad = g_ref[j, :, c].astype(F32)
                    for raw_ref, to_ref, n in ((c_ref, wid_ref, 0), (p_ref, sho_ref, 4)):
                        scale, mean, shift, spread = rows_s[n : n + 4]
                        value = scale * grad - m * (shift + (raw_ref[j, :, c].astype(F32) - mean) * spread)
                        to_ref[j, :, c] = value.astype(BF)
            left = wid_ref[:, :, k * middle : (k + 1) * middle].reshape(half * batch, middle)
            part = nt(left, weight.of(w_ref, k))
            back = part if back is None else back + part
        m = m_ref[:, :1]
        raw = b_ref[...]
        sig, act = silu_parts(raw * sb_ref[0:1] + sb_ref[1:2])
        grad = back.reshape(half, batch, middle) * m * (sig + act * (1.0 - sig))
        out_ref[...] = grad
        sum_ref[0] += fold(jnp.sum(grad, axis=0))
        sum_ref[1] += fold(jnp.sum(grad * ((raw - sb_ref[2:3]) * sb_ref[3:4]), axis=0))
        send_sums(send_ref, sum_ref, pl.program_id(0) == half - 1)

    return call(
        body,
        (half,),
        (grad_one, raw_c, raw_p, stats, weight.array, raw_b, stats_b, mask),
        (
            row_block(half, batch, wide),
            row_block(half, batch, wide),
            row_block(half, batch, wide),
            whole(stats.shape),
            weight.block(),
            row_block(half, batch, middle),
            whole(stats_b.shape),
            whole(mask.shape),
        ),
        (
            ((pixels, batch, wide), BF),
            ((pixels, batch, wide), BF),
            ((pixels, batch, middle), F32),
            (exchange_shape(2 * middle), F32),
        ),
        (
            row_block(half, batch, wide),
            row_block(half, batch, wide),
            row_block(half, batch, middle),
            whole(exchange_shape(2 * middle)),
        ),
        scratch=[pltpu.VMEM((2, 8, middle), F32)],
        flops=2 * raw_c.size * middle,
        moved=raw_c.size * 16,
    )


def kernel_join(excited, outputs, raw_g, stats_g, mask, weight, half):
    pixels, batch, middle = excited.shape
    group = middle // 4
    wide = weight.count * middle

    def body(x_ref, o1, o2, r_ref, sg_ref, m_ref, w_ref, join_ref, raw_ref, off_ref, sum_ref):
        zero_first(sum_ref)
        m = m_ref[:, :group]
        join_ref[:, :, :group] = x_ref[...]
        join_ref[:, :, group : 2 * group] = o1[...]
        join_ref[:, :, 2 * group : 3 * group] = o2[...]
        act = silu_parts(r_ref[...] * sg_ref[0:1] + sg_ref[1:2])[1] * m
        join_ref[:, :, 3 * group :] = act.astype(BF)

        @pl.when(pl.program_id(0) == 0)
        def _():
            for k in range(weight.count):
                few = nn(join_ref[half // 2], weight.of(w_ref, k))
                off_ref[0:1, k * middle : (k + 1) * middle] = mean_of(few, m_ref[:, :1])

        left = join_ref[...].reshape(half * batch, middle)
        m = m_ref[:, :1]
        for k in range(weight.count):
            raw = nn(left, weight.of(w_ref, k)).reshape(half, batch, middle)
            span = slice(k * middle, (k + 1) * middle)
            offset = off_ref[0:1, span]
            raw_ref[:, :, span] = (raw - offset).astype(BF)
            sum_ref[0, :, span] += fold(jnp.sum(raw, axis=0) * m)
            sum_ref[1, :, span] += fold(jnp.sum(raw * raw, axis=0) * m)

    part = row_block(half, batch, group)
    return call(
        body,
        (half,),
        (excited, outputs[0], outputs[1], raw_g, stats_g, mask, weight.array),
        (part, part, part, part, whole(stats_g.shape), whole(mask.shape), weight.block()),
        (((pixels, batch, middle), BF), ((pixels, batch, wide), BF), ((8, wide), F32), ((2, 8, wide), F32)),
        (row_block(half, batch, middle), row_block(half, batch, wide), whole((8, wide)), whole((2, 8, wide))),
        flops=2 * excited.size * wide,
        moved=excited.size * 4 + pixels * batch * wide * 4,
    )


def kernel_final_back(grad_total, raw_e, stats, mask, weight, raw_g, stats_g, half):
    pixels, batch, wide = raw_e.shape
    middle = weight.array.shape[2]
    group = middle // 4

    def body(g_ref, e_ref, s_ref, m_ref, w_ref, r_ref, sg_ref, fin_ref, out_ref, pre_ref, send_ref, sum_ref):
        zero_first(sum_ref)
        m = m_ref[...]

        back = None
        for k in range(weight.count):
            for c in chunks(middle):
                c = slice(k * middle + c.start, k * middle + c.stop)
                scale, mean, shift, spread = (s_ref[n : n + 1, c] for n in range(4))
                for j in range(half):
                    value = scale * g_ref[j, :, c].astype(F32) - m * (
                        shift + (e_ref[j, :, c].astype(F32) - mean) * spread
                    )
                    fin_ref[j, :, c] = value.astype(BF)
            left = fin_ref[:, :, k * middle : (k + 1) * middle].reshape(half * batch, middle)
            part = nt(left, weight.of(w_ref, k))
            back = part if back is None else back + part
        back = back.reshape(half, batch, middle)
        out_ref[...] = back
        raw = r_ref[...]
        sig, act = silu_parts(raw * sg_ref[0:1] + sg_ref[1:2])
        pre = back[:, :, 3 * group :] * m_ref[:, :group] * (sig + act * (1.0 - sig))
        pre_ref[...] = pre
        sum_ref[0] += fold(jnp.sum(pre, axis=0))
        sum_ref[1] += fold(jnp.sum(pre * (raw - sg_ref[2:3]), axis=0))
        send_sums(send_ref, sum_ref, pl.program_id(0) == half - 1)

    part = row_block(half, batch, group)
    return call(
        body,
        (half,),
        (grad_total, raw_e, stats, mask, weight.array, raw_g, stats_g),
        (
            row_block(half, batch, wide),
            row_block(half, batch, wide),
            whole(stats.shape),
            whole(mask.shape),
            weight.block(),
            part,
            whole(stats_g.shape),
        ),
        (
            ((pixels, batch, wide), BF),
            ((pixels, batch, middle), F32),
            ((pixels, batch, group), F32),
            (exchange_shape(2 * group), F32),
        ),
        (row_block(half, batch, wide), row_block(half, batch, middle), part, whole(exchange_shape(2 * group))),
        scratch=[pltpu.VMEM((2, 8, group), F32)],
        flops=2 * raw_e.size * middle,
        moved=raw_e.size * 10,
    )


def kernel_weight_grad(left, right, dp, fsdp, rows, first, total, into=None):
    pixels, batch, depth = left.shape
    columns = right.shape[2]
    middle = min(columns, 512)
    owners = dp * fsdp

    def body(*refs):
        a_ref, b_ref, out_ref = refs[0], refs[1], refs[-1]
        value = tn(a_ref[...].reshape(-1, depth), b_ref[...].reshape(-1, middle)).astype(BF)
        value = value.reshape(dp, fsdp, rows, middle)
        for d in range(dp):
            out_ref[:, d] = value[d]

    ins = (left, right)
    in_specs = [
        pl.BlockSpec((pixels, batch, depth), lambda k: (0, 0, 0)),
        pl.BlockSpec((pixels, batch, middle), lambda k: (0, 0, k)),
    ]
    alias = {}
    if into is not None:
        ins += (into,)
        in_specs.append(pl.BlockSpec(memory_space=pl.ANY))
        alias = {2: 0}
    return pl.pallas_call(
        body,
        grid=(columns // middle,),
        in_specs=in_specs,
        out_specs=pl.BlockSpec((fsdp, dp, rows, middle), lambda k: (0, 0, first + k, 0)),
        out_shape=jax.ShapeDtypeStruct((fsdp, dp, total, middle), BF),
        input_output_aliases=alias,
        compiler_params=pltpu.CompilerParams(
            vmem_limit_bytes=56 * 1024 * 1024, dimension_semantics=("arbitrary",)
        ),
        cost_estimate=pl.CostEstimate(
            flops=2 * left.size * columns,
            bytes_accessed=left.size * 2 + right.size * 2 + owners * rows * columns * 2,
            transcendentals=0,
        ),
    )(*ins)


def frame_rows(rows):
    return lax.broadcasted_iota(jnp.int32, (1, rows, 128), 1)


def shift_frames(value, frames):
    shape = value.shape
    value = value.reshape(-1, frames, 128)
    spot = frame_rows(frames)
    before = jnp.where(spot == 0, 0.0, pltpu.roll(value, 1, 1))
    after_ = jnp.where(spot == frames - 1, 0.0, pltpu.roll(value, frames - 1, 1))
    return before.reshape(shape), after_.reshape(shape)


def nine_taps(pad, cols, half, batch):
    for r in range(3):
        for c in range(3):
            lane = (r * 3 + c) * 128
            part = pad[r : r + half, c : c + half]
            cols[:, lane : lane + 128] = part.reshape(half * half * batch, 128)


def clear_border(pad, half):
    pad[0] = jnp.zeros_like(pad[0])
    pad[half + 1] = jnp.zeros_like(pad[0])
    pad[:, 0] = jnp.zeros_like(pad[:, 0])
    pad[:, half + 1] = jnp.zeros_like(pad[:, 0])


def kernel_motion(rows_d, stats, mask, weight, windows, half):
    pixels, batch, middle = rows_d.shape
    narrow = weight.shape[1]

    def body(d_ref, s_ref, m_ref, w_ref, act_ref, raw_ref, win_ref, sq_ref):
        for c in chunks(middle):
            al, be, m = s_ref[0:1, c], s_ref[1:2, c], m_ref[...]

            @pl.loop(0, half)
            def _(i):
                for j in range(half):
                    act = silu_parts(d_ref[i * half + j, :, c] * al + be)[1] * m
                    act_ref[i * half + j, :, c] = act.astype(BF)

        raw = nn(act_ref[...].reshape(pixels * batch, middle), w_ref[...])
        raw_ref[...] = raw.reshape(pixels, batch, narrow)
        square = jnp.zeros((batch, narrow), F32)
        sums = [jnp.zeros((batch, narrow), F32) for _ in range(9)]
        for p in range(pixels):
            value = raw_ref[p]
            square = square + value * value
            for t in range(9):
                if windows[p // half][p % half][t]:
                    sums[t] = sums[t] + value
        for t in range(9):
            win_ref[t] = sums[t]
        sq_ref[...] = square

    return call(
        body,
        (1,),
        (rows_d, stats, mask, weight),
        (whole(rows_d.shape), whole(stats.shape), whole(mask.shape), whole(weight.shape)),
        (
            (rows_d.shape, BF),
            ((pixels, batch, narrow), F32),
            ((9, batch, narrow), F32),
            ((batch, narrow), F32),
        ),
        (
            whole(rows_d.shape),
            whole((pixels, batch, narrow)),
            whole((9, batch, narrow)),
            whole((batch, narrow)),
        ),
        flops=2 * rows_d.size * narrow,
        moved=rows_d.size * 6,
    )


def kernel_group(source, extra, taps, weight, mask, index, half, frames):
    pixels, batch, middle = source.shape
    group = 128

    def body(*refs):
        if index == 1:
            x_ref, e_ref, t_ref, w_ref, m_ref, first_ref, pad_ref, raw_ref, send_ref, cols, sum_ref = refs
            excited = (x_ref[...].astype(F32) * e_ref[...]).astype(BF)
            first_ref[...] = excited
            piece = first_ref[:, :, group : 2 * group].astype(F32)
        else:
            x_ref, r_ref, s_ref, t_ref, w_ref, m_ref, first_ref, pad_ref, raw_ref, send_ref, cols, sum_ref = refs
            act = silu_parts(r_ref[...] * s_ref[0:1] + s_ref[1:2])[1] * m_ref[:, :group]
            first_ref[...] = act.astype(BF)
            piece = x_ref[...].astype(F32) + first_ref[...].astype(F32)
        before, after_ = shift_frames(piece, frames)
        value = t_ref[0:1] * before + t_ref[1:2] * piece + t_ref[2:3] * after_
        clear_border(pad_ref, half)
        pad_ref[1 : half + 1, 1 : half + 1] = value.astype(BF).reshape(half, half, batch, group)
        nine_taps(pad_ref, cols, half, batch)
        raw = nn(cols[...], w_ref[...]).reshape(pixels, batch, group)
        raw_ref[...] = raw
        m = m_ref[:, :group]
        sum_ref[0] = fold(jnp.sum(raw, axis=0) * m)
        sum_ref[1] = fold(jnp.sum(raw * raw, axis=0) * m)
        send_sums(send_ref, sum_ref)

    block = (pixels, batch, group)
    if index == 1:
        ins = (source, extra, taps, weight, mask)
        first = (source.shape, BF)
        specs = tuple(whole(a.shape) for a in ins)
    else:
        ins = (source, extra[0], extra[1], taps, weight, mask)
        first = (block, BF)
        specs = ((block, lambda i: (0, 0, index)),) + tuple(whole(a.shape) for a in ins[1:])
    outs = (
        first,
        ((half + 2, half + 2, batch, group), BF),
        (block, F32),
        (exchange_shape(2 * group), F32),
    )
    return call(
        body,
        (1,),
        ins,
        specs,
        outs,
        tuple(whole(o[0]) for o in outs),
        scratch=[pltpu.VMEM((pixels * batch, 9 * group), BF), pltpu.VMEM((2, 8, group), F32)],
        flops=2 * pixels * batch * 9 * group * group,
        moved=pixels * batch * group * 12,
    )


def kernel_group_weights(pad, grad, half):
    pixels, batch, group = grad.shape

    def body(p_ref, g_ref, out_ref, cols):
        nine_taps(p_ref, cols, half, batch)
        out_ref[...] = tn(cols[...], g_ref[...].reshape(pixels * batch, group)).astype(BF)

    return call(
        body,
        (1,),
        (pad, grad),
        (whole(pad.shape), whole(grad.shape)),
        (((9 * group, group), BF),),
        (whole((9 * group, group)),),
        scratch=[pltpu.VMEM((pixels * batch, 9 * group), BF)],
        flops=2 * grad.size * 9 * group,
        moved=grad.size * 6,
    )[0]


def kernel_group_back(
    grad, raw, stats, weight, taps, excited, previous, joined, lower, mask, index, half, frames
):
    pixels, batch, group = grad.shape
    block = (pixels, batch, group)
    rows = pixels * batch

    def body(*refs):
        g_ref, r_ref, s_ref, w_ref, t_ref, x_ref, j_ref, m_ref = refs[:8]
        pad, cols, sum_ref = refs[-3:]
        m = m_ref[:, :group]
        raw = r_ref[...]
        value = s_ref[0:1] * g_ref[...] - m * (s_ref[2:3] + (raw - s_ref[1:2]) * s_ref[3:4])
        if index > 1:
            p_ref, l_ref, ls_ref, gg_ref, gp_ref, tg_ref, pre_ref, send_ref = refs[8:16]
        else:
            g2_ref, g3_ref, d_ref, gg_ref, gp_ref, tg_ref, at_ref = refs[8:15]
        gg_ref[...] = value.astype(BF)
        clear_border(pad, half)
        pad[1 : half + 1, 1 : half + 1] = gg_ref[...].reshape(half, half, batch, group)
        nine_taps(pad, cols, half, batch)
        back = nn(cols[...], w_ref[...]).reshape(block)
        before, after_ = shift_frames(back, frames)
        below = t_ref[0:1] * after_ + t_ref[1:2] * back + t_ref[2:3] * before
        gp_ref[...] = below
        piece = x_ref[...].astype(F32)
        if index > 1:
            piece = piece + p_ref[...].astype(F32)
        tg_ref[0] = fold(jnp.sum(after_ * piece, axis=0))
        tg_ref[1] = fold(jnp.sum(back * piece, axis=0))
        tg_ref[2] = fold(jnp.sum(before * piece, axis=0))
        if index > 1:
            raw = l_ref[...]
            sig, act = silu_parts(raw * ls_ref[0:1] + ls_ref[1:2])
            pre = (j_ref[...] + below) * m * (sig + act * (1.0 - sig))
            pre_ref[...] = pre
            sum_ref[0] = fold(jnp.sum(pre, axis=0))
            sum_ref[1] = fold(jnp.sum(pre * (raw - ls_ref[2:3]), axis=0))
            send_sums(send_ref, sum_ref)
        else:
            for k, source in enumerate((j_ref, gp_ref, g2_ref, g3_ref)):
                span = slice(k * group, (k + 1) * group)
                at_ref[:, span] = jnp.sum(source[...] * d_ref[:, :, span].astype(F32), axis=0)

    column = lambda k: (block, lambda i: (0, 0, k))
    ins = [grad, raw, stats, weight, taps, excited, joined, mask]
    specs = [whole(a.shape) for a in ins]
    specs[5] = column(index)
    specs[6] = column(index - 1)
    outs = [(block, BF), (block, F32), ((3, 8, group), F32)]
    if index > 1:
        more = [previous, lower[0], lower[1]]
        outs += [(block, F32), (exchange_shape(2 * group), F32)]
    else:
        more = list(previous)
        outs += [((batch, 4 * group), F32)]
    return call(
        body,
        (1,),
        ins + more,
        specs + [whole(a.shape) for a in more],
        outs,
        [whole(o[0]) for o in outs],
        scratch=[
            pltpu.VMEM((half + 2, half + 2, batch, group), BF),
            pltpu.VMEM((rows, 9 * group), BF),
            pltpu.VMEM((2, 8, group), F32),
        ],
        flops=2 * rows * 9 * group * group,
        moved=rows * group * 24,
    )


def kernel_motion_back(
    joined, pieces, attend, rows_d, stats_d, raw_m, kmap, change, stats_m, weight, mask, half
):
    pixels, batch, middle = rows_d.shape
    narrow = raw_m.shape[2]
    group = middle // 4

    def body(j_ref, p1, p2, p3, e_ref, d_ref, sd_ref, r_ref, k_ref, c_ref, sm_ref, w_ref, m_ref, out_ref, mg_ref, send_ref, sum_ref):
        zero_first(sum_ref)
        mn = m_ref[:, :narrow]
        grad = (k_ref[...] * c_ref[0] - c_ref[1]) * mn
        value = sm_ref[0:1] * grad - mn * (sm_ref[2:3] + (r_ref[...] - sm_ref[1:2]) * sm_ref[3:4])
        mg_ref[...] = value.astype(BF)
        back = nt(mg_ref[...].reshape(half * batch, narrow), w_ref[...])
        back = back.reshape(half, batch, middle)
        m = m_ref[:, :group]
        for k, ref in enumerate((j_ref, p1, p2, p3)):
            c = slice(k * group, (k + 1) * group)
            raw = d_ref[:, :, c]
            sig, act = silu_parts(raw * sd_ref[0:1, c] + sd_ref[1:2, c])
            out = (ref[...] * e_ref[:, c] + back[:, :, c]) * m * (sig + act * (1.0 - sig))
            out_ref[:, :, c] = out
            sum_ref[0, :, c] += fold(jnp.sum(out, axis=0))
            sum_ref[1, :, c] += fold(jnp.sum(out * (raw - sd_ref[2:3, c]), axis=0))
        send_sums(send_ref, sum_ref, pl.program_id(0) == half - 1)

    part = row_block(half, batch, group)
    ins = (joined,) + tuple(pieces)
    ins += (attend, rows_d, stats_d, raw_m, kmap, change, stats_m, weight, mask)
    return call(
        body,
        (half,),
        ins,
        (
            part,
            part,
            part,
            part,
            whole(attend.shape),
            row_block(half, batch, middle),
            whole(stats_d.shape),
            row_block(half, batch, narrow),
            ((half, 1, narrow), lambda i: (i, 0, 0)),
            whole(change.shape),
            whole(stats_m.shape),
            whole(weight.shape),
            whole(mask.shape),
        ),
        (
            ((pixels, batch, middle), F32),
            ((pixels, batch, narrow), BF),
            (exchange_shape(2 * middle), F32),
        ),
        (row_block(half, batch, middle), row_block(half, batch, narrow), whole(exchange_shape(2 * middle))),
        scratch=[pltpu.VMEM((2, 8, middle), F32)],
        flops=2 * rows_d.size * narrow,
        moved=rows_d.size * 12,
    )


class Sums:
    def __init__(self, dp, fsdp):
        self.devices = dp * fsdp
        half = self.devices // 2
        self.groups = [[2 * i + c for i in range(half)] for c in range(2)]
        self.swap = [(i, i ^ 1) for i in range(self.devices)]

    def flat(self, values):
        size = values.shape[0]
        if size <= 2048:
            copies = jnp.broadcast_to(values[None], (self.devices, size))
            return jnp.sum(lax.all_to_all(copies, AXES, 0, 0), axis=0)
        core = lax.axis_index("fsdp") % 2
        halves = values.reshape(2, size // 2)
        mine = lax.dynamic_index_in_dim(halves, core, 0, False)
        other = lax.dynamic_index_in_dim(halves, 1 - core, 0, False)
        mine = mine + lax.ppermute(other, AXES, self.swap)
        copies = jnp.broadcast_to(mine[None], (self.devices // 2, size // 2))
        mine = jnp.sum(lax.all_to_all(copies, AXES, 0, 0, axis_index_groups=self.groups), axis=0)
        other = lax.ppermute(mine, AXES, self.swap)
        low = jnp.where(core == 0, mine, other)
        high = jnp.where(core == 0, other, mine)
        return jnp.concatenate([low, high])

    def ready(self, copies, count):
        total = jnp.sum(lax.all_to_all(copies, AXES, 0, 0, tiled=True), axis=(0, 1))
        return list(total.reshape(count, -1))

    def __call__(self, *arrays):
        sizes = [a.size for a in arrays]
        extra = -sum(sizes) % 256
        parts = [a.reshape(-1) for a in arrays]
        if extra:
            parts.append(jnp.zeros((extra,), F32))
        merged = self.flat(jnp.concatenate(parts))
        out, begin = [], 0
        for a, size in zip(arrays, sizes):
            out.append(merged[begin : begin + size].reshape(a.shape))
            begin += size
        return out


def pairs_of(dp, fsdp):
    return [(i, i ^ 1) for i in range(dp * fsdp)]


def same_core(fsdp):
    return [[2 * i + c for i in range(fsdp // 2)] for c in range(2)]


def quick_gather(dp, fsdp, value):
    value = lax.all_to_all(jnp.broadcast_to(value[None], (dp,) + value.shape), "dp", 0, 0)
    value = lax.all_to_all(
        jnp.broadcast_to(value[None], (fsdp // 2,) + value.shape),
        "fsdp",
        0,
        0,
        axis_index_groups=same_core(fsdp),
    )
    other = lax.ppermute(value, AXES, pairs_of(dp, fsdp))
    core = lax.axis_index("fsdp") % 2
    low = jnp.where(core == 0, value, other)
    high = jnp.where(core == 0, other, value)
    both = jnp.stack([low, high], axis=2).swapaxes(0, 1)
    return both.reshape((dp * fsdp,) + both.shape[3:])


def scatter_cores(dp, fsdp, value):
    core = lax.axis_index("fsdp") % 2
    mine = lax.dynamic_index_in_dim(value, core, 0, False)
    other = lax.dynamic_index_in_dim(value, 1 - core, 0, False)
    other = lax.ppermute(other, AXES, pairs_of(dp, fsdp))
    return (mine.astype(F32) + other.astype(F32)).astype(BF)


def scatter_halves(dp, value, bit):
    mine = (lax.axis_index("dp") >> bit) & 1
    other = lax.dynamic_index_in_dim(value, 1 - mine, 0, False)
    other = lax.ppermute(other, "dp", [(i, i ^ (1 << bit)) for i in range(dp)])
    mine = lax.dynamic_index_in_dim(value, mine, 0, False)
    return (mine.astype(F32) + other.astype(F32)).astype(BF)


def scatter_fsdp(fsdp, value):
    value = lax.all_to_all(value, "fsdp", 0, 0, axis_index_groups=same_core(fsdp))
    return jnp.sum(value.astype(F32), axis=0)


def scatter_dp(value):
    return jnp.sum(lax.all_to_all(value, "dp", 0, 0).astype(F32), axis=0)


def by_low_bit(count):
    order = [0]
    while len(order) < count:
        order = [2 * i for i in order] + [2 * i + 1 for i in order]
    return order


def after(value, *others):
    return lax.optimization_barrier((value, others))[0]


def affine(total, square, count, gain, bias, offset=0.0):
    mean = total / count
    inv = lax.rsqrt(square / count - mean * mean + EPSILON)
    alpha = gain * inv
    mean = mean - offset
    return mean, inv, alpha, bias - mean * alpha


def local(
    dp,
    fsdp,
    clip_count,
    frame_count,
    frame_mask,
    features,
    w_reduce1,
    w_spatial1,
    w_expand1,
    w_project1,
    w_reduce2,
    w_motion_in,
    w_motion_out,
    w_spatial2,
    w_expand2,
    gains,
    biases,
    motion_taps,
    temporal_taps,
    cotangent,
):
    devices = dp * fsdp
    sums = Sums(dp, fsdp)
    slots, frames, height = features.shape[:3]
    half = height // 2
    area = half * half
    c_in = features.shape[-1]
    middle = w_reduce1.shape[1]
    group = middle // 4
    wide = w_expand1.shape[1]
    narrow = w_motion_in.shape[1]
    valid = (
        (jnp.arange(slots)[:, None] < clip_count[0])
        & (jnp.arange(frames)[None, :] < frame_count[:, None])
        & (frame_mask == 1)
    ).astype(F32)
    mask = valid[None, None, :, :, None]
    mask_rows = jnp.broadcast_to(valid.reshape(-1, 1), (slots * frames, 256))
    fmask = valid[:, :, None]
    widths = [middle, middle, wide, wide, middle, narrow, middle, group, group, group, wide]
    starts = [sum(widths[:k]) for k in range(len(widths))]
    gain = [gains[s : s + w] for s, w in zip(starts, widths)]
    bias = [biases[s : s + w] for s, w in zip(starts, widths)]

    feats = features.transpose(0, 2, 3, 1, 4).reshape(slots, -1, c_in)

    def gather(value):
        return lax.all_gather(value, AXES, axis=0, tiled=False)

    def rows_of(value):
        return jnp.pad(value, ((0, 0), (0, -value.shape[1] % middle))).reshape(
            value.shape[0], -1, middle
        )

    def columns_of(value):
        rows = value.shape[0]
        return value.reshape(rows, -1, middle).swapaxes(0, 1).reshape(-1, middle)

    own = middle // devices
    full_reduce1 = quick_gather(dp, fsdp, w_reduce1).reshape(c_in, middle)
    rows1, rowsp, rows2 = w_expand1.shape[0], w_project1.shape[0], w_reduce2.shape[0]
    blocks = wide // middle
    aligned = own % 16 == 0

    def gather_packed(*parts):
        value = gather(jnp.concatenate([part[0] for part in parts]))
        begin, flat, places = 0, [], []
        for part, rows, count in parts:
            places.append((rows * (1 if aligned else devices), begin // rows, count))
            mine = value[:, begin : begin + part.shape[0]]
            flat.append(mine.reshape(devices, -1, rows, middle).swapaxes(0, 1).reshape(-1, middle))
            begin += part.shape[0]
        array = value if aligned else jnp.concatenate(flat)[None]
        return [Packed(array, *place) for place in places]

    project1, expand1, spatial1 = gather_packed(
        (columns_of(w_project1), rowsp, blocks),
        (columns_of(w_expand1), rows1, blocks),
        (w_spatial1.reshape(-1, middle), own, 1),
    )
    taps1 = [Packed(spatial1.array, spatial1.rows, spatial1.first + t, 1) for t in range(9)]
    smalls = jnp.concatenate(
        [w_spatial2.reshape(1, -1), w_motion_in.reshape(1, -1), w_motion_out.reshape(1, -1)], axis=1
    )
    rowse = w_expand2.shape[0]
    late_rows = rows2 + columns_of(w_expand2).shape[0]
    smalls = rows_of(smalls)[0]
    reduce2, expand2, tail = gather_packed(
        (w_reduce2, rows2, 1),
        (columns_of(w_expand2), rowse, blocks),
        (smalls, 1, smalls.shape[0]),
    )
    if aligned:
        flat_small = tail.array[:, late_rows:].reshape(devices, -1)
    else:
        flat_small = (
            tail.array[0, late_rows * devices :]
            .reshape(-1, devices, middle)
            .swapaxes(0, 1)
            .reshape(devices, -1)
        )
    batch = slots * frames
    pixel_rows = (area, batch)
    size_s, size_m = w_spatial2.size, w_motion_in.size
    kernels = (
        flat_small[:, :size_s].reshape(devices, 27, -1).swapaxes(0, 1).reshape(3, 9, group, group)
    )
    small = flat_small[:, size_s : size_s + 2 * size_m].reshape(devices, 2, own, narrow)
    full_motion_in = small[:, 0].reshape(middle, narrow)
    full_motion_out = small[:, 1].reshape(middle, narrow).astype(F32)

    raw_a, off_a, sums_a = kernel_reduce1(feats, full_reduce1, mask_rows, height, frames)
    sum_a, square_a, frame_total, pairs = sums(
        jnp.sum(sums_a[0], axis=0),
        jnp.sum(sums_a[1], axis=0),
        jnp.sum(valid),
        jnp.sum(valid[:, :-1] * valid[:, 1:]),
    )
    count_big = frame_total * (height * height)
    count = frame_total * area
    mean_a, inv_a, alpha_a, beta_a = affine(
        sum_a, square_a, count_big, gain[0], bias[0], off_a[0]
    )
    act_a = kernel_act(raw_a, jnp.stack([alpha_a, beta_a]), mask_rows)
    raw_b, sums_b = kernel_conv_down(act_a, mask_rows, taps1)
    raw_b = raw_b.reshape(area, batch, middle)
    sampled = (
        features.reshape(slots, frames, half, 2, half, 2, c_in)[:, :, :, 0, :, 0]
        .transpose(2, 3, 0, 1, 4)
        .reshape(area, batch, c_in)
    )
    raw_p, off_p, sums_p = kernel_project(sampled, mask_rows, project1)

    def moments(raw):
        return total_over(raw * mask), total_over(raw * raw * mask)

    sum_b, square_b = sums.ready(sums_b, 2)
    mean_b, inv_b, alpha_b, beta_b = affine(sum_b, square_b, count, gain[1], bias[1])
    act_b, raw_c, off_c, sums_c = kernel_expand(
        raw_b, jnp.stack([alpha_b, beta_b]), mask_rows, expand1, half
    )
    sums_c, sums_p = jnp.sum(sums_c, axis=1), jnp.sum(sums_p, axis=1)
    sum_c, square_c, sum_p, square_p = sums(sums_c[0], sums_c[1], sums_p[0], sums_p[1])
    mean_c, inv_c, alpha_c, beta_c = affine(sum_c, square_c, count, gain[2], bias[2], off_c[0])
    mean_p, inv_p, alpha_p, beta_p = affine(sum_p, square_p, count, gain[3], bias[3], off_p[0])
    stats_one = jnp.stack(
        [alpha_c, alpha_p, beta_c + beta_p, mean_c, inv_c, mean_p, inv_p, jnp.zeros_like(mean_p)]
    )
    block_one, rows_d, sums_d = kernel_block_one(
        raw_c, raw_p, stats_one, mask_rows, reduce2, half
    )

    sum_d, square_d = sums.ready(sums_d, 2)
    mean_d, inv_d, alpha_d, beta_d = affine(sum_d, square_d, count, gain[4], bias[4])
    inside = [
        [
            [int(0 <= y - r + 1 < half and 0 <= x - c + 1 < half) for r in range(3) for c in range(3)]
            for x in range(half)
        ]
        for y in range(half)
    ]
    windows = jnp.array(inside, F32)
    act_d, raw_m, in_window, square_rows = kernel_motion(
        rows_d, jnp.stack([alpha_d, beta_d]), mask_rows, full_motion_in, inside, half
    )
    in_window = in_window.reshape(9, slots, frames, narrow)
    kmap = jnp.sum(windows[..., None] * motion_taps, axis=2)
    ksum = jnp.sum(kmap, axis=(0, 1))
    mapped = jnp.sum(in_window * motion_taps[:, None, None, :], axis=0)
    plain = in_window[4]
    vnext = later(fmask)
    pool_raw = (vnext / area) * (later(mapped * fmask) - fmask * plain)
    pool_one = (vnext / area) * (later(fmask) * ksum - fmask * area)
    flat_raw = pool_raw.reshape(-1, narrow)
    flat_valid = valid.reshape(-1, 1)
    gram = lax.dot_general(
        flat_raw * flat_valid, flat_raw, (((0,), (0,)), ((), ())), precision=HIGHEST
    )
    sum_m, square_m, pool_a, gram_aa = sums(
        total_over(plain * fmask),
        total_over(square_rows.reshape(plain.shape) * fmask),
        jnp.sum(flat_raw * flat_valid, axis=0), gram
    )
    mean_m, inv_m, alpha_m, beta_m = affine(sum_m, square_m, count, gain[5], bias[5])
    step = ksum / area - 1.0
    pool_b = pairs * step
    gram_ab = pool_a[:, None] * step[None, :]
    gram_bb = pairs * step[:, None] * step[None, :]
    pooled = alpha_m * pool_raw + beta_m * pool_one
    lifted = jnp.einsum("cfr,or->cfo", pooled, full_motion_out, precision=HIGHEST)
    gram_p = (
        alpha_m[:, None] * alpha_m * gram_aa
        + alpha_m[:, None] * beta_m * gram_ab
        + beta_m[:, None] * alpha_m * gram_ab.T
        + beta_m[:, None] * beta_m * gram_bb
    )
    sum_x = jnp.dot(full_motion_out, alpha_m * pool_a + beta_m * pool_b, precision=HIGHEST)
    square_x = jnp.sum(jnp.dot(full_motion_out, gram_p, precision=HIGHEST) * full_motion_out, axis=1)
    mean_x, inv_x, alpha_x, beta_x = affine(sum_x, square_x, frame_total, gain[6], bias[6])
    sigma = jax.nn.sigmoid(lifted * alpha_x + beta_x)
    attend1 = 2.0 * sigma
    attend_rows = attend1.reshape(batch, middle)
    tap_rows = [temporal_taps[k] for k in range(3)]
    excited, pad, raw, partial = kernel_group(
        act_d, attend_rows, tap_rows[0], kernels[0].reshape(-1, group), mask_rows, 1, half, frames
    )
    pads, raws, stats, outputs = [pad], [raw], [], []
    for k in range(3):
        stats.append(affine(*sums.ready(partial, 2), count, gain[7 + k], bias[7 + k]))
        if k < 2:
            out, pad, raw, partial = kernel_group(
                excited,
                (raws[k], jnp.stack(stats[k][2:])),
                tap_rows[k + 1],
                kernels[k + 1].reshape(-1, group),
                mask_rows,
                k + 2,
                half,
                frames,
            )
            pads.append(pad)
            raws.append(raw)
            outputs.append(out)
    joined, raw_e, off_e, sums_e = kernel_join(
        excited, outputs, raws[2], jnp.stack(stats[2][2:]), mask_rows, expand2, half
    )
    sums_e = jnp.sum(sums_e, axis=1)
    mean_e, inv_e, alpha_e, beta_e = affine(
        *sums(sums_e[0], sums_e[1]), count, gain[10], bias[10], off_e[0]
    )
    def by_owner(values, number):
        return (
            values.astype(BF)
            .reshape(dp, fsdp, -1, number, middle)
            .transpose(1, 0, 3, 2, 4)
            .reshape(fsdp, dp, -1, middle)
        )

    shifts = [None] * 11
    spreads = [None] * 11

    result, grad_total, sums_e = kernel_result(
        raw_e,
        block_one,
        cotangent.transpose(0, 2, 3, 1, 4),
        jnp.stack([alpha_e, beta_e, mean_e]),
        mask_rows,
        half,
    )
    sums_e = jnp.sum(sums_e, axis=1)
    shifts[10], spreads[10] = sums(sums_e[0], sums_e[1] * inv_e)

    def back_stats(index, mean, inv):
        scale = gain[index] * inv
        return [scale, mean, scale * shifts[index] / count, scale * inv * spreads[index] / count]

    def lower(k):
        return raws[k], jnp.stack([stats[k][2], stats[k][3], stats[k][0]])

    flipped = [kernels[k][::-1].transpose(0, 2, 1).reshape(9 * group, group) for k in range(3)]
    final_grad, grad_joined, grad_pre, partial = kernel_final_back(
        grad_total,
        raw_e,
        jnp.stack(back_stats(10, mean_e, inv_e)),
        mask_rows,
        expand2,
        *lower(2),
        half,
    )
    kernel_grads = [None] * 3
    temporal_grads = [None] * 3
    grad_pieces = [None] * 3
    for k in (2, 1, 0):
        mean, inv, alpha, _ = stats[k]
        shifts[7 + k], spreads[7 + k] = sums.ready(partial, 2)
        spreads[7 + k] = spreads[7 + k] * inv
        got = kernel_group_back(
            grad_pre,
            raws[k],
            jnp.stack(
                [alpha, mean, alpha * shifts[7 + k] / count, alpha * inv * spreads[7 + k] / count]
            ),
            flipped[k],
            tap_rows[k],
            excited,
            outputs[k - 1] if k else (grad_pieces[1], grad_pieces[2], act_d),
            grad_joined,
            lower(k - 1) if k else None,
            mask_rows,
            k + 1,
            half,
            frames,
        )
        group_grad, grad_pieces[k], sums_t = got[:3]
        if k:
            grad_pre, partial = got[3:]
        else:
            grad_attend = got[3].reshape(slots, frames, middle)
        temporal_grads[k] = jnp.sum(sums_t, axis=1)
        kernel_grads[k] = kernel_group_weights(pads[k], group_grad, half)
    grad_kernels = rows_of(
        jnp.stack(kernel_grads).reshape(27, devices, -1).swapaxes(0, 1).astype(BF).reshape(devices, -1)
    )
    total_a = blocks * rowse + grad_kernels.shape[1]
    total_a += -total_a % 16
    if aligned:
        packed_a = kernel_weight_grad(joined, final_grad, dp, fsdp, rowse, 0, blocks * rowse)
        rest = grad_kernels.reshape(dp, fsdp, -1, middle).swapaxes(0, 1)
        rest = jnp.pad(rest, ((0, 0), (0, 0), (0, -rest.shape[2] % 16), (0, 0)))
        packed_a = jnp.concatenate([packed_a, rest], axis=2)
    else:
        packed_a = jnp.concatenate(
            [
                by_owner(weight_grad(joined, final_grad), blocks),
                grad_kernels.reshape(dp, fsdp, -1, middle).swapaxes(0, 1),
            ],
            axis=2,
        )
        packed_a = jnp.pad(
            packed_a, ((0, 0), (0, 0), (0, total_a - packed_a.shape[2]), (0, 0))
        )
    grad_x = grad_attend * 2.0 * sigma * (1.0 - sigma)
    unit_x = (lifted - mean_x) * inv_x
    pool_unit = (pool_raw - mean_m * pool_one) * inv_m
    grad_e = jnp.einsum("cfo,or->cfr", grad_x, full_motion_out * alpha_x[:, None], precision=HIGHEST)
    shifts[6], spreads[6], first_t, second_t = sums(
        jnp.sum(grad_x, axis=(0, 1)),
        jnp.sum(grad_x * unit_x, axis=(0, 1)),
        jnp.sum(grad_e * pool_one, axis=(0, 1)),
        jnp.sum(grad_e * pool_unit, axis=(0, 1)),
    )
    shifts[6], packed_a = lax.optimization_barrier((shifts[6], packed_a))
    mine_a = lax.psum_scatter(
        packed_a.reshape(-1, middle), "fsdp", scatter_dimension=0, tiled=True
    )
    lift_b = jnp.dot(
        full_motion_out, alpha_m[:, None] * gram_ab + beta_m[:, None] * gram_bb, precision=HIGHEST
    )
    lift_a = jnp.dot(
        full_motion_out, alpha_m[:, None] * gram_aa + beta_m[:, None] * gram_ab.T, precision=HIGHEST
    )
    unit_b = inv_x[:, None] * (lift_b - mean_x[:, None] * pool_b)
    unit_a = inv_x[:, None] * (lift_a - mean_x[:, None] * pool_a)
    unit_u = (unit_a - unit_b * mean_m) * inv_m
    pool_u = (pool_a - pool_b * mean_m) * inv_m
    back_x = full_motion_out * alpha_x[:, None]
    shifts[5] = first_t - jnp.sum(
        back_x * (shifts[6][:, None] * pool_b + spreads[6][:, None] * unit_b), axis=0
    ) / frame_total
    spreads[5] = second_t - jnp.sum(
        back_x * (shifts[6][:, None] * pool_u + spreads[6][:, None] * unit_u), axis=0
    ) / frame_total
    grad_lifted = alpha_x * (grad_x - fmask * (shifts[6] + unit_x * spreads[6]) / frame_total)
    grad_motion_out = jnp.einsum("cfo,cfr->or", grad_lifted, pooled, precision=HIGHEST)
    grad_pooled = jnp.einsum("cfo,or->cfr", grad_lifted, full_motion_out, precision=HIGHEST)
    grad_change = grad_pooled * vnext / area
    reduced_windows = later(
        fmask * (alpha_m * in_window + beta_m * jnp.sum(windows, axis=(0, 1))[:, None, None, None])
    )
    motion_tap_grad = jnp.sum(grad_change * reduced_windows, axis=(1, 2))
    grad_narrow, motion_grad, sums_narrow = kernel_motion_back(
        grad_joined,
        grad_pieces,
        attend_rows,
        rows_d,
        jnp.stack([alpha_d, beta_d, mean_d]),
        raw_m,
        kmap.reshape(area, 1, narrow),
        jnp.stack([earlier(grad_change), grad_change]).reshape(2, batch, narrow),
        jnp.stack(
            [alpha_m, mean_m, alpha_m * shifts[5] / count, alpha_m * inv_m * spreads[5] / count]
        ),
        full_motion_in,
        mask_rows,
        half,
    )
    grad_motion_in = weight_grad(act_d, motion_grad)
    shifts[4], spreads[4] = sums.ready(sums_narrow, 2)
    spreads[4] = spreads[4] * inv_d
    small_grads = jnp.concatenate(
        [grad_motion_in.reshape(devices, -1), grad_motion_out.reshape(devices, -1)], axis=1
    )
    narrow_grad, grad_one, sums_one = kernel_block_back(
        grad_narrow,
        rows_d,
        jnp.stack(back_stats(4, mean_d, inv_d)),
        reduce2,
        grad_total,
        raw_c,
        raw_p,
        stats_one,
        mask_rows,
        half,
    )
    sums_one, mine_a = lax.optimization_barrier((sums_one, mine_a))
    mine_a = lax.psum_scatter(mine_a, "dp", scatter_dimension=0, tiled=True)
    sums_one = jnp.sum(sums_one, axis=1)
    shifts[2], spreads[2], spreads[3], motion_total, temporal_total = sums(
        sums_one[0],
        sums_one[1] * inv_c,
        sums_one[2] * inv_p,
        motion_tap_grad,
        jnp.stack(temporal_grads),
    )
    shifts[3] = shifts[2]
    stats_two = jnp.stack(back_stats(2, mean_c, inv_c) + back_stats(3, mean_p, inv_p))
    total = blocks * (rowsp + rows1)
    if aligned:
        packed_r = kernel_weight_grad(block_one, narrow_grad, dp, fsdp, rows2, 0, rows2)
    else:
        packed_r = by_owner(weight_grad(block_one, narrow_grad), 1)
    stats_two, packed_r = lax.optimization_barrier((stats_two, packed_r))
    mine_r = lax.psum_scatter(
        packed_r.reshape(-1, middle), "fsdp", scatter_dimension=0, tiled=True
    )
    widen_grad, shortcut_grad, grad_strided, sums_strided = kernel_expand_back(
        grad_one,
        raw_c,
        raw_p,
        stats_two,
        expand1,
        raw_b,
        jnp.stack([alpha_b, beta_b, mean_b, inv_b]),
        mask_rows,
        half,
    )
    if aligned:
        packed_b = kernel_weight_grad(
            act_b, widen_grad, dp, fsdp, rows1, blocks * rowsp // rows1, total
        )
        packed_b = kernel_weight_grad(
            sampled, shortcut_grad, dp, fsdp, rowsp, 0, total, packed_b
        )
    else:
        packed_b = jnp.concatenate(
            [
                by_owner(weight_grad(sampled, shortcut_grad), blocks),
                by_owner(weight_grad(act_b, widen_grad), blocks),
            ],
            axis=2,
        )
    shifts[1], spreads[1] = sums.ready(sums_strided, 2)
    shifts[1], spreads[1], packed_b, mine_a = lax.optimization_barrier(
        (shifts[1], spreads[1], packed_b, mine_a)
    )
    packed_b, mine_r = lax.optimization_barrier((packed_b, mine_r))

    def columns_back(value, rows):
        return value.reshape(blocks, rows, middle).swapaxes(0, 1).reshape(rows, wide)

    mine_a = mine_a.astype(F32)
    own_expand2 = columns_back(mine_a[: blocks * rowse], rowse)
    own_kernels = mine_a[blocks * rowse :].reshape(-1)[:size_s]
    mine_b = packed_b.reshape(-1, middle)
    mine_b = lax.psum_scatter(mine_b, "fsdp", scatter_dimension=0, tiled=True)
    grad_spatial1, strided_grad = kernel_conv_down_weights(
        act_a, grad_strided, raw_b, jnp.stack(back_stats(1, mean_b, inv_b)), mask_rows, dp, fsdp
    )
    strided_grad = strided_grad.reshape(half, half, batch, middle)
    sum_c1 = scatter_cores(dp, fsdp, grad_spatial1)
    strided_grad, sum_c1 = lax.optimization_barrier((strided_grad, sum_c1))
    sum_c = scatter_halves(dp, sum_c1.reshape((2, -1) + sum_c1.shape[1:]), 0)
    grad_first, sums_first = kernel_conv_down_back(
        strided_grad,
        taps1,
        raw_a,
        jnp.stack([alpha_a, beta_a, mean_a, inv_a]),
        mask_rows,
    )
    shifts[0], spreads[0] = sums.ready(sums_first, 2)
    stats_first = jnp.stack(
        [
            alpha_a,
            mean_a,
            alpha_a * shifts[0] / count_big,
            alpha_a * inv_a * spreads[0] / count_big,
        ]
    )
    stats_first, sum_c, mine_b = lax.optimization_barrier((stats_first, sum_c, mine_b))
    mine_b = jnp.concatenate([mine_b.reshape(dp, -1, middle), mine_r.reshape(dp, -1, middle)], axis=1)
    mine_b = mine_b.reshape(-1, middle)
    mine_b = lax.psum_scatter(mine_b, "dp", scatter_dimension=0, tiled=True).astype(F32)
    cut1 = blocks * rowsp
    cut2 = cut1 + blocks * rows1
    own_project1 = columns_back(mine_b[:cut1], rowsp)
    own_expand1 = columns_back(mine_b[cut1:cut2], rows1)
    own_reduce2 = mine_b[cut2:]
    for bit in range(1, dp.bit_length() - 1):
        sum_c = scatter_halves(dp, sum_c.reshape((2, -1) + sum_c.shape[1:]), bit)
    sum_c = sum_c.reshape(fsdp // 2, -1, middle)
    first_grad, grad_reduce1 = kernel_first_grad(
        grad_first, raw_a, feats, stats_first, mask_rows, frames
    )
    grad_reduce1, sum_c = lax.optimization_barrier((grad_reduce1, sum_c))
    sum_d = jnp.concatenate(
        [grad_reduce1.reshape(devices, -1, middle), rows_of(small_grads.astype(BF))], axis=1
    )
    rows_d = sum_d.shape[1]
    sum_d = sum_d.reshape((dp, fsdp // 2, 2) + sum_d.shape[1:]).transpose(2, 1, 0, 3, 4)
    sum_d = scatter_cores(dp, fsdp, sum_d).reshape(fsdp // 2, -1, middle)
    both = scatter_fsdp(fsdp, jnp.concatenate([sum_d, sum_c], axis=1))
    grad_features = None
    for pair in range(slots // 2):
        grad_features = kernel_grad_features(
            first_grad, full_reduce1, shortcut_grad, project1, height, frames, pair, grad_features
        )
        if pair == 0:
            grad_features, both = lax.optimization_barrier((grad_features, both))
    own_spatial1 = both[dp * rows_d :]
    sum_d = scatter_dp(both[: dp * rows_d].astype(BF).reshape(dp, rows_d, middle))
    rows_first = c_in // devices
    own_reduce1 = sum_d[:rows_first]
    own_motion = sum_d[rows_first:].reshape(-1)[: 2 * size_m].reshape(2, own, narrow)
    grad_features = grad_features.reshape(slots, height, height, frames, c_in)
    return (
        result.transpose(0, 3, 1, 2, 4),
        grad_features.transpose(0, 3, 1, 2, 4),
        own_reduce1,
        own_spatial1.reshape(9, own * middle),
        own_expand1,
        own_project1,
        own_reduce2,
        own_motion[0],
        own_motion[1],
        own_kernels.reshape(27, -1),
        own_expand2,
        jnp.concatenate(spreads),
        jnp.concatenate(shifts),
        motion_total,
        temporal_total,
    )


def solution(mesh):
    dp, fsdp = mesh.shape["dp"], mesh.shape["fsdp"]

    def run(*arrays):
        return local(dp, fsdp, *arrays)

    rows = P(AXES, None)
    columns = P(None, AXES)
    clips = P(AXES, None, None, None, None)
    return jax.shard_map(
        run,
        mesh=mesh,
        in_specs=(
            P(AXES),
            P(AXES),
            rows,
            clips,
            rows,
            columns,
            rows,
            rows,
            rows,
            rows,
            rows,
            columns,
            rows,
            P(),
            P(),
            P(),
            P(),
            clips,
        ),
        out_specs=(
            clips,
            clips,
            rows,
            columns,
            rows,
            rows,
            rows,
            rows,
            rows,
            columns,
            rows,
            P(),
            P(),
            P(),
            P(),
        ),
        check_vma=False,
    )
```
